32 devices in a mesh: dp: 4 (over y, core), fsdp: 8 (over z, x).
Axes of the slice: x: 2, y: 2, z: 4, core: 2. Of those that a mesh axis runs over, the one named last changes fastest.
Arguments:
- gate_act: bfloat16 [1536, 14336], P('dp', 'fsdp'), may hold values from -6 to 6
- up_act: bfloat16 [1536, 14336], P('dp', 'fsdp'), may hold values from -6 to 6
- out_grad: bfloat16 [1536, 5120], P('dp', 'fsdp'), may hold values from -6 to 6
- down_weight: bfloat16 [14336, 5120], P('fsdp'), may hold values from -0.046875 to 0.046875
- val_hidden: bfloat16 [1024, 14336], P('dp', 'fsdp'), may hold values from -4 to 4
- val_grad: bfloat16 [1024, 5120], P('dp', 'fsdp'), may hold values from -6 to 6
- assign: int32 [12], P('dp'), may hold values from 0 to 3
Outputs:
- grad_gate: bfloat16 [1536, 14336], P('dp', 'fsdp')
- grad_up: bfloat16 [1536, 14336], P('dp', 'fsdp')
- weight_grad: bfloat16 [14336, 5120], P('fsdp', 'dp')
- row_scores: float32 [12, 4], P('dp')
- group_values: float32 [4], replicated
The draws below stay inside these ranges and needn't reach their ends.
All inputs are finite; a program needn't handle non-finite values.
Results may differ from the reference program's by a relative error of at most 0.012.
The reference program's roundings to bfloat16 on the way count: a program that leaves them out, or rounds other values in their place, can miss the bound.
Values may be sent and summed in bfloat16 or wider, within the bound.
No kernel may reach another device: no remote copies, remote signals or barrier semaphores. Data moves between devices by JAX's collectives and lax.ppermute only.
A program may use at most 128 MiB of HBM per device.

```python
import jax
import jax.numpy as jnp
from jax import lax

D = 5120
FFW = 14336
L = 128
VAL = 256
R_DEV = 3
GROUPS = 4
ROWS = 12
TOKENS = 1536
VTOK = 1024
N_DP = 4


def place_ends(entries, rng, least, high):
    place = [jax.random.randint(jax.random.fold_in(rng, axis), (), 0, length) for axis, length in enumerate(entries.shape)]
    widest = entries.shape.index(max(entries.shape))
    beside = place[:widest] + [(place[widest] + 1) % entries.shape[widest]] + place[widest + 1:]
    return entries.at[tuple(place)].set(least).at[tuple(beside)].set(high)


def with_spikes(result, own_key, source, target, blocks, factor):
    def block_of(position):
        return (jnp.arange(result.shape[position]) // (result.shape[position] // blocks)).reshape((-1,) + (1,) * (result.ndim - 1 - position))

    first = jax.random.permutation(own_key, blocks)[block_of(target)]
    other_side = (block_of(target) + blocks // 2) % blocks
    return jnp.where((block_of(source) == first) | (block_of(source) == other_side), factor * result, result)


def levels(rng, dims, cuts, least, top_value):
    level, own = 1.0, jax.random.fold_in(rng, 6)
    for position, parts in cuts:
        draws = jnp.exp(jax.random.uniform(jax.random.fold_in(own, position), (parts,), jnp.float32, least / len(cuts), top_value / len(cuts)))
        level = level * jnp.repeat(draws, dims[position] // parts).reshape([-1 if axis == position else 1 for axis in range(len(dims))])
    return level


def scatter_about(stream_key, extent, spread, bound, split=(), kind=jnp.bfloat16):
    result = jax.random.normal(stream_key, extent, jnp.float32) * spread
    if len(split) > 0:
        result = levels(stream_key, extent, split, -0.22, 0.18) * result
    return jnp.clip(result, min=-bound, max=bound).astype(kind)


def noise_with(key, extent, spread, bound, split, heavy, held_as=jnp.bfloat16):
    values = spread * jax.random.normal(key, extent, jnp.float32)
    if split:
        values = values * levels(key, extent, split, -0.22, 0.18)
    return jnp.clip(with_spikes(values, jax.random.fold_in(key, 3), *heavy), -bound, bound).astype(held_as)


def setup_inputs(seed: int = 0) -> dict:
    key_list = jax.random.split(jax.random.key(seed), 8)
    gate_act = scatter_about(key_list[0], (TOKENS, FFW), 1.0, 6.0, ((0, 4), (1, 8)))
    up_act = scatter_about(key_list[1], (TOKENS, FFW), 1.0, 6.0, ((0, 4), (1, 8)))
    out_grad = noise_with(key_list[2], (TOKENS, D), 1.0, 6.0, ((0, 4), (1, 8)), (0, 1, 8, 2.0))
    down_weight = scatter_about(key_list[3], (FFW, D), FFW ** -0.5, 0.046875, ((0, 8),))
    val_hidden = scatter_about(key_list[4], (VTOK, FFW), 0.5, 4.0, ((0, 4), (1, 8)))
    val_grad = scatter_about(key_list[5], (VTOK, D), 1.0, 6.0, ((0, 4), (1, 8)))
    assign = place_ends(jax.random.randint(key_list[6], (ROWS,), 0, GROUPS), jax.random.fold_in(key_list[6], 1), 0, GROUPS - 1).astype(jnp.int32)
    return dict(gate_act=gate_act, up_act=up_act, out_grad=out_grad, down_weight=down_weight, val_hidden=val_hidden, val_grad=val_grad, assign=assign)


def reference(gate_act, up_act, out_grad, down_weight, val_hidden, val_grad, assign):
    gate = gate_act.astype(jnp.float32)
    up = up_act.astype(jnp.float32)
    sig = jax.nn.sigmoid(gate)
    act = gate * sig
    hidden = (act * up).astype(jnp.bfloat16)
    grad_hidden = jnp.dot(out_grad, down_weight.T, preferred_element_type=jnp.float32)
    grad_gate = (grad_hidden * up * sig * (1.0 + gate * (1.0 - sig))).astype(jnp.bfloat16)
    grad_up = (grad_hidden * act).astype(jnp.bfloat16)
    block = R_DEV * L
    hid_blocks = hidden.reshape(N_DP, block, FFW)
    grad_blocks = out_grad.reshape(N_DP, block, D)

    def accumulate(total, pieces):
        part = jnp.dot(pieces[0].T, pieces[1], preferred_element_type=jnp.float32).astype(jnp.bfloat16)
        part = lax.optimization_barrier(part)
        return (total + part.astype(jnp.float32), None)
    weight_sum, unused = lax.scan(accumulate, jnp.zeros((FFW, D), jnp.float32), (hid_blocks, grad_blocks))
    weight_grad = weight_sum.astype(jnp.bfloat16)
    hidden_gram = jnp.dot(hidden, val_hidden.T, preferred_element_type=jnp.float32)
    grad_gram = jnp.dot(out_grad, val_grad.T, preferred_element_type=jnp.float32)
    product = (hidden_gram * grad_gram).reshape(R_DEV * N_DP, L, N_DP, VAL)
    scale = 1.0 / jnp.sqrt(jnp.float32(L) * VAL * FFW * D)
    row_scores = lax.optimization_barrier(jnp.sum(product, axis=(1, 3))) * scale
    onehot = (assign[:, None] == jnp.arange(N_DP, dtype=jnp.int32)[None, :]).astype(jnp.float32)
    group_values = lax.optimization_barrier(jnp.sum(onehot * row_scores, axis=0))
    return (grad_gate, grad_up, weight_grad, row_scores, group_values)
```

```python
import jax
import jax.numpy as jnp
from jax import lax
from jax.sharding import PartitionSpec as P

D = 5120
FFW = 14336
L = 128
VAL = 256

F32 = jnp.float32
BF16 = jnp.bfloat16


def dot_nt(a, b):
    return lax.dot_general(a, b, (((1,), (1,)), ((), ())), preferred_element_type=F32)


def dot_tn(a, b):
    return lax.dot_general(a, b, (((0,), (0,)), ((), ())), preferred_element_type=F32)


def per_device(gate_act, up_act, out_grad, down_weight, val_hidden, val_grad, assign):
    dp_count = lax.axis_size("dp")
    me = lax.axis_index("dp")
    rows_here = assign.shape[0]
    tok_count = gate_act.shape[0]
    gate = gate_act.astype(F32)
    up = up_act.astype(F32)
    sig = jax.nn.sigmoid(gate)
    act = gate * sig
    hidden = (act * up).astype(BF16)

    hidden, gate_act, up_act = lax.optimization_barrier((hidden, gate_act, up_act))
    gate = gate_act.astype(F32)
    up = up_act.astype(F32)
    sig = jax.nn.sigmoid(gate)
    act = gate * sig

    grad_feat = lax.all_gather(out_grad, "dp", axis=0, tiled=True)
    piece = lax.all_gather(out_grad, "fsdp", axis=1, tiled=True)
    hidden_all = lax.all_gather(hidden, "dp", axis=0, tiled=True)

    grad_gram = lax.psum(dot_nt(grad_feat, val_grad), "fsdp")

    grad_cols = lax.all_to_all(piece, "dp", split_axis=1, concat_axis=0, tiled=True)

    grad_hidden = dot_nt(piece, down_weight)
    grad_gate = (grad_hidden * up * sig * (1.0 + gate * (1.0 - sig))).astype(BF16)
    grad_up = (grad_hidden * act).astype(BF16)

    hidden_gram = dot_nt(hidden_all, val_hidden)
    product = hidden_gram * grad_gram
    part = jnp.sum(product.reshape(dp_count * rows_here, tok_count // rows_here * VAL), axis=1)

    weight_grad = dot_tn(hidden_all, grad_cols).astype(BF16)

    scale = 1.0 / jnp.sqrt(F32(L) * VAL * FFW * D)
    mine = jnp.concatenate([part, assign.astype(F32)])
    every = lax.all_gather(mine, ("dp", "fsdp"), axis=0, tiled=False)
    every = every.reshape(dp_count, -1, mine.shape[0])
    rows = dp_count * rows_here
    scores = jnp.sum(every[:, :, :rows], axis=1) * scale
    groups = every[:, 0, rows:].reshape(rows)
    onehot = (groups[None, :] == jnp.arange(dp_count, dtype=F32)[:, None]).astype(F32)
    group_values = jnp.sum(onehot * scores, axis=1)
    row_scores = lax.dynamic_slice_in_dim(scores, me * rows_here, rows_here, axis=1).T
    return (grad_gate, grad_up, weight_grad, row_scores, group_values)


def solution(mesh):
    in_specs = (
        P("dp", "fsdp"),
        P("dp", "fsdp"),
        P("dp", "fsdp"),
        P("fsdp", None),
        P("dp", "fsdp"),
        P("dp", "fsdp"),
        P("dp"),
    )
    out_specs = (P("dp", "fsdp"), P("dp", "fsdp"), P("fsdp", "dp"), P("dp", None), P())
    return jax.shard_map(
        per_device, mesh=mesh, in_specs=in_specs, out_specs=out_specs, check_vma=False
    )
```

```python
import functools

import jax
import jax.numpy as jnp
from jax import lax
from jax.experimental import pallas as pl
from jax.experimental.pallas import tpu as pltpu
from jax.sharding import PartitionSpec as P

D = 5120
FFW = 14336
L = 128
VAL = 256

F32 = jnp.float32
BF16 = jnp.bfloat16
VMEM_LIMIT = 48 * 1024 * 1024


def dot_nt(a, b):
    return lax.dot_general(a, b, (((1,), (1,)), ((), ())), preferred_element_type=F32)


def dot_tn(a, b):
    return lax.dot_general(a, b, (((0,), (0,)), ((), ())), preferred_element_type=F32)


def swap(x, axis, k):
    n = lax.axis_size(axis)
    return lax.ppermute(x, axis, [(s, s ^ k) for s in range(n)])


def shift(x, axis, k):
    n = lax.axis_size(axis)
    return lax.ppermute(x, axis, [(s, (s + k) % n) for s in range(n)])


def whole(shape):
    return pl.BlockSpec(shape, lambda *_: (0,) * len(shape))


def grads_body(n, width, offs_ref, *refs):
    blocks, (w_ref, gate_ref, up_ref, gg_ref, gu_ref) = refs[:n], refs[n:]
    total = None
    for j in range(n):
        cols = pl.ds(pl.multiple_of(offs_ref[j], 128), width)
        term = dot_nt(blocks[j][...], w_ref[:, cols])
        total = term if total is None else total + term
    gate = gate_ref[...].astype(F32)
    up = up_ref[...].astype(F32)
    sig = jax.nn.sigmoid(gate)
    gg_ref[...] = (total * up * sig * (1.0 + gate * (1.0 - sig))).astype(BF16)
    gu_ref[...] = (total * (gate * sig)).astype(BF16)


def grads(offs, blocks, weight, gate, up):
    n = len(blocks)
    toks, width = blocks[0].shape
    units, feats = weight.shape
    tile = 256
    cols = pl.BlockSpec((toks, tile), lambda i, _: (0, i))
    out = jax.ShapeDtypeStruct((toks, units), BF16)
    return pl.pallas_call(
        functools.partial(grads_body, n, width),
        grid_spec=pltpu.PrefetchScalarGridSpec(
            num_scalar_prefetch=1,
            grid=(units // tile,),
            in_specs=[whole((toks, width))] * n
            + [pl.BlockSpec((tile, feats), lambda i, _: (i, 0)), cols, cols],
            out_specs=[cols, cols],
        ),
        out_shape=(out, out),
        compiler_params=pltpu.CompilerParams(vmem_limit_bytes=VMEM_LIMIT),
        cost_estimate=pl.CostEstimate(
            flops=2 * toks * units * feats,
            bytes_accessed=2 * (units * feats + toks * feats + 4 * toks * units),
            transcendentals=toks * units,
        ),
        name="grads",
    )(offs, *blocks, weight, gate, up)


def wgrad_body(n, width, offs_ref, *refs):
    hid, cols, out_ref = refs[:n], refs[n : 2 * n], refs[2 * n]
    for half in range(2):
        total = None
        for k in range(n):
            term = dot_tn(hid[k][...], cols[k][half])
            total = term if total is None else total + term
        place = pl.ds(pl.multiple_of(offs_ref[half], 128), width)
        out_ref[:, place] = total.astype(BF16)


def wgrad(offs, hid, cols):
    n = len(hid)
    toks, units = hid[0].shape
    width = cols[0].shape[2]
    tile = 256
    return pl.pallas_call(
        functools.partial(wgrad_body, n, width),
        grid_spec=pltpu.PrefetchScalarGridSpec(
            num_scalar_prefetch=1,
            grid=(units // tile,),
            in_specs=[pl.BlockSpec((toks, tile), lambda i, _: (0, i))] * n
            + [whole((2, toks, width))] * n,
            out_specs=pl.BlockSpec((tile, 2 * width), lambda i, _: (i, 0)),
        ),
        out_shape=jax.ShapeDtypeStruct((units, 2 * width), BF16),
        compiler_params=pltpu.CompilerParams(vmem_limit_bytes=VMEM_LIMIT),
        cost_estimate=pl.CostEstimate(
            flops=4 * n * toks * units * width,
            bytes_accessed=2 * (n * toks * (units + 2 * width) + 2 * units * width),
            transcendentals=0,
        ),
        name="wgrad",
    )(offs, *hid, *cols)


def gram_body(n, parts, *refs):
    toks_refs, (val_ref, out_ref) = refs[:n], refs[n:]
    for k in range(n):
        toks = toks_refs[k].shape[0]
        size = toks // parts
        part = dot_nt(toks_refs[k][...], val_ref[...])
        for p in range(parts):
            out_ref[p % 2, p // 2, k * size : (k + 1) * size] = part[p * size : (p + 1) * size]


def gram(toks_dp, vals, parts, name):
    n = len(toks_dp)
    toks, feats = toks_dp[0].shape
    count = vals.shape[0]
    return pl.pallas_call(
        functools.partial(gram_body, n, parts),
        out_shape=jax.ShapeDtypeStruct((2, parts // 2, n * toks // parts, count), F32),
        compiler_params=pltpu.CompilerParams(vmem_limit_bytes=VMEM_LIMIT),
        cost_estimate=pl.CostEstimate(
            flops=2 * n * toks * count * feats,
            bytes_accessed=2 * (n * toks + count) * feats + 4 * n * toks * count,
            transcendentals=0,
        ),
        name=name,
    )(*toks_dp, vals)


def gram_sum(part):
    n_fs = lax.axis_size("fsdp")
    inner = lax.axis_index("fsdp") % 2
    away = lax.dynamic_index_in_dim(part, 1 - inner, axis=0, keepdims=False)
    kept = lax.dynamic_index_in_dim(part, inner, axis=0, keepdims=False)
    pair = kept + swap(away, "fsdp", 1)
    groups = [list(range(x, n_fs, 2)) for x in range(2)]
    pair = lax.all_to_all(
        pair, "fsdp", split_axis=0, concat_axis=0, axis_index_groups=groups, tiled=True
    )
    return jnp.sum(pair, axis=0)


def per_device(gate_act, up_act, out_grad, down_weight, val_hidden, val_grad, assign):
    n_dp = lax.axis_size("dp")
    n_fs = lax.axis_size("fsdp")
    d = lax.axis_index("dp")
    f = lax.axis_index("fsdp")
    rows_here = assign.shape[0]
    toks, width = out_grad.shape
    n_out = n_fs // 2
    outer, inner = f // 2, f % 2

    gate = gate_act.astype(F32)
    up = up_act.astype(F32)
    hidden = (gate * jax.nn.sigmoid(gate) * up).astype(BF16)

    ring = [out_grad]
    for _ in range(n_out - 1):
        ring.append(shift(ring[-1], "fsdp", 2))
    pairs = [(own, swap(own, "fsdp", 1)) for own in ring]

    def over_dp(x):
        far = swap(x, "dp", 2)
        return [x, swap(x, "dp", 1), far, swap(far, "dp", 1)]

    grad_dp = over_dp(out_grad)
    hid_dp = over_dp(hidden)

    def columns_of(q):
        at = (outer - q) % n_out
        return jnp.stack([lax.select_n(at, *[p[i] for p in pairs]) for i in range(2)])

    cols_dp = [columns_of(d)] + [swap(columns_of(d ^ k), "dp", k) for k in range(1, n_dp)]

    grad_gram = gram_sum(gram(grad_dp, val_grad, n_fs, "grad_gram"))
    hidden_gram = gram_sum(gram(hid_dp, val_hidden, n_fs, "hidden_gram"))
    by_tok = jnp.sum(hidden_gram * grad_gram, axis=1).reshape(n_dp, toks // n_fs)

    place = jnp.arange(n_out, dtype=jnp.int32)
    place = ((outer - place) % n_out)[:, None] * 2 + jnp.stack([inner, 1 - inner])[None, :]
    offs = (place * width).reshape(-1).astype(jnp.int32)
    blocks = [b for p in pairs for b in p]
    grad_gate, grad_up = grads(offs, blocks, down_weight, gate_act, up_act)

    half_offs = (jnp.stack([inner, 1 - inner]) * width).astype(jnp.int32)
    weight_grad = wgrad(half_offs, hid_dp, cols_dp)

    row_of = (f * (toks // n_fs) + jnp.arange(toks // n_fs)) // (toks // rows_here)
    in_row = (row_of[:, None] == jnp.arange(rows_here)[None, :]).astype(F32)
    by_row = jnp.sum(by_tok[:, :, None] * in_row[None], axis=1)
    mine = jnp.concatenate([by_row.reshape(-1), assign.astype(F32)])
    mine = jnp.pad(mine, (0, 128 - mine.shape[0]))
    every = lax.all_to_all(
        jnp.broadcast_to(mine[None], (n_dp * n_fs, 128)),
        ("dp", "fsdp"), split_axis=0, concat_axis=0, tiled=True,
    ).reshape(n_dp, n_fs, 128)
    rows = n_dp * rows_here
    scale = 1.0 / jnp.sqrt(F32(L) * VAL * FFW * D)
    sums = jnp.sum(every[:, :, :rows], axis=1).reshape(n_dp, n_dp, rows_here)
    groups = every[:, 0, rows : rows + rows_here]
    scores = jnp.stack(
        [jnp.stack([sums[g, t ^ g] for g in range(n_dp)], axis=-1) for t in range(n_dp)]
    ) * scale
    onehot = (groups[:, :, None] == jnp.arange(n_dp, dtype=F32)).astype(F32)
    group_values = jnp.sum(onehot * scores, axis=(0, 1))
    row_scores = lax.dynamic_index_in_dim(scores, d, axis=0, keepdims=False)
    return (grad_gate, grad_up, weight_grad, row_scores, group_values)


def per_device_any(gate_act, up_act, out_grad, down_weight, val_hidden, val_grad, assign):
    n_dp = lax.axis_size("dp")
    me = lax.axis_index("dp")
    rows_here = assign.shape[0]
    toks = gate_act.shape[0]
    gate = gate_act.astype(F32)
    up = up_act.astype(F32)
    sig = jax.nn.sigmoid(gate)
    act = gate * sig
    hidden = (act * up).astype(BF16)
    grad_feat = lax.all_gather(out_grad, "dp", axis=0, tiled=True)
    piece = lax.all_gather(out_grad, "fsdp", axis=1, tiled=True)
    hidden_all = lax.all_gather(hidden, "dp", axis=0, tiled=True)
    grad_gram = lax.psum(dot_nt(grad_feat, val_grad), "fsdp")
    grad_cols = lax.all_to_all(piece, "dp", split_axis=1, concat_axis=0, tiled=True)
    grad_hidden = dot_nt(piece, down_weight)
    grad_gate = (grad_hidden * up * sig * (1.0 + gate * (1.0 - sig))).astype(BF16)
    grad_up = (grad_hidden * act).astype(BF16)
    product = dot_nt(hidden_all, val_hidden) * grad_gram
    part = jnp.sum(product.reshape(n_dp * rows_here, toks // rows_here * VAL), axis=1)
    weight_grad = dot_tn(hidden_all, grad_cols).astype(BF16)
    scale = 1.0 / jnp.sqrt(F32(L) * VAL * FFW * D)
    scores = lax.all_gather(lax.psum(part, "fsdp"), "dp") * scale
    groups = lax.all_gather(assign, "dp", tiled=True)
    onehot = (groups[None, :] == jnp.arange(n_dp, dtype=jnp.int32)[:, None]).astype(F32)
    group_values = jnp.sum(onehot * scores, axis=1)
    row_scores = lax.dynamic_slice_in_dim(scores, me * rows_here, rows_here, axis=1).T
    return (grad_gate, grad_up, weight_grad, row_scores, group_values)


def solution(mesh):
    in_specs = (
        P("dp", "fsdp"),
        P("dp", "fsdp"),
        P("dp", "fsdp"),
        P("fsdp", None),
        P("dp", "fsdp"),
        P("dp", "fsdp"),
        P("dp"),
    )
    out_specs = (P("dp", "fsdp"), P("dp", "fsdp"), P("fsdp", "dp"), P("dp", None), P())
    n_dp, n_fs = mesh.shape["dp"], mesh.shape["fsdp"]
    fits = n_dp == 4 and n_fs == 2 * n_dp
    return jax.shard_map(
        per_device if fits else per_device_any,
        mesh=mesh, in_specs=in_specs, out_specs=out_specs, check_vma=False,
    )
```

```python
import functools

import jax
import jax.numpy as jnp
from jax import lax
from jax.experimental import pallas as pl
from jax.experimental.pallas import tpu as pltpu
from jax.sharding import PartitionSpec as P

D = 5120
FFW = 14336
L = 128
VAL = 256

F32 = jnp.float32
BF16 = jnp.bfloat16
VMEM_LIMIT = 48 * 1024 * 1024


def dot_nt(a, b):
    return lax.dot_general(a, b, (((1,), (1,)), ((), ())), preferred_element_type=F32)


def dot_tn(a, b):
    return lax.dot_general(a, b, (((0,), (0,)), ((), ())), preferred_element_type=F32)


def swap(x, axis, k):
    n = lax.axis_size(axis)
    return lax.ppermute(x, axis, [(s, s ^ k) for s in range(n)])


def shift(x, axis, k):
    n = lax.axis_size(axis)
    return lax.ppermute(x, axis, [(s, (s + k) % n) for s in range(n)])


def whole(shape):
    return pl.BlockSpec(shape, lambda *_: (0,) * len(shape))


ANY = pl.BlockSpec(memory_space=pl.ANY)


def params():
    return pltpu.CompilerParams(vmem_limit_bytes=VMEM_LIMIT)


def hidden_body(gate_ref, up_ref, order_ref, out_ref):
    gate = gate_ref[...].astype(F32)
    up = up_ref[...].astype(F32)
    out_ref[...] = (gate * jax.nn.sigmoid(gate) * up).astype(BF16).T


def hidden_units(gate, up, order):
    toks, units = gate.shape
    tile = 256
    cols = pl.BlockSpec((toks, tile), lambda i: (0, i))
    return pl.pallas_call(
        hidden_body,
        grid=(units // tile,),
        in_specs=[cols, cols, ANY],
        out_specs=pl.BlockSpec((tile, toks), lambda i: (i, 0)),
        out_shape=jax.ShapeDtypeStruct((units, toks), BF16),
        compiler_params=params(),
        cost_estimate=pl.CostEstimate(
            flops=4 * toks * units, bytes_accessed=6 * toks * units, transcendentals=toks * units
        ),
        name="hidden",
    )(gate, up, order)


def arrange_body(n, at_ref, *refs):
    blocks, (order_ref, out_ref) = refs[:n], refs[n:]
    for j in range(n):
        out_ref[at_ref[j]] = blocks[j][...]


def arrange(at, blocks, order, name):
    n = len(blocks)
    vmem = pl.BlockSpec(memory_space=pltpu.VMEM)
    return pl.pallas_call(
        functools.partial(arrange_body, n),
        in_specs=[pl.BlockSpec(memory_space=pltpu.SMEM)] + [vmem] * n + [ANY],
        out_specs=vmem,
        out_shape=jax.ShapeDtypeStruct((n,) + blocks[0].shape, BF16),
        compiler_params=params(),
        cost_estimate=pl.CostEstimate(
            flops=0, bytes_accessed=4 * n * blocks[0].size, transcendentals=0
        ),
        name=name,
    )(at, *blocks, order)


def grads_body(offs_ref, own_ref, other_ref, w_ref, gate_ref, up_ref, gg_ref, gu_ref, piece):
    n, toks, width = own_ref.shape

    @pl.when(pl.program_id(0) == 0)
    def _():
        for half, ref in enumerate((own_ref, other_ref)):
            for j in range(n):
                place = pl.multiple_of(offs_ref[half] + 2 * j * width, 128)
                piece[:, pl.ds(place, width)] = ref[j]

    total = dot_nt(piece[...], w_ref[...])
    gate = gate_ref[...].astype(F32)
    up = up_ref[...].astype(F32)
    sig = jax.nn.sigmoid(gate)
    gg_ref[...] = (total * up * sig * (1.0 + gate * (1.0 - sig))).astype(BF16)
    gu_ref[...] = (total * (gate * sig)).astype(BF16)


def grads(offs, own, other, weight, gate, up):
    n, toks, width = own.shape
    units, feats = weight.shape
    tile = 256
    cols = pl.BlockSpec((toks, tile), lambda i, _: (0, i))
    out = jax.ShapeDtypeStruct((toks, units), BF16)
    return pl.pallas_call(
        grads_body,
        grid_spec=pltpu.PrefetchScalarGridSpec(
            num_scalar_prefetch=1,
            grid=(units // tile,),
            in_specs=[whole(own.shape)] * 2
            + [pl.BlockSpec((tile, feats), lambda i, _: (i, 0)), cols, cols],
            out_specs=[cols, cols],
            scratch_shapes=[pltpu.VMEM((toks, feats), BF16)],
        ),
        out_shape=(out, out),
        compiler_params=params(),
        cost_estimate=pl.CostEstimate(
            flops=2 * toks * units * feats,
            bytes_accessed=2 * (units * feats + toks * feats + 4 * toks * units),
            transcendentals=toks * units,
        ),
        name="grads",
    )(offs, own, other, weight, gate, up)


def wgrad_body(offs_ref, hid_ref, own_ref, other_ref, order_ref, out_ref, cols):
    n, toks, width = own_ref.shape

    @pl.when(pl.program_id(0) == 0)
    def _():
        for half, ref in enumerate((own_ref, other_ref)):
            place = pl.ds(pl.multiple_of(offs_ref[half], 128), width)
            for k in range(n):
                cols[k * toks : (k + 1) * toks, place] = ref[k]

    out_ref[...] = lax.dot_general(
        hid_ref[...], cols[...], (((1,), (0,)), ((), ())), preferred_element_type=F32
    ).astype(BF16)


def wgrad(offs, hid, own, other, order):
    units, total = hid.shape
    width = own.shape[2]
    tile = units // 4
    return pl.pallas_call(
        wgrad_body,
        grid_spec=pltpu.PrefetchScalarGridSpec(
            num_scalar_prefetch=1,
            grid=(units // tile,),
            in_specs=[pl.BlockSpec((tile, total), lambda i, _: (i, 0))]
            + [whole(own.shape)] * 2
            + [ANY],
            out_specs=pl.BlockSpec((tile, 2 * width), lambda i, _: (i, 0)),
            scratch_shapes=[pltpu.VMEM((total, 2 * width), BF16)],
        ),
        out_shape=jax.ShapeDtypeStruct((units, 2 * width), BF16),
        compiler_params=params(),
        cost_estimate=pl.CostEstimate(
            flops=4 * total * units * width,
            bytes_accessed=2 * (total * (units + 2 * width) + 2 * units * width),
            transcendentals=0,
        ),
        name="wgrad",
    )(offs, hid, own, other, order)


def put_slices(part, out_ref):
    inner, outer, size, _ = out_ref.shape
    for p in range(inner * outer):
        out_ref[p % inner, p // inner] = part[p * size : (p + 1) * size]


def gram_shape(count, total, parts):
    return jax.ShapeDtypeStruct((2, parts // 2, count // parts, total), F32)


def grad_gram_body(offs_ref, *refs):
    toks_refs, (val_ref, order_ref, out_ref, wide) = refs[:-4], refs[-4:]
    for k, ref in enumerate(toks_refs):
        toks = ref.shape[0]
        wide[:, pl.ds(pl.multiple_of(offs_ref[k], 128), toks)] = dot_nt(val_ref[...], ref[...])
    put_slices(wide[...], out_ref)


def hidden_gram_body(offs_ref, *refs):
    hid, (val_ref, order_ref, out_ref, all_ref) = refs[:-4], refs[-4:]
    for k, ref in enumerate(hid):
        toks = ref.shape[1]
        all_ref[:, pl.ds(pl.multiple_of(offs_ref[k], 128), toks)] = ref[...]
    part = lax.dot_general(
        val_ref[...], all_ref[...], (((1,), (0,)), ((), ())), preferred_element_type=F32
    )
    put_slices(part, out_ref)


def gram_call(body, offs, operands, order, shapes, scratch, flops, name):
    vmem = pl.BlockSpec(memory_space=pltpu.VMEM)
    return pl.pallas_call(
        body,
        in_specs=[pl.BlockSpec(memory_space=pltpu.SMEM)] + [vmem] * len(operands) + [ANY],
        out_specs=[vmem] * len(shapes),
        out_shape=shapes,
        scratch_shapes=scratch,
        compiler_params=params(),
        cost_estimate=pl.CostEstimate(
            flops=flops,
            bytes_accessed=sum(x.size * x.dtype.itemsize for x in [*operands, *shapes]),
            transcendentals=0,
        ),
        name=name,
    )(offs, *operands, order)


def gram_sum(part):
    n_fs = lax.axis_size("fsdp")
    inner = lax.axis_index("fsdp") % 2
    away = lax.dynamic_index_in_dim(part, 1 - inner, axis=0, keepdims=False)
    kept = lax.dynamic_index_in_dim(part, inner, axis=0, keepdims=False)
    pair = kept + swap(away, "fsdp", 1)
    groups = [list(range(x, n_fs, 2)) for x in range(2)]
    every = lax.all_to_all(
        pair, "fsdp", split_axis=0, concat_axis=0, axis_index_groups=groups, tiled=True
    )
    return jnp.sum(every, axis=0), pair


def per_device(gate_act, up_act, out_grad, down_weight, val_hidden, val_grad, assign):
    n_dp = lax.axis_size("dp")
    n_fs = lax.axis_size("fsdp")
    d = lax.axis_index("dp")
    f = lax.axis_index("fsdp")
    rows_here = assign.shape[0]
    toks, width = out_grad.shape
    units = gate_act.shape[1]
    total = n_dp * toks
    n_out = n_fs // 2
    outer, inner = f // 2, f % 2

    def over_dp(x):
        far = swap(x, "dp", 2)
        near = swap(jnp.stack([x, far]), "dp", 1)
        return [x, near[0], far, near[1]]

    ring = [out_grad]
    for _ in range(n_out - 1):
        ring.append(shift(ring[-1], "fsdp", 2))
    others = [swap(own, "fsdp", 1) for own in ring]

    far = swap(out_grad, "dp", 2)
    grad_dp = [out_grad, swap(out_grad, "dp", 1), far, swap(far, "dp", 1)]
    hid_dp = over_dp(hidden_units(gate_act, up_act, grad_dp[1]))

    at = (outer - jnp.arange(n_out, dtype=jnp.int32)) % n_out
    own = arrange(at, ring, others[0], "own_features")
    own_cols = lax.all_to_all(own, "dp", split_axis=0, concat_axis=0, tiled=True)
    other = arrange(at, others, own, "other_features")
    other_cols = lax.all_to_all(other, "dp", split_axis=0, concat_axis=0, tiled=True)

    tok_offs = (d ^ jnp.arange(n_dp, dtype=jnp.int32)) * toks
    vals = val_grad.shape[0]
    shape = gram_shape(vals, total, n_fs)
    (part,) = gram_call(
        grad_gram_body, tok_offs, [*grad_dp, val_grad], own, [shape],
        [pltpu.VMEM((vals, total), F32)], 2 * vals * total * width, "grad_gram",
    )
    grad_gram, _ = gram_sum(part)
    part, hid_all = gram_call(
        hidden_gram_body, tok_offs, [*hid_dp, val_hidden], other,
        [shape, jax.ShapeDtypeStruct((units, total), BF16)], [],
        2 * vals * total * units, "hidden_gram",
    )
    hidden_gram, order = gram_sum(part)
    by_row = jnp.sum(hidden_gram * grad_gram, axis=0)
    by_row = jnp.sum(by_row.reshape(n_dp * rows_here, toks // rows_here), axis=1)

    offs = (jnp.stack([inner, 1 - inner]) * width).astype(jnp.int32)
    grad_gate, grad_up = grads(offs, own, other, down_weight, gate_act, up_act)
    weight_grad = wgrad(offs, hid_all, own_cols, other_cols, order)

    mine = jnp.concatenate([by_row, assign.astype(F32)])
    mine = jnp.pad(mine, (0, 128 - mine.shape[0]))
    every = lax.all_to_all(
        jnp.broadcast_to(mine[None], (n_dp * n_fs, 128)),
        ("dp", "fsdp"), split_axis=0, concat_axis=0, tiled=True,
    ).reshape(n_dp, n_fs, 128)
    rows = n_dp * rows_here
    scale = 1.0 / jnp.sqrt(F32(L) * VAL * FFW * D)
    scores = jnp.sum(every[:, :, :rows], axis=1) * scale
    groups = every[:, 0, rows : rows + rows_here].reshape(rows)
    onehot = (groups[None, :] == jnp.arange(n_dp, dtype=F32)[:, None]).astype(F32)
    group_values = jnp.sum(onehot * scores, axis=1)
    row_scores = lax.dynamic_slice_in_dim(scores, d * rows_here, rows_here, axis=1).T
    return (grad_gate, grad_up, weight_grad, row_scores, group_values)


def per_device_any(gate_act, up_act, out_grad, down_weight, val_hidden, val_grad, assign):
    n_dp = lax.axis_size("dp")
    me = lax.axis_index("dp")
    rows_here = assign.shape[0]
    toks = gate_act.shape[0]
    gate = gate_act.astype(F32)
    up = up_act.astype(F32)
    sig = jax.nn.sigmoid(gate)
    act = gate * sig
    hidden = (act * up).astype(BF16)
    grad_feat = lax.all_gather(out_grad, "dp", axis=0, tiled=True)
    piece = lax.all_gather(out_grad, "fsdp", axis=1, tiled=True)
    hidden_all = lax.all_gather(hidden, "dp", axis=0, tiled=True)
    grad_gram = lax.psum(dot_nt(grad_feat, val_grad), "fsdp")
    grad_cols = lax.all_to_all(piece, "dp", split_axis=1, concat_axis=0, tiled=True)
    grad_hidden = dot_nt(piece, down_weight)
    grad_gate = (grad_hidden * up * sig * (1.0 + gate * (1.0 - sig))).astype(BF16)
    grad_up = (grad_hidden * act).astype(BF16)
    product = dot_nt(hidden_all, val_hidden) * grad_gram
    part = jnp.sum(product.reshape(n_dp * rows_here, toks // rows_here * VAL), axis=1)
    weight_grad = dot_tn(hidden_all, grad_cols).astype(BF16)
    scale = 1.0 / jnp.sqrt(F32(L) * VAL * FFW * D)
    scores = lax.all_gather(lax.psum(part, "fsdp"), "dp") * scale
    groups = lax.all_gather(assign, "dp", tiled=True)
    onehot = (groups[None, :] == jnp.arange(n_dp, dtype=jnp.int32)[:, None]).astype(F32)
    group_values = jnp.sum(onehot * scores, axis=1)
    row_scores = lax.dynamic_slice_in_dim(scores, me * rows_here, rows_here, axis=1).T
    return (grad_gate, grad_up, weight_grad, row_scores, group_values)


def solution(mesh):
    in_specs = (
        P("dp", "fsdp"),
        P("dp", "fsdp"),
        P("dp", "fsdp"),
        P("fsdp", None),
        P("dp", "fsdp"),
        P("dp", "fsdp"),
        P("dp"),
    )
    out_specs = (P("dp", "fsdp"), P("dp", "fsdp"), P("fsdp", "dp"), P("dp", None), P())
    n_dp, n_fs = mesh.shape["dp"], mesh.shape["fsdp"]
    fits = n_dp == 4 and n_fs == 2 * n_dp
    return jax.shard_map(
        per_device if fits else per_device_any,
        mesh=mesh, in_specs=in_specs, out_specs=out_specs, check_vma=False,
    )
```

```python
import functools

import jax
import jax.numpy as jnp
from jax import lax
from jax.experimental import pallas as pl
from jax.experimental.pallas import tpu as pltpu
from jax.sharding import PartitionSpec as P

D = 5120
FFW = 14336
L = 128
VAL = 256

F32 = jnp.float32
BF16 = jnp.bfloat16
VMEM_LIMIT = 48 * 1024 * 1024


def dot_nt(a, b):
    return lax.dot_general(a, b, (((1,), (1,)), ((), ())), preferred_element_type=F32)


def dot_tn(a, b):
    return lax.dot_general(a, b, (((0,), (0,)), ((), ())), preferred_element_type=F32)


def swap(x, axis, k):
    n = lax.axis_size(axis)
    return lax.ppermute(x, axis, [(s, s ^ k) for s in range(n)])


def shift(x, axis, k):
    n = lax.axis_size(axis)
    return lax.ppermute(x, axis, [(s, (s + k) % n) for s in range(n)])


def whole(shape):
    return pl.BlockSpec(shape, lambda *_: (0,) * len(shape))


ANY = pl.BlockSpec(memory_space=pl.ANY)


def params():
    return pltpu.CompilerParams(vmem_limit_bytes=VMEM_LIMIT)


def after_body(*refs):
    pass


def after(x, *order):
    return pl.pallas_call(
        after_body,
        in_specs=[ANY] * (1 + len(order)),
        out_specs=ANY,
        out_shape=jax.ShapeDtypeStruct(x.shape, x.dtype),
        input_output_aliases={0: 0},
        name="after",
    )(x, *order)


def hidden_body(gate_ref, up_ref, out_ref):
    gate = gate_ref[...].astype(F32)
    up = up_ref[...].astype(F32)
    out_ref[...] = (gate * jax.nn.sigmoid(gate) * up).astype(BF16).T


def hidden_units(gate, up):
    toks, units = gate.shape
    tile = 256
    cols = pl.BlockSpec((toks, tile), lambda i: (0, i))
    return pl.pallas_call(
        hidden_body,
        grid=(units // tile,),
        in_specs=[cols, cols],
        out_specs=pl.BlockSpec((tile, toks), lambda i: (i, 0)),
        out_shape=jax.ShapeDtypeStruct((units, toks), BF16),
        compiler_params=params(),
        cost_estimate=pl.CostEstimate(
            flops=4 * toks * units, bytes_accessed=6 * toks * units, transcendentals=toks * units
        ),
        name="hidden",
    )(gate, up)


def arrange_body(n, at_ref, *refs):
    blocks, (order_ref, out_ref) = refs[:n], refs[n:]
    for j in range(n):
        out_ref[at_ref[j]] = blocks[j][...]


def arrange(at, blocks, order, name):
    n = len(blocks)
    vmem = pl.BlockSpec(memory_space=pltpu.VMEM)
    return pl.pallas_call(
        functools.partial(arrange_body, n),
        in_specs=[pl.BlockSpec(memory_space=pltpu.SMEM)] + [vmem] * n + [ANY],
        out_specs=vmem,
        out_shape=jax.ShapeDtypeStruct((n,) + blocks[0].shape, BF16),
        compiler_params=params(),
        cost_estimate=pl.CostEstimate(
            flops=0, bytes_accessed=4 * n * blocks[0].size, transcendentals=0
        ),
        name=name,
    )(at, *blocks, order)


def grads_body(
    offs_ref, own_ref, other_ref, w_ref, gate_ref, up_ref, order_ref, gg_ref, gu_ref, piece
):
    n, toks, width = own_ref.shape

    @pl.when(pl.program_id(0) == 0)
    def _():
        for half, ref in enumerate((own_ref, other_ref)):
            for j in range(n):
                place = pl.multiple_of(offs_ref[half] + 2 * j * width, 128)
                piece[:, pl.ds(place, width)] = ref[j]

    total = dot_nt(piece[...], w_ref[...])
    gate = gate_ref[...].astype(F32)
    up = up_ref[...].astype(F32)
    sig = jax.nn.sigmoid(gate)
    gg_ref[...] = (total * up * sig * (1.0 + gate * (1.0 - sig))).astype(BF16)
    gu_ref[...] = (total * (gate * sig)).astype(BF16)


def grads(offs, own, other, weight, gate, up, order):
    n, toks, width = own.shape
    units, feats = weight.shape
    tile = 256
    cols = pl.BlockSpec((toks, tile), lambda i, _: (0, i))
    out = jax.ShapeDtypeStruct((toks, units), BF16)
    return pl.pallas_call(
        grads_body,
        grid_spec=pltpu.PrefetchScalarGridSpec(
            num_scalar_prefetch=1,
            grid=(units // tile,),
            in_specs=[whole(own.shape)] * 2
            + [pl.BlockSpec((tile, feats), lambda i, _: (i, 0)), cols, cols, ANY],
            out_specs=[cols, cols],
            scratch_shapes=[pltpu.VMEM((toks, feats), BF16)],
        ),
        out_shape=(out, out),
        compiler_params=params(),
        cost_estimate=pl.CostEstimate(
            flops=2 * toks * units * feats,
            bytes_accessed=2 * (units * feats + toks * feats + 4 * toks * units),
            transcendentals=toks * units,
        ),
        name="grads",
    )(offs, own, other, weight, gate, up, order)


def wgrad_body(offs_ref, hid_ref, own_ref, other_ref, order_ref, out_ref, cols):
    n, toks, width = own_ref.shape

    @pl.when(pl.program_id(0) == 0)
    def _():
        for half, ref in enumerate((own_ref, other_ref)):
            place = pl.ds(pl.multiple_of(offs_ref[half], 128), width)
            for k in range(n):
                cols[k * toks : (k + 1) * toks, place] = ref[k]

    out_ref[...] = lax.dot_general(
        hid_ref[...], cols[...], (((1,), (0,)), ((), ())), preferred_element_type=F32
    ).astype(BF16)


def wgrad(offs, hid, own, other, order):
    units, total = hid.shape
    width = own.shape[2]
    tile = units // 4
    return pl.pallas_call(
        wgrad_body,
        grid_spec=pltpu.PrefetchScalarGridSpec(
            num_scalar_prefetch=1,
            grid=(units // tile,),
            in_specs=[pl.BlockSpec((tile, total), lambda i, _: (i, 0))]
            + [whole(own.shape)] * 2
            + [ANY],
            out_specs=pl.BlockSpec((tile, 2 * width), lambda i, _: (i, 0)),
            scratch_shapes=[pltpu.VMEM((total, 2 * width), BF16)],
        ),
        out_shape=jax.ShapeDtypeStruct((units, 2 * width), BF16),
        compiler_params=params(),
        cost_estimate=pl.CostEstimate(
            flops=4 * total * units * width,
            bytes_accessed=2 * (total * (units + 2 * width) + 2 * units * width),
            transcendentals=0,
        ),
        name="wgrad",
    )(offs, hid, own, other, order)


def put_slices(inner_ref, part, kept_ref, away_ref):
    outer, size, _ = kept_ref.shape
    for inner in range(2):

        @pl.when(inner_ref[0] == inner)
        def _():
            for p in range(2 * outer):
                out_ref = kept_ref if p % 2 == inner else away_ref
                out_ref[p // 2] = part[p * size : (p + 1) * size]


def grad_gram_body(inner_ref, offs_ref, *refs):
    toks_refs, (val_ref, order_ref, kept_ref, away_ref, wide) = refs[:-5], refs[-5:]
    for k, ref in enumerate(toks_refs):
        toks = ref.shape[0]
        wide[:, pl.ds(pl.multiple_of(offs_ref[k], 128), toks)] = dot_nt(val_ref[...], ref[...])
    put_slices(inner_ref, wide, kept_ref, away_ref)


def hidden_gram_body(inner_ref, offs_ref, *refs):
    hid, (val_ref, order_ref, kept_ref, away_ref, all_ref, wide) = refs[:-6], refs[-6:]
    for k, ref in enumerate(hid):
        toks = ref.shape[1]
        all_ref[:, pl.ds(pl.multiple_of(offs_ref[k], 128), toks)] = ref[...]
    wide[...] = lax.dot_general(
        val_ref[...], all_ref[...], (((1,), (0,)), ((), ())), preferred_element_type=F32
    )
    put_slices(inner_ref, wide, kept_ref, away_ref)


def gram_call(body, inner, offs, operands, order, parts, extra, name):
    smem = pl.BlockSpec(memory_space=pltpu.SMEM)
    vmem = pl.BlockSpec(memory_space=pltpu.VMEM)
    *toks, vals = operands
    total = sum(x.size for x in toks) // vals.shape[1]
    half = jax.ShapeDtypeStruct((parts // 2, vals.shape[0] // parts, total), F32)
    shapes = [half, half, *extra]
    return pl.pallas_call(
        body,
        in_specs=[smem, smem] + [vmem] * len(operands) + [ANY],
        out_specs=[vmem] * len(shapes),
        out_shape=shapes,
        scratch_shapes=[pltpu.VMEM((vals.shape[0], total), F32)],
        compiler_params=params(),
        cost_estimate=pl.CostEstimate(
            flops=2 * vals.size * total,
            bytes_accessed=sum(x.size * x.dtype.itemsize for x in [*operands, *shapes]),
            transcendentals=0,
        ),
        name=name,
    )(inner, offs, *operands, order)


def add_body(a_ref, b_ref, order_ref, out_ref):
    out_ref[...] = a_ref[...] + b_ref[...]


def add(a, b, order, name):
    vmem = pl.BlockSpec(memory_space=pltpu.VMEM)
    return pl.pallas_call(
        add_body,
        in_specs=[vmem, vmem, ANY],
        out_specs=vmem,
        out_shape=jax.ShapeDtypeStruct(a.shape, a.dtype),
        compiler_params=params(),
        cost_estimate=pl.CostEstimate(
            flops=a.size, bytes_accessed=12 * a.size, transcendentals=0
        ),
        name=name,
    )(a, b, order)


def spread(pair):
    n_fs = lax.axis_size("fsdp")
    groups = [list(range(x, n_fs, 2)) for x in range(2)]
    return lax.all_to_all(
        pair, "fsdp", split_axis=0, concat_axis=0, axis_index_groups=groups, tiled=True
    )


def line_body(rows, assign_ref, hid_ref, grad_ref, out_ref):
    n, _, total = hid_ref.shape
    hid, grad = hid_ref[0], grad_ref[0]
    for j in range(1, n):
        hid += hid_ref[j]
        grad += grad_ref[j]
    by_tok = jnp.sum(hid * grad, axis=0, keepdims=True)
    size = total // rows
    lane = lax.broadcasted_iota(jnp.int32, (1, 128), 1)
    line = jnp.zeros((1, 128), F32)
    for r in range(rows):
        row = jnp.sum(by_tok[:, r * size : (r + 1) * size], axis=1, keepdims=True)
        line = jnp.where(lane == r, row, line)
    for r in range(assign_ref.shape[0]):
        line = jnp.where(lane == rows + r, assign_ref[r].astype(F32), line)
    out_ref[...] = jnp.broadcast_to(line, out_ref.shape)


def score_line(assign, hid, grad, rows, copies):
    vmem = pl.BlockSpec(memory_space=pltpu.VMEM)
    return pl.pallas_call(
        functools.partial(line_body, rows),
        in_specs=[pl.BlockSpec(memory_space=pltpu.SMEM), vmem, vmem],
        out_specs=vmem,
        out_shape=jax.ShapeDtypeStruct((copies, 128), F32),
        compiler_params=params(),
        cost_estimate=pl.CostEstimate(
            flops=4 * hid.size, bytes_accessed=8 * hid.size, transcendentals=0
        ),
        name="score_line",
    )(assign, hid, grad)


def per_device(gate_act, up_act, out_grad, down_weight, val_hidden, val_grad, assign):
    n_dp = lax.axis_size("dp")
    n_fs = lax.axis_size("fsdp")
    d = lax.axis_index("dp")
    f = lax.axis_index("fsdp")
    rows_here = assign.shape[0]
    toks, width = out_grad.shape
    units = gate_act.shape[1]
    total = n_dp * toks
    n_out = n_fs // 2
    outer, inner = f // 2, f % 2

    first = shift(out_grad, "fsdp", 2)
    others = [swap(out_grad, "fsdp", 1)]
    far = swap(out_grad, "dp", 2)
    near = swap(out_grad, "dp", 1)
    first = after(first, others[0], far, near)
    hidden = after(hidden_units(gate_act, up_act), first)
    grad_dp = [out_grad, near, far, swap(far, "dp", 1)]
    far = swap(hidden, "dp", 2)
    ring = [out_grad, first]
    for _ in range(n_out - 2):
        others.append(swap(ring[-1], "fsdp", 1))
        ring.append(after(shift(ring[-1], "fsdp", 2), others[-1]))
    others.append(swap(ring[-1], "fsdp", 1))

    at = (outer - jnp.arange(n_out, dtype=jnp.int32)) % n_out
    own = arrange(at, ring, others[1], "own_features")
    own_cols = lax.all_to_all(own, "dp", split_axis=0, concat_axis=0, tiled=True)

    tok_offs = (d ^ jnp.arange(n_dp, dtype=jnp.int32)) * toks
    inner_at = inner.reshape(1).astype(jnp.int32)
    grad_kept, away = gram_call(
        grad_gram_body, inner_at, tok_offs, [*grad_dp, val_grad], own, n_fs, [], "grad_gram"
    )
    grad_came = swap(away, "fsdp", 1)

    far = after(far, away, others[2])
    hid_dp = [hidden, swap(hidden, "dp", 1), far, swap(far, "dp", 1)]

    other = arrange(at, others, far, "other_features")
    other_cols = lax.all_to_all(other, "dp", split_axis=0, concat_axis=0, tiled=True)

    hid_kept, away, hid_all = gram_call(
        hidden_gram_body, inner_at, tok_offs, [*hid_dp, val_hidden], other, n_fs,
        [jax.ShapeDtypeStruct((units, total), BF16)], "hidden_gram",
    )
    hid_came = swap(away, "fsdp", 1)
    grad_sums = spread(add(grad_kept, grad_came, away, "grad_pair"))
    pair = add(hid_kept, hid_came, grad_came, "hidden_pair")
    hid_sums = spread(pair)

    offs = (jnp.stack([inner, 1 - inner]) * width).astype(jnp.int32)
    grad_gate, grad_up = grads(offs, own, other, down_weight, gate_act, up_act, pair)

    mine = score_line(assign, hid_sums, grad_sums, n_dp * rows_here, n_dp * n_fs)
    every = lax.all_to_all(
        mine, ("dp", "fsdp"), split_axis=0, concat_axis=0, tiled=True
    ).reshape(n_dp, n_fs, 128)
    weight_grad = wgrad(offs, hid_all, own_cols, other_cols, mine)

    rows = n_dp * rows_here
    scale = 1.0 / jnp.sqrt(F32(L) * VAL * FFW * D)
    scores = jnp.sum(every[:, :, :rows], axis=1) * scale
    groups = every[:, 0, rows : rows + rows_here].reshape(rows)
    onehot = (groups[None, :] == jnp.arange(n_dp, dtype=F32)[:, None]).astype(F32)
    group_values = jnp.sum(onehot * scores, axis=1)
    row_scores = lax.dynamic_slice_in_dim(scores, d * rows_here, rows_here, axis=1).T
    return (grad_gate, grad_up, weight_grad, row_scores, group_values)


def per_device_any(gate_act, up_act, out_grad, down_weight, val_hidden, val_grad, assign):
    n_dp = lax.axis_size("dp")
    me = lax.axis_index("dp")
    rows_here = assign.shape[0]
    toks = gate_act.shape[0]
    gate = gate_act.astype(F32)
    up = up_act.astype(F32)
    sig = jax.nn.sigmoid(gate)
    act = gate * sig
    hidden = (act * up).astype(BF16)
    grad_feat = lax.all_gather(out_grad, "dp", axis=0, tiled=True)
    piece = lax.all_gather(out_grad, "fsdp", axis=1, tiled=True)
    hidden_all = lax.all_gather(hidden, "dp", axis=0, tiled=True)
    grad_gram = lax.psum(dot_nt(grad_feat, val_grad), "fsdp")
    grad_cols = lax.all_to_all(piece, "dp", split_axis=1, concat_axis=0, tiled=True)
    grad_hidden = dot_nt(piece, down_weight)
    grad_gate = (grad_hidden * up * sig * (1.0 + gate * (1.0 - sig))).astype(BF16)
    grad_up = (grad_hidden * act).astype(BF16)
    product = dot_nt(hidden_all, val_hidden) * grad_gram
    part = jnp.sum(product.reshape(n_dp * rows_here, toks // rows_here * VAL), axis=1)
    weight_grad = dot_tn(hidden_all, grad_cols).astype(BF16)
    scale = 1.0 / jnp.sqrt(F32(L) * VAL * FFW * D)
    scores = lax.all_gather(lax.psum(part, "fsdp"), "dp") * scale
    groups = lax.all_gather(assign, "dp", tiled=True)
    onehot = (groups[None, :] == jnp.arange(n_dp, dtype=jnp.int32)[:, None]).astype(F32)
    group_values = jnp.sum(onehot * scores, axis=1)
    row_scores = lax.dynamic_slice_in_dim(scores, me * rows_here, rows_here, axis=1).T
    return (grad_gate, grad_up, weight_grad, row_scores, group_values)


def solution(mesh):
    in_specs = (
        P("dp", "fsdp"),
        P("dp", "fsdp"),
        P("dp", "fsdp"),
        P("fsdp", None),
        P("dp", "fsdp"),
        P("dp", "fsdp"),
        P("dp"),
    )
    out_specs = (P("dp", "fsdp"), P("dp", "fsdp"), P("fsdp", "dp"), P("dp", None), P())
    n_dp, n_fs = mesh.shape["dp"], mesh.shape["fsdp"]
    fits = n_dp == 4 and n_fs == 2 * n_dp
    return jax.shard_map(
        per_device if fits else per_device_any,
        mesh=mesh, in_specs=in_specs, out_specs=out_specs, check_vma=False,
    )
```

```python
import functools

import jax
import jax.numpy as jnp
from jax import lax
from jax.experimental import pallas as pl
from jax.experimental.pallas import tpu as pltpu
from jax.sharding import PartitionSpec as P

D = 5120
FFW = 14336
L = 128
VAL = 256

F32 = jnp.float32
BF16 = jnp.bfloat16
VMEM_LIMIT = 48 * 1024 * 1024


def dot_nt(a, b):
    return lax.dot_general(a, b, (((1,), (1,)), ((), ())), preferred_element_type=F32)


def dot_tn(a, b):
    return lax.dot_general(a, b, (((0,), (0,)), ((), ())), preferred_element_type=F32)


def swap(x, axis, k):
    n = lax.axis_size(axis)
    return lax.ppermute(x, axis, [(s, s ^ k) for s in range(n)])


def shift(x, axis, k):
    n = lax.axis_size(axis)
    return lax.ppermute(x, axis, [(s, (s + k) % n) for s in range(n)])


def whole(shape):
    return pl.BlockSpec(shape, lambda *_: (0,) * len(shape))


ANY = pl.BlockSpec(memory_space=pl.ANY)
SMALL = pl.CostEstimate(flops=1024, bytes_accessed=1024, transcendentals=0)


def params():
    return pltpu.CompilerParams(vmem_limit_bytes=VMEM_LIMIT)


def after_body(*refs):
    pass


def after(x, *order):
    return pl.pallas_call(
        after_body,
        in_specs=[ANY] * (1 + len(order)),
        out_specs=ANY,
        out_shape=jax.ShapeDtypeStruct(x.shape, x.dtype),
        input_output_aliases={0: 0},
        cost_estimate=SMALL,
        name="after",
    )(x, *order)


def hidden_body(gate_ref, up_ref, out_ref):
    gate = gate_ref[...].astype(F32)
    up = up_ref[...].astype(F32)
    out_ref[...] = (gate * jax.nn.sigmoid(gate) * up).astype(BF16).T


def hidden_units(gate, up):
    toks, units = gate.shape
    tile = 256
    cols = pl.BlockSpec((toks, tile), lambda i: (0, i))
    return pl.pallas_call(
        hidden_body,
        grid=(units // tile,),
        in_specs=[cols, cols],
        out_specs=pl.BlockSpec((tile, toks), lambda i: (i, 0)),
        out_shape=jax.ShapeDtypeStruct((units, toks), BF16),
        compiler_params=params(),
        cost_estimate=SMALL,
        name="hidden",
    )(gate, up)


def arrange_body(n, at_ref, *refs):
    blocks, (order_ref, out_ref) = refs[:n], refs[n:]
    for j in range(n):
        out_ref[at_ref[j]] = blocks[j][...]


def arrange(at, blocks, order, name):
    n = len(blocks)
    vmem = pl.BlockSpec(memory_space=pltpu.VMEM)
    return pl.pallas_call(
        functools.partial(arrange_body, n),
        in_specs=[pl.BlockSpec(memory_space=pltpu.SMEM)] + [vmem] * n + [ANY],
        out_specs=vmem,
        out_shape=jax.ShapeDtypeStruct((n,) + blocks[0].shape, BF16),
        compiler_params=params(),
        cost_estimate=SMALL,
        name=name,
    )(at, *blocks, order)


def grads_body(
    offs_ref, own_ref, other_ref, w_ref, gate_ref, up_ref, order_ref, gg_ref, gu_ref, piece
):
    n, toks, width = own_ref.shape

    @pl.when(pl.program_id(0) == 0)
    def _():
        for half, ref in enumerate((own_ref, other_ref)):
            for j in range(n):
                place = pl.multiple_of(offs_ref[half] + 2 * j * width, 128)
                piece[:, pl.ds(place, width)] = ref[j]

    total = dot_nt(piece[...], w_ref[...])
    gate = gate_ref[...].astype(F32)
    up = up_ref[...].astype(F32)
    sig = jax.nn.sigmoid(gate)
    gg_ref[...] = (total * up * sig * (1.0 + gate * (1.0 - sig))).astype(BF16)
    gu_ref[...] = (total * (gate * sig)).astype(BF16)


def grads(offs, own, other, weight, gate, up, order):
    n, toks, width = own.shape
    units, feats = weight.shape
    tile = 256
    cols = pl.BlockSpec((toks, tile), lambda i, _: (0, i))
    out = jax.ShapeDtypeStruct((toks, units), BF16)
    return pl.pallas_call(
        grads_body,
        grid_spec=pltpu.PrefetchScalarGridSpec(
            num_scalar_prefetch=1,
            grid=(units // tile,),
            in_specs=[whole(own.shape)] * 2
            + [pl.BlockSpec((tile, feats), lambda i, _: (i, 0)), cols, cols, ANY],
            out_specs=[cols, cols],
            scratch_shapes=[pltpu.VMEM((toks, feats), BF16)],
        ),
        out_shape=(out, out),
        compiler_params=params(),
        cost_estimate=SMALL,
        name="grads",
    )(offs, own, other, weight, gate, up, order)


def wgrad_body(offs_ref, hid_ref, own_ref, other_ref, order_ref, out_ref, cols):
    n, toks, width = own_ref.shape

    @pl.when(pl.program_id(0) == 0)
    def _():
        for half, ref in enumerate((own_ref, other_ref)):
            place = pl.ds(pl.multiple_of(offs_ref[half], 128), width)
            for k in range(n):
                cols[k * toks : (k + 1) * toks, place] = ref[k]

    out_ref[...] = lax.dot_general(
        hid_ref[...], cols[...], (((1,), (0,)), ((), ())), preferred_element_type=F32
    ).astype(BF16)


def wgrad(offs, hid, own, other, order):
    units, total = hid.shape
    width = own.shape[2]
    tile = units // 4
    return pl.pallas_call(
        wgrad_body,
        grid_spec=pltpu.PrefetchScalarGridSpec(
            num_scalar_prefetch=1,
            grid=(units // tile,),
            in_specs=[pl.BlockSpec((tile, total), lambda i, _: (i, 0))]
            + [whole(own.shape)] * 2
            + [ANY],
            out_specs=pl.BlockSpec((tile, 2 * width), lambda i, _: (i, 0)),
            scratch_shapes=[pltpu.VMEM((total, 2 * width), BF16)],
        ),
        out_shape=jax.ShapeDtypeStruct((units, 2 * width), BF16),
        compiler_params=params(),
        cost_estimate=SMALL,
        name="wgrad",
    )(offs, hid, own, other, order)


def put_slices(inner_ref, part, kept_ref, away_ref):
    outer, size, _ = kept_ref.shape
    for inner in range(2):

        @pl.when(inner_ref[0] == inner)
        def _():
            for p in range(2 * outer):
                out_ref = kept_ref if p % 2 == inner else away_ref
                out_ref[p // 2] = part[p * size : (p + 1) * size]


def grad_gram_body(inner_ref, offs_ref, *refs):
    toks_refs, (val_ref, order_ref, kept_ref, away_ref, wide) = refs[:-5], refs[-5:]
    for k, ref in enumerate(toks_refs):
        toks = ref.shape[0]
        wide[:, pl.ds(pl.multiple_of(offs_ref[k], 128), toks)] = dot_nt(val_ref[...], ref[...])
    put_slices(inner_ref, wide, kept_ref, away_ref)


def hidden_gram_body(inner_ref, offs_ref, *refs):
    hid, (val_ref, order_ref, kept_ref, away_ref, all_ref, wide) = refs[:-6], refs[-6:]
    for k, ref in enumerate(hid):
        toks = ref.shape[1]
        all_ref[:, pl.ds(pl.multiple_of(offs_ref[k], 128), toks)] = ref[...]
    wide[...] = lax.dot_general(
        val_ref[...], all_ref[...], (((1,), (0,)), ((), ())), preferred_element_type=F32
    )
    put_slices(inner_ref, wide, kept_ref, away_ref)


def gram_call(body, inner, offs, operands, order, parts, extra, name):
    smem = pl.BlockSpec(memory_space=pltpu.SMEM)
    vmem = pl.BlockSpec(memory_space=pltpu.VMEM)
    *toks, vals = operands
    total = sum(x.size for x in toks) // vals.shape[1]
    half = jax.ShapeDtypeStruct((parts // 2, vals.shape[0] // parts, total), F32)
    shapes = [half, half, *extra]
    return pl.pallas_call(
        body,
        in_specs=[smem, smem] + [vmem] * len(operands) + [ANY],
        out_specs=[vmem] * len(shapes),
        out_shape=shapes,
        scratch_shapes=[pltpu.VMEM((vals.shape[0], total), F32)],
        compiler_params=params(),
        cost_estimate=SMALL,
        name=name,
    )(inner, offs, *operands, order)


def add_body(a_ref, b_ref, order_ref, out_ref):
    out_ref[...] = a_ref[...] + b_ref[...]


def add(a, b, order, name):
    vmem = pl.BlockSpec(memory_space=pltpu.VMEM)
    return pl.pallas_call(
        add_body,
        in_specs=[vmem, vmem, ANY],
        out_specs=vmem,
        out_shape=jax.ShapeDtypeStruct(a.shape, a.dtype),
        compiler_params=params(),
        cost_estimate=SMALL,
        name=name,
    )(a, b, order)


def spread(pair):
    n_fs = lax.axis_size("fsdp")
    groups = [list(range(x, n_fs, 2)) for x in range(2)]
    return lax.all_to_all(
        pair, "fsdp", split_axis=0, concat_axis=0, axis_index_groups=groups, tiled=True
    )


def line_body(rows, assign_ref, hid_ref, grad_ref, out_ref):
    n, _, total = hid_ref.shape
    hid, grad = hid_ref[0], grad_ref[0]
    for j in range(1, n):
        hid += hid_ref[j]
        grad += grad_ref[j]
    by_tok = jnp.sum(hid * grad, axis=0, keepdims=True)
    size = total // rows
    lane = lax.broadcasted_iota(jnp.int32, (1, 128), 1)
    line = jnp.zeros((1, 128), F32)
    for r in range(rows):
        row = jnp.sum(by_tok[:, r * size : (r + 1) * size], axis=1, keepdims=True)
        line = jnp.where(lane == r, row, line)
    for r in range(assign_ref.shape[0]):
        line = jnp.where(lane == rows + r, assign_ref[r].astype(F32), line)
    out_ref[...] = jnp.broadcast_to(line, out_ref.shape)


def score_line(assign, hid, grad, rows, copies):
    vmem = pl.BlockSpec(memory_space=pltpu.VMEM)
    return pl.pallas_call(
        functools.partial(line_body, rows),
        in_specs=[pl.BlockSpec(memory_space=pltpu.SMEM), vmem, vmem],
        out_specs=vmem,
        out_shape=jax.ShapeDtypeStruct((copies, 128), F32),
        compiler_params=params(),
        cost_estimate=SMALL,
        name="score_line",
    )(assign, hid, grad)


def per_device(gate_act, up_act, out_grad, down_weight, val_hidden, val_grad, assign):
    n_dp = lax.axis_size("dp")
    n_fs = lax.axis_size("fsdp")
    d = lax.axis_index("dp")
    f = lax.axis_index("fsdp")
    rows_here = assign.shape[0]
    toks, width = out_grad.shape
    units = gate_act.shape[1]
    total = n_dp * toks
    n_out = n_fs // 2
    outer, inner = f // 2, f % 2

    first = shift(out_grad, "fsdp", 2)
    others = [swap(out_grad, "fsdp", 1)]
    far = swap(out_grad, "dp", 2)
    near = swap(out_grad, "dp", 1)
    first = after(first, others[0], far, near)
    hidden = after(hidden_units(gate_act, up_act), first)
    grad_dp = [out_grad, near, far, swap(far, "dp", 1)]
    far = swap(hidden, "dp", 2)
    ring = [out_grad, first]
    for _ in range(n_out - 2):
        others.append(swap(ring[-1], "fsdp", 1))
        ring.append(after(shift(ring[-1], "fsdp", 2), others[-1]))
    others.append(swap(ring[-1], "fsdp", 1))

    at = (outer - jnp.arange(n_out, dtype=jnp.int32)) % n_out
    own = arrange(at, ring, others[1], "own_features")
    own_cols = lax.all_to_all(own, "dp", split_axis=0, concat_axis=0, tiled=True)

    tok_offs = (d ^ jnp.arange(n_dp, dtype=jnp.int32)) * toks
    inner_at = inner.reshape(1).astype(jnp.int32)
    grad_kept, away = gram_call(
        grad_gram_body, inner_at, tok_offs, [*grad_dp, val_grad], own, n_fs, [], "grad_gram"
    )
    grad_came = swap(away, "fsdp", 1)

    far = after(far, away, others[2])
    hid_dp = [hidden, swap(hidden, "dp", 1), far, swap(far, "dp", 1)]

    other = arrange(at, others, far, "other_features")
    other_cols = lax.all_to_all(other, "dp", split_axis=0, concat_axis=0, tiled=True)

    hid_kept, away, hid_all = gram_call(
        hidden_gram_body, inner_at, tok_offs, [*hid_dp, val_hidden], other, n_fs,
        [jax.ShapeDtypeStruct((units, total), BF16)], "hidden_gram",
    )
    hid_came = swap(away, "fsdp", 1)
    grad_sums = spread(add(grad_kept, grad_came, away, "grad_pair"))
    pair = add(hid_kept, hid_came, grad_came, "hidden_pair")
    hid_sums = spread(pair)

    offs = (jnp.stack([inner, 1 - inner]) * width).astype(jnp.int32)
    grad_gate, grad_up = grads(offs, own, other, down_weight, gate_act, up_act, pair)

    mine = score_line(assign, hid_sums, grad_sums, n_dp * rows_here, n_dp * n_fs)
    every = lax.all_to_all(
        mine, ("dp", "fsdp"), split_axis=0, concat_axis=0, tiled=True
    ).reshape(n_dp, n_fs, 128)
    weight_grad = wgrad(offs, hid_all, own_cols, other_cols, mine)

    rows = n_dp * rows_here
    scale = 1.0 / jnp.sqrt(F32(L) * VAL * FFW * D)
    scores = jnp.sum(every[:, :, :rows], axis=1) * scale
    groups = every[:, 0, rows : rows + rows_here].reshape(rows)
    onehot = (groups[None, :] == jnp.arange(n_dp, dtype=F32)[:, None]).astype(F32)
    group_values = jnp.sum(onehot * scores, axis=1)
    row_scores = lax.dynamic_slice_in_dim(scores, d * rows_here, rows_here, axis=1).T
    return (grad_gate, grad_up, weight_grad, row_scores, group_values)


def per_device_any(gate_act, up_act, out_grad, down_weight, val_hidden, val_grad, assign):
    n_dp = lax.axis_size("dp")
    me = lax.axis_index("dp")
    rows_here = assign.shape[0]
    toks = gate_act.shape[0]
    gate = gate_act.astype(F32)
    up = up_act.astype(F32)
    sig = jax.nn.sigmoid(gate)
    act = gate * sig
    hidden = (act * up).astype(BF16)
    grad_feat = lax.all_gather(out_grad, "dp", axis=0, tiled=True)
    piece = lax.all_gather(out_grad, "fsdp", axis=1, tiled=True)
    hidden_all = lax.all_gather(hidden, "dp", axis=0, tiled=True)
    grad_gram = lax.psum(dot_nt(grad_feat, val_grad), "fsdp")
    grad_cols = lax.all_to_all(piece, "dp", split_axis=1, concat_axis=0, tiled=True)
    grad_hidden = dot_nt(piece, down_weight)
    grad_gate = (grad_hidden * up * sig * (1.0 + gate * (1.0 - sig))).astype(BF16)
    grad_up = (grad_hidden * act).astype(BF16)
    product = dot_nt(hidden_all, val_hidden) * grad_gram
    part = jnp.sum(product.reshape(n_dp * rows_here, toks // rows_here * VAL), axis=1)
    weight_grad = dot_tn(hidden_all, grad_cols).astype(BF16)
    scale = 1.0 / jnp.sqrt(F32(L) * VAL * FFW * D)
    scores = lax.all_gather(lax.psum(part, "fsdp"), "dp") * scale
    groups = lax.all_gather(assign, "dp", tiled=True)
    onehot = (groups[None, :] == jnp.arange(n_dp, dtype=jnp.int32)[:, None]).astype(F32)
    group_values = jnp.sum(onehot * scores, axis=1)
    row_scores = lax.dynamic_slice_in_dim(scores, me * rows_here, rows_here, axis=1).T
    return (grad_gate, grad_up, weight_grad, row_scores, group_values)


def solution(mesh):
    in_specs = (
        P("dp", "fsdp"),
        P("dp", "fsdp"),
        P("dp", "fsdp"),
        P("fsdp", None),
        P("dp", "fsdp"),
        P("dp", "fsdp"),
        P("dp"),
    )
    out_specs = (P("dp", "fsdp"), P("dp", "fsdp"), P("fsdp", "dp"), P("dp", None), P())
    n_dp, n_fs = mesh.shape["dp"], mesh.shape["fsdp"]
    fits = n_dp == 4 and n_fs == 2 * n_dp
    return jax.shard_map(
        per_device if fits else per_device_any,
        mesh=mesh, in_specs=in_specs, out_specs=out_specs, check_vma=False,
    )
```

```python
import functools

import jax
import jax.numpy as jnp
from jax import lax
from jax.experimental import pallas as pl
from jax.experimental.pallas import tpu as pltpu
from jax.sharding import PartitionSpec as P

D = 5120
FFW = 14336
L = 128
VAL = 256

F32 = jnp.float32
BF16 = jnp.bfloat16
VMEM_LIMIT = 32 * 1024 * 1024


def dot_nt(a, b):
    return lax.dot_general(a, b, (((1,), (1,)), ((), ())), preferred_element_type=F32)


def dot_tn(a, b):
    return lax.dot_general(a, b, (((0,), (0,)), ((), ())), preferred_element_type=F32)


def swap(x, axis, k):
    n = lax.axis_size(axis)
    return lax.ppermute(x, axis, [(s, s ^ k) for s in range(n)])


def shift(x, axis, k):
    n = lax.axis_size(axis)
    return lax.ppermute(x, axis, [(s, (s + k) % n) for s in range(n)])


def whole(shape):
    return pl.BlockSpec(shape, lambda *_: (0,) * len(shape))


ANY = pl.BlockSpec(memory_space=pl.ANY)
SMALL = pl.CostEstimate(flops=1024, bytes_accessed=1024, transcendentals=0)


def params():
    return pltpu.CompilerParams(vmem_limit_bytes=VMEM_LIMIT)


def after_body(*refs):
    pass


def after(x, *order):
    return pl.pallas_call(
        after_body,
        in_specs=[ANY] * (1 + len(order)),
        out_specs=ANY,
        out_shape=jax.ShapeDtypeStruct(x.shape, x.dtype),
        input_output_aliases={0: 0},
        cost_estimate=SMALL,
        name="after",
    )(x, *order)


def hidden_body(gate_ref, up_ref, out_ref):
    gate = gate_ref[...].astype(F32)
    up = up_ref[...].astype(F32)
    out_ref[...] = (gate * jax.nn.sigmoid(gate) * up).astype(BF16).T


def hidden_units(gate, up):
    toks, units = gate.shape
    tile = 256
    cols = pl.BlockSpec((toks, tile), lambda i: (0, i))
    return pl.pallas_call(
        hidden_body,
        grid=(units // tile,),
        in_specs=[cols, cols],
        out_specs=pl.BlockSpec((tile, toks), lambda i: (i, 0)),
        out_shape=jax.ShapeDtypeStruct((units, toks), BF16),
        compiler_params=params(),
        cost_estimate=SMALL,
        name="hidden",
    )(gate, up)


def arrange_body(n, at_ref, *refs):
    blocks, (order_ref, out_ref, sems) = refs[:n], refs[n:]
    copies = [
        pltpu.make_async_copy(blocks[j], out_ref.at[at_ref[j]], sems.at[j]) for j in range(n)
    ]
    for copy in copies:
        copy.start()
    for copy in copies:
        copy.wait()


def arrange(at, blocks, order, name):
    n = len(blocks)
    return pl.pallas_call(
        functools.partial(arrange_body, n),
        in_specs=[pl.BlockSpec(memory_space=pltpu.SMEM)] + [ANY] * (n + 1),
        out_specs=ANY,
        out_shape=jax.ShapeDtypeStruct((n,) + blocks[0].shape, BF16),
        scratch_shapes=[pltpu.SemaphoreType.DMA((n,))],
        compiler_params=params(),
        cost_estimate=SMALL,
        name=name,
    )(at, *blocks, order)


def grads_body(
    offs_ref, own_ref, other_ref, w_ref, gate_ref, up_ref, order_ref, gg_ref, gu_ref, piece
):
    n, toks, width = own_ref.shape

    @pl.when(pl.program_id(0) == 0)
    def _():
        for half, ref in enumerate((own_ref, other_ref)):
            for j in range(n):
                place = pl.multiple_of(offs_ref[half] + 2 * j * width, 128)
                piece[:, pl.ds(place, width)] = ref[j]

    total = dot_nt(piece[...], w_ref[...])
    gate = gate_ref[...].astype(F32)
    up = up_ref[...].astype(F32)
    sig = jax.nn.sigmoid(gate)
    gg_ref[...] = (total * up * sig * (1.0 + gate * (1.0 - sig))).astype(BF16)
    gu_ref[...] = (total * (gate * sig)).astype(BF16)


def grads(offs, own, other, weight, gate, up, order):
    n, toks, width = own.shape
    units, feats = weight.shape
    tile = 256
    cols = pl.BlockSpec((toks, tile), lambda i, _: (0, i))
    out = jax.ShapeDtypeStruct((toks, units), BF16)
    return pl.pallas_call(
        grads_body,
        grid_spec=pltpu.PrefetchScalarGridSpec(
            num_scalar_prefetch=1,
            grid=(units // tile,),
            in_specs=[whole(own.shape)] * 2
            + [pl.BlockSpec((tile, feats), lambda i, _: (i, 0)), cols, cols, ANY],
            out_specs=[cols, cols],
            scratch_shapes=[pltpu.VMEM((toks, feats), BF16)],
        ),
        out_shape=(out, out),
        compiler_params=params(),
        cost_estimate=pl.CostEstimate(
            flops=2 * toks * units * feats,
            bytes_accessed=2 * (units * feats + toks * feats + 4 * toks * units),
            transcendentals=toks * units,
        ),
        name="grads",
    )(offs, own, other, weight, gate, up, order)


def wgrad_body(offs_ref, hid_ref, own_ref, other_ref, order_ref, out_ref, cols):
    n, toks, width = own_ref.shape

    @pl.when(pl.program_id(0) == 0)
    def _():
        for half, ref in enumerate((own_ref, other_ref)):
            place = pl.ds(pl.multiple_of(offs_ref[half], 128), width)
            for k in range(n):
                cols[k * toks : (k + 1) * toks, place] = ref[k]

    out_ref[...] = lax.dot_general(
        hid_ref[...], cols[...], (((1,), (0,)), ((), ())), preferred_element_type=F32
    ).astype(BF16)


def wgrad(offs, hid, own, other, order):
    units, total = hid.shape
    width = own.shape[2]
    tile = units // 4
    return pl.pallas_call(
        wgrad_body,
        grid_spec=pltpu.PrefetchScalarGridSpec(
            num_scalar_prefetch=1,
            grid=(units // tile,),
            in_specs=[pl.BlockSpec((tile, total), lambda i, _: (i, 0))]
            + [whole(own.shape)] * 2
            + [ANY],
            out_specs=pl.BlockSpec((tile, 2 * width), lambda i, _: (i, 0)),
            scratch_shapes=[pltpu.VMEM((total, 2 * width), BF16)],
        ),
        out_shape=jax.ShapeDtypeStruct((units, 2 * width), BF16),
        compiler_params=params(),
        cost_estimate=pl.CostEstimate(
            flops=4 * total * units * width,
            bytes_accessed=2 * (total * (units + 2 * width) + 2 * units * width),
            transcendentals=0,
        ),
        name="wgrad",
    )(offs, hid, own, other, order)


def put_slices(inner_ref, part, kept_ref, away_ref):
    outer, size, _ = kept_ref.shape
    for inner in range(2):

        @pl.when(inner_ref[0] == inner)
        def _():
            for p in range(2 * outer):
                out_ref = kept_ref if p % 2 == inner else away_ref
                out_ref[p // 2] = part[p * size : (p + 1) * size]


def grad_gram_body(inner_ref, offs_ref, *refs):
    toks_refs, (val_ref, order_ref, kept_ref, away_ref, wide) = refs[:-5], refs[-5:]
    for k, ref in enumerate(toks_refs):
        toks = ref.shape[0]
        wide[:, pl.ds(pl.multiple_of(offs_ref[k], 128), toks)] = dot_nt(val_ref[...], ref[...])
    put_slices(inner_ref, wide, kept_ref, away_ref)


def hidden_gram_body(inner_ref, offs_ref, *refs):
    hid, (val_ref, order_ref, kept_ref, away_ref, all_ref, wide) = refs[:-6], refs[-6:]
    for k, ref in enumerate(hid):
        toks = ref.shape[1]
        all_ref[:, pl.ds(pl.multiple_of(offs_ref[k], 128), toks)] = ref[...]
    wide[...] = lax.dot_general(
        val_ref[...], all_ref[...], (((1,), (0,)), ((), ())), preferred_element_type=F32
    )
    put_slices(inner_ref, wide, kept_ref, away_ref)


def gram_call(body, inner, offs, operands, order, parts, extra, name):
    smem = pl.BlockSpec(memory_space=pltpu.SMEM)
    vmem = pl.BlockSpec(memory_space=pltpu.VMEM)
    *toks, vals = operands
    total = sum(x.size for x in toks) // vals.shape[1]
    half = jax.ShapeDtypeStruct((parts // 2, vals.shape[0] // parts, total), F32)
    shapes = [half, half, *extra]
    return pl.pallas_call(
        body,
        in_specs=[smem, smem] + [vmem] * len(operands) + [ANY],
        out_specs=[vmem] * len(shapes),
        out_shape=shapes,
        scratch_shapes=[pltpu.VMEM((vals.shape[0], total), F32)],
        compiler_params=params(),
        cost_estimate=SMALL,
        name=name,
    )(inner, offs, *operands, order)


def pair_body(n, outer_ref, kept_ref, came_ref, order_ref, *out_refs):
    for step in range(n):
        at = lax.rem(outer_ref[0] + step, n)
        out_refs[step][...] = kept_ref[at] + came_ref[at]


def pair_sum(outer, kept, came, order, name):
    n, *size = kept.shape
    vmem = pl.BlockSpec(memory_space=pltpu.VMEM)
    return pl.pallas_call(
        functools.partial(pair_body, n),
        in_specs=[pl.BlockSpec(memory_space=pltpu.SMEM), vmem, vmem, ANY],
        out_specs=[vmem] * n,
        out_shape=[jax.ShapeDtypeStruct(size, F32)] * n,
        compiler_params=params(),
        cost_estimate=SMALL,
        name=name,
    )(outer, kept, came, order)


def spread(slices):
    return [x if j == 0 else shift(x, "fsdp", 2 * j) for j, x in enumerate(slices)]


def line_body(rows, n, assign_ref, *refs):
    hid, grad, (order_ref, out_ref) = refs[:n], refs[n : 2 * n], refs[2 * n :]
    hid_sum = sum(ref[...] for ref in hid)
    grad_sum = sum(ref[...] for ref in grad)
    by_tok = jnp.sum(hid_sum * grad_sum, axis=0, keepdims=True)
    size = by_tok.shape[1] // rows
    lane = lax.broadcasted_iota(jnp.int32, (1, 128), 1)
    line = jnp.zeros((1, 128), F32)
    for r in range(rows):
        row = jnp.sum(by_tok[:, r * size : (r + 1) * size], axis=1, keepdims=True)
        line = jnp.where(lane == r, row, line)
    for r in range(assign_ref.shape[0]):
        line = jnp.where(lane == rows + r, assign_ref[r].astype(F32), line)
    out_ref[...] = jnp.broadcast_to(line, out_ref.shape)


def score_line(assign, hid, grad, order, rows, copies):
    n = len(hid)
    vmem = pl.BlockSpec(memory_space=pltpu.VMEM)
    return pl.pallas_call(
        functools.partial(line_body, rows, n),
        in_specs=[pl.BlockSpec(memory_space=pltpu.SMEM)] + [vmem] * (2 * n) + [ANY],
        out_specs=vmem,
        out_shape=jax.ShapeDtypeStruct((copies, 128), F32),
        compiler_params=params(),
        cost_estimate=SMALL,
        name="score_line",
    )(assign, *hid, *grad, order)


def per_device(gate_act, up_act, out_grad, down_weight, val_hidden, val_grad, assign):
    n_dp = lax.axis_size("dp")
    n_fs = lax.axis_size("fsdp")
    d = lax.axis_index("dp")
    f = lax.axis_index("fsdp")
    rows_here = assign.shape[0]
    toks, width = out_grad.shape
    units = gate_act.shape[1]
    total = n_dp * toks
    n_out = n_fs // 2
    outer, inner = f // 2, f % 2

    at = (outer - jnp.arange(n_out, dtype=jnp.int32)) % n_out
    tok_offs = (d ^ jnp.arange(n_dp, dtype=jnp.int32)) * toks
    inner_at = inner.reshape(1).astype(jnp.int32)
    outer_at = outer.reshape(1).astype(jnp.int32)

    first = shift(out_grad, "fsdp", 2)
    others = [swap(out_grad, "fsdp", 1)]
    far = swap(out_grad, "dp", 2)
    near = swap(out_grad, "dp", 1)
    first = after(first, others[0], far, near)
    hidden = after(hidden_units(gate_act, up_act), first)
    grad_dp = [out_grad, near, far, swap(far, "dp", 1)]
    far = swap(hidden, "dp", 2)
    near = swap(hidden, "dp", 1)

    grad_kept, away = gram_call(
        grad_gram_body, inner_at, tok_offs, [*grad_dp, val_grad], first, n_fs, [], "grad_gram"
    )
    grad_came = swap(away, "fsdp", 1)
    ring = [out_grad, first]
    for _ in range(n_out - 2):
        others.append(swap(ring[-1], "fsdp", 1))
        ring.append(after(shift(ring[-1], "fsdp", 2), others[-1], away))
    others.append(swap(ring[-1], "fsdp", 1))

    far = after(far, ring[-1])
    hid_dp = [hidden, near, far, swap(far, "dp", 1)]
    own = arrange(at, ring, far, "own_features")
    own_cols = lax.all_to_all(own, "dp", split_axis=0, concat_axis=0, tiled=True)
    grad_pair = pair_sum(outer_at, grad_kept, grad_came, own, "grad_pair")
    grad_sums = spread(grad_pair)

    hid_kept, away, hid_all = gram_call(
        hidden_gram_body, inner_at, tok_offs, [*hid_dp, val_hidden], grad_pair[0], n_fs,
        [jax.ShapeDtypeStruct((units, total), BF16)], "hidden_gram",
    )
    hid_came = swap(away, "fsdp", 1)
    other = arrange(at, others, away, "other_features")
    other_cols = lax.all_to_all(other, "dp", split_axis=0, concat_axis=0, tiled=True)
    hid_pair = pair_sum(outer_at, hid_kept, hid_came, other, "hidden_pair")
    hid_sums = spread(hid_pair)

    offs = (jnp.stack([inner, 1 - inner]) * width).astype(jnp.int32)
    grad_gate, grad_up = grads(offs, own, other, down_weight, gate_act, up_act, hid_pair[0])

    mine = score_line(
        assign, hid_sums, grad_sums, grad_up, n_dp * rows_here, n_dp * n_fs
    )
    every = lax.all_to_all(
        mine, ("dp", "fsdp"), split_axis=0, concat_axis=0, tiled=True
    ).reshape(n_dp, n_fs, 128)
    weight_grad = wgrad(offs, hid_all, own_cols, other_cols, mine)

    rows = n_dp * rows_here
    scale = 1.0 / jnp.sqrt(F32(L) * VAL * FFW * D)
    scores = jnp.sum(every[:, :, :rows], axis=1) * scale
    groups = every[:, 0, rows : rows + rows_here].reshape(rows)
    onehot = (groups[None, :] == jnp.arange(n_dp, dtype=F32)[:, None]).astype(F32)
    group_values = jnp.sum(onehot * scores, axis=1)
    row_scores = lax.dynamic_slice_in_dim(scores, d * rows_here, rows_here, axis=1).T
    return (grad_gate, grad_up, weight_grad, row_scores, group_values)


def per_device_any(gate_act, up_act, out_grad, down_weight, val_hidden, val_grad, assign):
    n_dp = lax.axis_size("dp")
    me = lax.axis_index("dp")
    rows_here = assign.shape[0]
    toks = gate_act.shape[0]
    gate = gate_act.astype(F32)
    up = up_act.astype(F32)
    sig = jax.nn.sigmoid(gate)
    act = gate * sig
    hidden = (act * up).astype(BF16)
    grad_feat = lax.all_gather(out_grad, "dp", axis=0, tiled=True)
    piece = lax.all_gather(out_grad, "fsdp", axis=1, tiled=True)
    hidden_all = lax.all_gather(hidden, "dp", axis=0, tiled=True)
    grad_gram = lax.psum(dot_nt(grad_feat, val_grad), "fsdp")
    grad_cols = lax.all_to_all(piece, "dp", split_axis=1, concat_axis=0, tiled=True)
    grad_hidden = dot_nt(piece, down_weight)
    grad_gate = (grad_hidden * up * sig * (1.0 + gate * (1.0 - sig))).astype(BF16)
    grad_up = (grad_hidden * act).astype(BF16)
    product = dot_nt(hidden_all, val_hidden) * grad_gram
    part = jnp.sum(product.reshape(n_dp * rows_here, toks // rows_here * VAL), axis=1)
    weight_grad = dot_tn(hidden_all, grad_cols).astype(BF16)
    scale = 1.0 / jnp.sqrt(F32(L) * VAL * FFW * D)
    scores = lax.all_gather(lax.psum(part, "fsdp"), "dp") * scale
    groups = lax.all_gather(assign, "dp", tiled=True)
    onehot = (groups[None, :] == jnp.arange(n_dp, dtype=jnp.int32)[:, None]).astype(F32)
    group_values = jnp.sum(onehot * scores, axis=1)
    row_scores = lax.dynamic_slice_in_dim(scores, me * rows_here, rows_here, axis=1).T
    return (grad_gate, grad_up, weight_grad, row_scores, group_values)


def solution(mesh):
    in_specs = (
        P("dp", "fsdp"),
        P("dp", "fsdp"),
        P("dp", "fsdp"),
        P("fsdp", None),
        P("dp", "fsdp"),
        P("dp", "fsdp"),
        P("dp"),
    )
    out_specs = (P("dp", "fsdp"), P("dp", "fsdp"), P("fsdp", "dp"), P("dp", None), P())
    n_dp, n_fs = mesh.shape["dp"], mesh.shape["fsdp"]
    fits = n_dp == 4 and n_fs == 2 * n_dp
    return jax.shard_map(
        per_device if fits else per_device_any,
        mesh=mesh, in_specs=in_specs, out_specs=out_specs, check_vma=False,
    )
```

```python
import functools

import jax
import jax.numpy as jnp
from jax import lax
from jax.experimental import pallas as pl
from jax.experimental.pallas import tpu as pltpu
from jax.sharding import PartitionSpec as P

D = 5120
FFW = 14336
L = 128
VAL = 256

F32 = jnp.float32
BF16 = jnp.bfloat16
VMEM_LIMIT = 32 * 1024 * 1024


def dot_nt(a, b):
    return lax.dot_general(a, b, (((1,), (1,)), ((), ())), preferred_element_type=F32)


def dot_tn(a, b):
    return lax.dot_general(a, b, (((0,), (0,)), ((), ())), preferred_element_type=F32)


def swap(x, axis, k):
    n = lax.axis_size(axis)
    return lax.ppermute(x, axis, [(s, s ^ k) for s in range(n)])


def shift(x, axis, k):
    n = lax.axis_size(axis)
    return lax.ppermute(x, axis, [(s, (s + k) % n) for s in range(n)])


def whole(shape):
    return pl.BlockSpec(shape, lambda *_: (0,) * len(shape))


ANY = pl.BlockSpec(memory_space=pl.ANY)
SMALL = pl.CostEstimate(flops=1024, bytes_accessed=1024, transcendentals=0)


def params():
    return pltpu.CompilerParams(vmem_limit_bytes=VMEM_LIMIT)


def after_body(*refs):
    pass


def after(x, *order):
    return pl.pallas_call(
        after_body,
        in_specs=[ANY] * (1 + len(order)),
        out_specs=ANY,
        out_shape=jax.ShapeDtypeStruct(x.shape, x.dtype),
        input_output_aliases={0: 0},
        cost_estimate=SMALL,
        name="after",
    )(x, *order)


def hidden_body(gate_ref, up_ref, hid_ref, by_gate_ref, by_up_ref):
    gate = gate_ref[...].astype(F32)
    up = up_ref[...].astype(F32)
    sig = jax.nn.sigmoid(gate)
    act = gate * sig
    hid_ref[...] = (act * up).astype(BF16).T
    by_gate_ref[...] = (up * sig * (1.0 + gate * (1.0 - sig))).astype(BF16)
    by_up_ref[...] = act.astype(BF16)


def hidden_units(gate, up):
    toks, units = gate.shape
    tile = 256
    cols = pl.BlockSpec((toks, tile), lambda i: (0, i))
    return pl.pallas_call(
        hidden_body,
        grid=(units // tile,),
        in_specs=[cols, cols],
        out_specs=[pl.BlockSpec((tile, toks), lambda i: (i, 0)), cols, cols],
        out_shape=[
            jax.ShapeDtypeStruct((units, toks), BF16),
            jax.ShapeDtypeStruct((toks, units), BF16),
            jax.ShapeDtypeStruct((toks, units), BF16),
        ],
        compiler_params=params(),
        cost_estimate=SMALL,
        name="hidden",
    )(gate, up)


def arrange_body(n, at_ref, *refs):
    blocks, (order_ref, out_ref, sems) = refs[:n], refs[n:]
    copies = [
        pltpu.make_async_copy(blocks[j], out_ref.at[at_ref[j]], sems.at[j]) for j in range(n)
    ]
    for copy in copies:
        copy.start()
    for copy in copies:
        copy.wait()


def arrange(at, blocks, order, name):
    n = len(blocks)
    return pl.pallas_call(
        functools.partial(arrange_body, n),
        in_specs=[pl.BlockSpec(memory_space=pltpu.SMEM)] + [ANY] * (n + 1),
        out_specs=pl.BlockSpec(memory_space=pltpu.VMEM),
        out_shape=jax.ShapeDtypeStruct((n,) + blocks[0].shape, BF16),
        scratch_shapes=[pltpu.SemaphoreType.DMA((n,))],
        compiler_params=params(),
        cost_estimate=SMALL,
        name=name,
    )(at, *blocks, order)


def grads_body(
    offs_ref, own_ref, other_ref, w_ref, by_gate_ref, by_up_ref, order_ref, gg_ref, gu_ref, piece
):
    n, toks, width = own_ref.shape

    @pl.when(pl.program_id(0) == 0)
    def _():
        for half, ref in enumerate((own_ref, other_ref)):
            for j in range(n):
                place = pl.multiple_of(offs_ref[half] + 2 * j * width, 128)
                piece[:, pl.ds(place, width)] = ref[j]

    total = dot_nt(piece[...], w_ref[...])
    gg_ref[...] = (total * by_gate_ref[...]).astype(BF16)
    gu_ref[...] = (total * by_up_ref[...]).astype(BF16)


def grads(offs, own, other, weight, by_gate, by_up, order):
    n, toks, width = own.shape
    units, feats = weight.shape
    tile = 256
    cols = pl.BlockSpec((toks, tile), lambda i, _: (0, i))
    out = jax.ShapeDtypeStruct((toks, units), BF16)
    return pl.pallas_call(
        grads_body,
        grid_spec=pltpu.PrefetchScalarGridSpec(
            num_scalar_prefetch=1,
            grid=(units // tile,),
            in_specs=[whole(own.shape)] * 2
            + [pl.BlockSpec((tile, feats), lambda i, _: (i, 0)), cols, cols, ANY],
            out_specs=[cols, cols],
            scratch_shapes=[pltpu.VMEM((toks, feats), BF16)],
        ),
        out_shape=(out, out),
        compiler_params=params(),
        cost_estimate=SMALL,
        name="grads",
    )(offs, own, other, weight, by_gate, by_up, order)


def wgrad_body(offs_ref, hid_ref, own_ref, other_ref, order_ref, out_ref, cols):
    n, toks, width = own_ref.shape

    @pl.when(pl.program_id(0) == 0)
    def _():
        for half, ref in enumerate((own_ref, other_ref)):
            place = pl.ds(pl.multiple_of(offs_ref[half], 128), width)
            for k in range(n):
                cols[k * toks : (k + 1) * toks, place] = ref[k]

    out_ref[...] = lax.dot_general(
        hid_ref[...], cols[...], (((1,), (0,)), ((), ())), preferred_element_type=F32
    ).astype(BF16)


def wgrad(offs, hid, own, other, order):
    units, total = hid.shape
    width = own.shape[2]
    tile = units // 4
    return pl.pallas_call(
        wgrad_body,
        grid_spec=pltpu.PrefetchScalarGridSpec(
            num_scalar_prefetch=1,
            grid=(units // tile,),
            in_specs=[pl.BlockSpec((tile, total), lambda i, _: (i, 0))]
            + [whole(own.shape)] * 2
            + [ANY],
            out_specs=pl.BlockSpec((tile, 2 * width), lambda i, _: (i, 0)),
            scratch_shapes=[pltpu.VMEM((total, 2 * width), BF16)],
        ),
        out_shape=jax.ShapeDtypeStruct((units, 2 * width), BF16),
        compiler_params=params(),
        cost_estimate=pl.CostEstimate(
            flops=4 * total * units * width,
            bytes_accessed=2 * (total * (units + 2 * width) + 2 * units * width),
            transcendentals=0,
        ),
        name="wgrad",
    )(offs, hid, own, other, order)


def put_slices(inner_ref, part, kept_ref, away_ref):
    outer, size, _ = kept_ref.shape
    for inner in range(2):

        @pl.when(inner_ref[0] == inner)
        def _():
            for p in range(2 * outer):
                out_ref = kept_ref if p % 2 == inner else away_ref
                out_ref[p // 2] = part[p * size : (p + 1) * size]


def grad_gram_body(inner_ref, offs_ref, *refs):
    toks_refs, (val_ref, order_ref, kept_ref, away_ref, wide) = refs[:-5], refs[-5:]
    for k, ref in enumerate(toks_refs):
        toks = ref.shape[0]
        wide[:, pl.ds(pl.multiple_of(offs_ref[k], 128), toks)] = dot_nt(val_ref[...], ref[...])
    put_slices(inner_ref, wide, kept_ref, away_ref)


def hidden_gram_body(inner_ref, offs_ref, *refs):
    hid, (val_ref, order_ref, kept_ref, away_ref, all_ref, wide) = refs[:-6], refs[-6:]
    for k, ref in enumerate(hid):
        toks = ref.shape[1]
        all_ref[:, pl.ds(pl.multiple_of(offs_ref[k], 128), toks)] = ref[...]
    wide[...] = lax.dot_general(
        val_ref[...], all_ref[...], (((1,), (0,)), ((), ())), preferred_element_type=F32
    )
    put_slices(inner_ref, wide, kept_ref, away_ref)


def gram_call(body, inner, offs, operands, order, parts, extra, name):
    smem = pl.BlockSpec(memory_space=pltpu.SMEM)
    vmem = pl.BlockSpec(memory_space=pltpu.VMEM)
    *toks, vals = operands
    total = sum(x.size for x in toks) // vals.shape[1]
    half = jax.ShapeDtypeStruct((parts // 2, vals.shape[0] // parts, total), F32)
    shapes = [half, half, *extra]
    return pl.pallas_call(
        body,
        in_specs=[smem, smem] + [vmem] * len(operands) + [ANY],
        out_specs=[vmem] * len(shapes),
        out_shape=shapes,
        scratch_shapes=[pltpu.VMEM((vals.shape[0], total), F32)],
        compiler_params=params(),
        cost_estimate=SMALL,
        name=name,
    )(inner, offs, *operands, order)


def pair_body(n, outer_ref, kept_ref, came_ref, order_ref, *out_refs):
    for step in range(n):
        at = lax.rem(outer_ref[0] + step, n)
        out_refs[step][...] = kept_ref[at] + came_ref[at]


def pair_sum(outer, kept, came, order, name):
    n, *size = kept.shape
    vmem = pl.BlockSpec(memory_space=pltpu.VMEM)
    return pl.pallas_call(
        functools.partial(pair_body, n),
        in_specs=[pl.BlockSpec(memory_space=pltpu.SMEM), vmem, vmem, ANY],
        out_specs=[vmem] * n,
        out_shape=[jax.ShapeDtypeStruct(size, F32)] * n,
        compiler_params=params(),
        cost_estimate=SMALL,
        name=name,
    )(outer, kept, came, order)


def spread(slices):
    return [x if j == 0 else shift(x, "fsdp", 2 * j) for j, x in enumerate(slices)]


def line_body(rows, n, assign_ref, *refs):
    hid, grad, out_ref = refs[:n], refs[n : 2 * n], refs[-1]
    hid_sum = sum(ref[...] for ref in hid)
    grad_sum = sum(ref[...] for ref in grad)
    by_tok = jnp.sum(hid_sum * grad_sum, axis=0, keepdims=True)
    size = by_tok.shape[1] // rows
    lane = lax.broadcasted_iota(jnp.int32, (1, 128), 1)
    line = jnp.zeros((1, 128), F32)
    for r in range(rows):
        row = jnp.sum(by_tok[:, r * size : (r + 1) * size], axis=1, keepdims=True)
        line = jnp.where(lane == r, row, line)
    for r in range(assign_ref.shape[0]):
        line = jnp.where(lane == rows + r, assign_ref[r].astype(F32), line)
    out_ref[...] = jnp.broadcast_to(line, out_ref.shape)


def score_line(assign, hid, grad, order, rows, copies):
    n = len(hid)
    vmem = pl.BlockSpec(memory_space=pltpu.VMEM)
    return pl.pallas_call(
        functools.partial(line_body, rows, n),
        in_specs=[pl.BlockSpec(memory_space=pltpu.SMEM)] + [vmem] * (2 * n) + [ANY] * len(order),
        out_specs=vmem,
        out_shape=jax.ShapeDtypeStruct((copies, 128), F32),
        compiler_params=params(),
        cost_estimate=SMALL,
        name="score_line",
    )(assign, *hid, *grad, *order)


def per_device(gate_act, up_act, out_grad, down_weight, val_hidden, val_grad, assign):
    n_dp = lax.axis_size("dp")
    n_fs = lax.axis_size("fsdp")
    d = lax.axis_index("dp")
    f = lax.axis_index("fsdp")
    rows_here = assign.shape[0]
    toks, width = out_grad.shape
    units = gate_act.shape[1]
    total = n_dp * toks
    n_out = n_fs // 2
    outer, inner = f // 2, f % 2

    at = (outer - jnp.arange(n_out, dtype=jnp.int32)) % n_out
    tok_offs = (d ^ jnp.arange(n_dp, dtype=jnp.int32)) * toks
    inner_at = inner.reshape(1).astype(jnp.int32)
    outer_at = outer.reshape(1).astype(jnp.int32)

    first = shift(out_grad, "fsdp", 2)
    others = [swap(out_grad, "fsdp", 1)]
    far = swap(out_grad, "dp", 2)
    near = swap(out_grad, "dp", 1)
    first = after(first, others[0], far, near)
    hidden, by_gate, by_up = hidden_units(gate_act, up_act)
    hidden = after(hidden, first)
    grad_dp = [out_grad, near, far, swap(far, "dp", 1)]
    far = swap(hidden, "dp", 2)
    near = swap(hidden, "dp", 1)

    grad_kept, away = gram_call(
        grad_gram_body, inner_at, tok_offs, [*grad_dp, val_grad], first, n_fs, [], "grad_gram"
    )
    grad_came = swap(away, "fsdp", 1)
    ring = [out_grad, first]
    for _ in range(n_out - 2):
        others.append(swap(ring[-1], "fsdp", 1))
        ring.append(after(shift(ring[-1], "fsdp", 2), others[-1], away))
    others.append(shift(others[-1], "fsdp", 2))

    far = after(far, ring[-1])
    hid_dp = [hidden, near, far, swap(far, "dp", 1)]
    own = arrange(at, ring, far, "own_features")
    own_cols = lax.all_to_all(own, "dp", split_axis=0, concat_axis=0, tiled=True)
    hid_kept, away, hid_all = gram_call(
        hidden_gram_body, inner_at, tok_offs, [*hid_dp, val_hidden], own, n_fs,
        [jax.ShapeDtypeStruct((units, total), BF16)], "hidden_gram",
    )
    hid_came = swap(away, "fsdp", 1)
    other = arrange(at, others, away, "other_features")
    other_cols = lax.all_to_all(other, "dp", split_axis=0, concat_axis=0, tiled=True)
    grad_pair = pair_sum(outer_at, grad_kept, grad_came, other, "grad_pair")
    grad_sums = spread(grad_pair)
    hid_pair = pair_sum(outer_at, hid_kept, hid_came, grad_pair[0], "hidden_pair")
    hid_sums = spread(hid_pair)

    offs = (jnp.stack([inner, 1 - inner]) * width).astype(jnp.int32)
    grad_gate, grad_up = grads(offs, own, other, down_weight, by_gate, by_up, hid_pair[0])

    mine = score_line(
        assign, hid_sums, grad_sums, [grad_up, other_cols], n_dp * rows_here, n_dp * n_fs
    )
    every = lax.all_to_all(
        mine, ("dp", "fsdp"), split_axis=0, concat_axis=0, tiled=True
    ).reshape(n_dp, n_fs, 128)
    weight_grad = wgrad(offs, hid_all, own_cols, other_cols, mine)

    rows = n_dp * rows_here
    scale = 1.0 / jnp.sqrt(F32(L) * VAL * FFW * D)
    scores = jnp.sum(every[:, :, :rows], axis=1) * scale
    groups = every[:, 0, rows : rows + rows_here].reshape(rows)
    onehot = (groups[None, :] == jnp.arange(n_dp, dtype=F32)[:, None]).astype(F32)
    group_values = jnp.sum(onehot * scores, axis=1)
    row_scores = lax.dynamic_slice_in_dim(scores, d * rows_here, rows_here, axis=1).T
    return (grad_gate, grad_up, weight_grad, row_scores, group_values)


def per_device_any(gate_act, up_act, out_grad, down_weight, val_hidden, val_grad, assign):
    n_dp = lax.axis_size("dp")
    me = lax.axis_index("dp")
    rows_here = assign.shape[0]
    toks = gate_act.shape[0]
    gate = gate_act.astype(F32)
    up = up_act.astype(F32)
    sig = jax.nn.sigmoid(gate)
    act = gate * sig
    hidden = (act * up).astype(BF16)
    grad_feat = lax.all_gather(out_grad, "dp", axis=0, tiled=True)
    piece = lax.all_gather(out_grad, "fsdp", axis=1, tiled=True)
    hidden_all = lax.all_gather(hidden, "dp", axis=0, tiled=True)
    grad_gram = lax.psum(dot_nt(grad_feat, val_grad), "fsdp")
    grad_cols = lax.all_to_all(piece, "dp", split_axis=1, concat_axis=0, tiled=True)
    grad_hidden = dot_nt(piece, down_weight)
    grad_gate = (grad_hidden * up * sig * (1.0 + gate * (1.0 - sig))).astype(BF16)
    grad_up = (grad_hidden * act).astype(BF16)
    product = dot_nt(hidden_all, val_hidden) * grad_gram
    part = jnp.sum(product.reshape(n_dp * rows_here, toks // rows_here * VAL), axis=1)
    weight_grad = dot_tn(hidden_all, grad_cols).astype(BF16)
    scale = 1.0 / jnp.sqrt(F32(L) * VAL * FFW * D)
    scores = lax.all_gather(lax.psum(part, "fsdp"), "dp") * scale
    groups = lax.all_gather(assign, "dp", tiled=True)
    onehot = (groups[None, :] == jnp.arange(n_dp, dtype=jnp.int32)[:, None]).astype(F32)
    group_values = jnp.sum(onehot * scores, axis=1)
    row_scores = lax.dynamic_slice_in_dim(scores, me * rows_here, rows_here, axis=1).T
    return (grad_gate, grad_up, weight_grad, row_scores, group_values)


def solution(mesh):
    in_specs = (
        P("dp", "fsdp"),
        P("dp", "fsdp"),
        P("dp", "fsdp"),
        P("fsdp", None),
        P("dp", "fsdp"),
        P("dp", "fsdp"),
        P("dp"),
    )
    out_specs = (P("dp", "fsdp"), P("dp", "fsdp"), P("fsdp", "dp"), P("dp", None), P())
    n_dp, n_fs = mesh.shape["dp"], mesh.shape["fsdp"]
    fits = n_dp == 4 and n_fs == 2 * n_dp
    return jax.shard_map(
        per_device if fits else per_device_any,
        mesh=mesh, in_specs=in_specs, out_specs=out_specs, check_vma=False,
    )
```

```python
import functools

import jax
import jax.numpy as jnp
from jax import lax
from jax.experimental import pallas as pl
from jax.experimental.pallas import tpu as pltpu
from jax.sharding import PartitionSpec as P

D = 5120
FFW = 14336
L = 128
VAL = 256

F32 = jnp.float32
BF16 = jnp.bfloat16
VMEM_LIMIT = 32 * 1024 * 1024


def dot_nt(a, b):
    return lax.dot_general(a, b, (((1,), (1,)), ((), ())), preferred_element_type=F32)


def dot_tn(a, b):
    return lax.dot_general(a, b, (((0,), (0,)), ((), ())), preferred_element_type=F32)


def swap(x, axis, k):
    n = lax.axis_size(axis)
    return lax.ppermute(x, axis, [(s, s ^ k) for s in range(n)])


def shift(x, axis, k):
    n = lax.axis_size(axis)
    return lax.ppermute(x, axis, [(s, (s + k) % n) for s in range(n)])


def whole(shape):
    return pl.BlockSpec(shape, lambda *_: (0,) * len(shape))


ANY = pl.BlockSpec(memory_space=pl.ANY)
SMALL = pl.CostEstimate(flops=1024, bytes_accessed=1024, transcendentals=0)


def params():
    return pltpu.CompilerParams(vmem_limit_bytes=VMEM_LIMIT)


def after_body(*refs):
    pass


def after(x, *order):
    return pl.pallas_call(
        after_body,
        in_specs=[ANY] * (1 + len(order)),
        out_specs=ANY,
        out_shape=jax.ShapeDtypeStruct(x.shape, x.dtype),
        input_output_aliases={0: 0},
        cost_estimate=SMALL,
        name="after",
    )(x, *order)


def hidden_body(gate_ref, up_ref, hid_ref, by_gate_ref, by_up_ref):
    gate = gate_ref[...].astype(F32)
    up = up_ref[...].astype(F32)
    sig = jax.nn.sigmoid(gate)
    act = gate * sig
    hid_ref[...] = (act * up).astype(BF16).T
    by_gate_ref[...] = (up * sig * (1.0 + gate * (1.0 - sig))).astype(BF16)
    by_up_ref[...] = act.astype(BF16)


def hidden_units(gate, up):
    toks, units = gate.shape
    tile = 256
    cols = pl.BlockSpec((toks, tile), lambda i: (0, i))
    return pl.pallas_call(
        hidden_body,
        grid=(units // tile,),
        in_specs=[cols, cols],
        out_specs=[pl.BlockSpec((tile, toks), lambda i: (i, 0)), cols, cols],
        out_shape=[
            jax.ShapeDtypeStruct((units, toks), BF16),
            jax.ShapeDtypeStruct((toks, units), BF16),
            jax.ShapeDtypeStruct((toks, units), BF16),
        ],
        compiler_params=params(),
        cost_estimate=SMALL,
        name="hidden",
    )(gate, up)


def arrange_body(n, to_ref, *refs):
    blocks, outs, sems = refs[:n], refs[-n - 1 : -1], refs[-1]
    for j in range(n):
        for k in range(n):

            @pl.when(to_ref[j] == k)
            def _():
                pltpu.make_async_copy(blocks[j], outs[k], sems.at[j]).start()

    for j in range(n):
        pltpu.make_async_copy(blocks[j], outs[0], sems.at[j]).wait()


def arrange(to, blocks, order, name):
    n = len(blocks)
    return pl.pallas_call(
        functools.partial(arrange_body, n),
        in_specs=[pl.BlockSpec(memory_space=pltpu.SMEM)] + [ANY] * (n + len(order)),
        out_specs=[pl.BlockSpec(memory_space=pltpu.VMEM)] * n,
        out_shape=[jax.ShapeDtypeStruct(blocks[0].shape, BF16)] * n,
        scratch_shapes=[pltpu.SemaphoreType.DMA((n,))],
        compiler_params=params(),
        cost_estimate=SMALL,
        name=name,
    )(to, *blocks, *order)


def grads_body(n, offs_ref, *refs):
    blocks, (w_ref, by_gate_ref, by_up_ref, order_ref, gg_ref, gu_ref, piece) = refs[:n], refs[n:]
    width = blocks[0].shape[1]

    @pl.when(pl.program_id(0) == 0)
    def _():
        for j in range(n):
            piece[:, pl.ds(pl.multiple_of(offs_ref[j], 128), width)] = blocks[j][...]

    total = dot_nt(piece[...], w_ref[...])
    gg_ref[...] = (total * by_gate_ref[...]).astype(BF16)
    gu_ref[...] = (total * by_up_ref[...]).astype(BF16)


def grads(offs, blocks, weight, by_gate, by_up, order):
    n = len(blocks)
    toks, width = blocks[0].shape
    units, feats = weight.shape
    tile = 256
    cols = pl.BlockSpec((toks, tile), lambda i, _: (0, i))
    out = jax.ShapeDtypeStruct((toks, units), BF16)
    return pl.pallas_call(
        functools.partial(grads_body, n),
        grid_spec=pltpu.PrefetchScalarGridSpec(
            num_scalar_prefetch=1,
            grid=(units // tile,),
            in_specs=[whole((toks, width))] * n
            + [pl.BlockSpec((tile, feats), lambda i, _: (i, 0)), cols, cols, ANY],
            out_specs=[cols, cols],
            scratch_shapes=[pltpu.VMEM((toks, feats), BF16)],
        ),
        out_shape=(out, out),
        compiler_params=params(),
        cost_estimate=SMALL,
        name="grads",
    )(offs, *blocks, weight, by_gate, by_up, order)


def wgrad_body(n, offs_ref, toks_ref, hid_ref, *refs):
    blocks, (order_ref, out_ref, cols) = refs[: 2 * n], refs[2 * n :]
    toks, width = blocks[0].shape

    @pl.when(pl.program_id(0) == 0)
    def _():
        for half in range(2):
            place = pl.ds(pl.multiple_of(offs_ref[half], 128), width)
            for k in range(n):
                rows = pl.ds(pl.multiple_of(toks_ref[k], 128), toks)
                cols[rows, place] = blocks[half * n + k][...]

    out_ref[...] = lax.dot_general(
        hid_ref[...], cols[...], (((1,), (0,)), ((), ())), preferred_element_type=F32
    ).astype(BF16)


def wgrad(offs, tok_offs, hid, blocks, order):
    units, total = hid.shape
    toks, width = blocks[0].shape
    n = total // toks
    tile = units // 4
    return pl.pallas_call(
        functools.partial(wgrad_body, n),
        grid_spec=pltpu.PrefetchScalarGridSpec(
            num_scalar_prefetch=2,
            grid=(units // tile,),
            in_specs=[pl.BlockSpec((tile, total), lambda i, *_: (i, 0))]
            + [whole((toks, width))] * (2 * n)
            + [ANY],
            out_specs=pl.BlockSpec((tile, 2 * width), lambda i, *_: (i, 0)),
            scratch_shapes=[pltpu.VMEM((total, 2 * width), BF16)],
        ),
        out_shape=jax.ShapeDtypeStruct((units, 2 * width), BF16),
        compiler_params=params(),
        cost_estimate=pl.CostEstimate(
            flops=4 * total * units * width,
            bytes_accessed=2 * (total * (units + 2 * width) + 2 * units * width),
            transcendentals=0,
        ),
        name="wgrad",
    )(offs, tok_offs, hid, *blocks, order)


def put_slices(inner_ref, part, kept_ref, away_ref):
    outer, size, _ = kept_ref.shape
    for inner in range(2):

        @pl.when(inner_ref[0] == inner)
        def _():
            for p in range(2 * outer):
                out_ref = kept_ref if p % 2 == inner else away_ref
                out_ref[p // 2] = part[p * size : (p + 1) * size]


def grad_gram_body(inner_ref, offs_ref, *refs):
    toks_refs, (val_ref, order_ref, kept_ref, away_ref, wide) = refs[:-5], refs[-5:]
    for k, ref in enumerate(toks_refs):
        toks = ref.shape[0]
        wide[:, pl.ds(pl.multiple_of(offs_ref[k], 128), toks)] = dot_nt(val_ref[...], ref[...])
    put_slices(inner_ref, wide, kept_ref, away_ref)


def hidden_gram_body(inner_ref, offs_ref, *refs):
    hid, (val_ref, order_ref, kept_ref, away_ref, all_ref, wide) = refs[:-6], refs[-6:]
    for k, ref in enumerate(hid):
        toks = ref.shape[1]
        all_ref[:, pl.ds(pl.multiple_of(offs_ref[k], 128), toks)] = ref[...]
    wide[...] = lax.dot_general(
        val_ref[...], all_ref[...], (((1,), (0,)), ((), ())), preferred_element_type=F32
    )
    put_slices(inner_ref, wide, kept_ref, away_ref)


def gram_call(body, inner, offs, operands, order, parts, extra, name):
    smem = pl.BlockSpec(memory_space=pltpu.SMEM)
    vmem = pl.BlockSpec(memory_space=pltpu.VMEM)
    *toks, vals = operands
    total = sum(x.size for x in toks) // vals.shape[1]
    half = jax.ShapeDtypeStruct((parts // 2, vals.shape[0] // parts, total), F32)
    shapes = [half, half, *extra]
    return pl.pallas_call(
        body,
        in_specs=[smem, smem] + [vmem] * len(operands) + [ANY],
        out_specs=[vmem] * len(shapes),
        out_shape=shapes,
        scratch_shapes=[pltpu.VMEM((vals.shape[0], total), F32)],
        compiler_params=params(),
        cost_estimate=SMALL,
        name=name,
    )(inner, offs, *operands, order)


def pair_body(kept_ref, came_ref, *refs):
    refs[-1][...] = kept_ref[...] + came_ref[...]


def pair_sum(kept, came, order, name):
    vmem = pl.BlockSpec(memory_space=pltpu.VMEM)
    return pl.pallas_call(
        pair_body,
        in_specs=[vmem, vmem] + [ANY] * len(order),
        out_specs=vmem,
        out_shape=jax.ShapeDtypeStruct(kept.shape, F32),
        compiler_params=params(),
        cost_estimate=SMALL,
        name=name,
    )(kept, came, *order)


def spread(pair):
    n_fs = lax.axis_size("fsdp")
    groups = [list(range(x, n_fs, 2)) for x in range(2)]
    return lax.all_to_all(
        pair, "fsdp", split_axis=0, concat_axis=0, axis_index_groups=groups, tiled=True
    )


def line_body(rows, assign_ref, hid_ref, grad_ref, *refs):
    out_ref = refs[-1]
    n = hid_ref.shape[0]
    hid_sum = sum(hid_ref[j] for j in range(n))
    grad_sum = sum(grad_ref[j] for j in range(n))
    by_tok = jnp.sum(hid_sum * grad_sum, axis=0, keepdims=True)
    size = by_tok.shape[1] // rows
    lane = lax.broadcasted_iota(jnp.int32, (1, 128), 1)
    line = jnp.zeros((1, 128), F32)
    for r in range(rows):
        row = jnp.sum(by_tok[:, r * size : (r + 1) * size], axis=1, keepdims=True)
        line = jnp.where(lane == r, row, line)
    for r in range(assign_ref.shape[0]):
        line = jnp.where(lane == rows + r, assign_ref[r].astype(F32), line)
    out_ref[...] = jnp.broadcast_to(line, out_ref.shape)


def score_line(assign, hid, grad, order, rows, copies):
    vmem = pl.BlockSpec(memory_space=pltpu.VMEM)
    return pl.pallas_call(
        functools.partial(line_body, rows),
        in_specs=[pl.BlockSpec(memory_space=pltpu.SMEM), vmem, vmem] + [ANY] * len(order),
        out_specs=vmem,
        out_shape=jax.ShapeDtypeStruct((copies, 128), F32),
        compiler_params=params(),
        cost_estimate=SMALL,
        name="score_line",
    )(assign, hid, grad, *order)


def per_device(gate_act, up_act, out_grad, down_weight, val_hidden, val_grad, assign):
    n_dp = lax.axis_size("dp")
    n_fs = lax.axis_size("fsdp")
    d = lax.axis_index("dp")
    f = lax.axis_index("fsdp")
    rows_here = assign.shape[0]
    toks, width = out_grad.shape
    units = gate_act.shape[1]
    total = n_dp * toks
    n_out = n_fs // 2
    outer, inner = f // 2, f % 2

    at = (outer - jnp.arange(n_out, dtype=jnp.int32)) % n_out
    tok_offs = (d ^ jnp.arange(n_dp, dtype=jnp.int32)) * toks
    inner_at = inner.reshape(1).astype(jnp.int32)
    to = at ^ d

    first = shift(out_grad, "fsdp", 2)
    others = [swap(out_grad, "fsdp", 1)]
    far = swap(out_grad, "dp", 2)
    near = swap(out_grad, "dp", 1)
    first = after(first, others[0], far, near)
    hidden, by_gate, by_up = hidden_units(gate_act, up_act)
    hidden = after(hidden, first)
    grad_dp = [out_grad, near, far, swap(far, "dp", 1)]
    far = swap(hidden, "dp", 2)
    near = swap(hidden, "dp", 1)

    grad_kept, away = gram_call(
        grad_gram_body, inner_at, tok_offs, [*grad_dp, val_grad], first, n_fs, [], "grad_gram"
    )
    grad_came = swap(away, "fsdp", 1)
    ring = [out_grad, first]
    for _ in range(n_out - 2):
        others.append(swap(ring[-1], "fsdp", 1))
        ring.append(after(shift(ring[-1], "fsdp", 2), others[-1], away))
    others.append(shift(others[-1], "fsdp", 2))

    def over_columns(blocks):
        return [x if k == 0 else swap(x, "dp", k) for k, x in enumerate(blocks)]

    far = after(far, ring[-1])
    hid_dp = [hidden, near, far, swap(far, "dp", 1)]
    own = arrange(to, ring, [far], "own_features")
    own_cols = over_columns(own)
    hid_kept, away, hid_all = gram_call(
        hidden_gram_body, inner_at, tok_offs, [*hid_dp, val_hidden], own[0], n_fs,
        [jax.ShapeDtypeStruct((units, total), BF16)], "hidden_gram",
    )
    hid_came = swap(away, "fsdp", 1)
    other = arrange(to, others, [away, grad_came], "other_features")
    other_cols = over_columns(other)
    grad_pair = pair_sum(grad_kept, grad_came, [other[0]], "grad_pair")
    grad_sums = spread(grad_pair)
    hid_pair = pair_sum(hid_kept, hid_came, [grad_pair, *own_cols], "hidden_pair")
    hid_sums = spread(hid_pair)

    offs = (jnp.stack([inner, 1 - inner]) * width).astype(jnp.int32)
    places = (offs[:, None] + at[None, :] * (2 * width)).reshape(-1)
    grad_gate, grad_up = grads(places, [*ring, *others], down_weight, by_gate, by_up, hid_pair)

    mine = score_line(
        assign, hid_sums, grad_sums, [grad_up, *other_cols], n_dp * rows_here, n_dp * n_fs
    )
    every = lax.all_to_all(
        mine, ("dp", "fsdp"), split_axis=0, concat_axis=0, tiled=True
    ).reshape(n_dp, n_fs, 128)
    weight_grad = wgrad(offs, tok_offs, hid_all, [*own_cols, *other_cols], mine)

    rows = n_dp * rows_here
    scale = 1.0 / jnp.sqrt(F32(L) * VAL * FFW * D)
    scores = jnp.sum(every[:, :, :rows], axis=1) * scale
    groups = every[:, 0, rows : rows + rows_here].reshape(rows)
    onehot = (groups[None, :] == jnp.arange(n_dp, dtype=F32)[:, None]).astype(F32)
    group_values = jnp.sum(onehot * scores, axis=1)
    row_scores = lax.dynamic_slice_in_dim(scores, d * rows_here, rows_here, axis=1).T
    return (grad_gate, grad_up, weight_grad, row_scores, group_values)


def per_device_any(gate_act, up_act, out_grad, down_weight, val_hidden, val_grad, assign):
    n_dp = lax.axis_size("dp")
    me = lax.axis_index("dp")
    rows_here = assign.shape[0]
    toks = gate_act.shape[0]
    gate = gate_act.astype(F32)
    up = up_act.astype(F32)
    sig = jax.nn.sigmoid(gate)
    act = gate * sig
    hidden = (act * up).astype(BF16)
    grad_feat = lax.all_gather(out_grad, "dp", axis=0, tiled=True)
    piece = lax.all_gather(out_grad, "fsdp", axis=1, tiled=True)
    hidden_all = lax.all_gather(hidden, "dp", axis=0, tiled=True)
    grad_gram = lax.psum(dot_nt(grad_feat, val_grad), "fsdp")
    grad_cols = lax.all_to_all(piece, "dp", split_axis=1, concat_axis=0, tiled=True)
    grad_hidden = dot_nt(piece, down_weight)
    grad_gate = (grad_hidden * up * sig * (1.0 + gate * (1.0 - sig))).astype(BF16)
    grad_up = (grad_hidden * act).astype(BF16)
    product = dot_nt(hidden_all, val_hidden) * grad_gram
    part = jnp.sum(product.reshape(n_dp * rows_here, toks // rows_here * VAL), axis=1)
    weight_grad = dot_tn(hidden_all, grad_cols).astype(BF16)
    scale = 1.0 / jnp.sqrt(F32(L) * VAL * FFW * D)
    scores = lax.all_gather(lax.psum(part, "fsdp"), "dp") * scale
    groups = lax.all_gather(assign, "dp", tiled=True)
    onehot = (groups[None, :] == jnp.arange(n_dp, dtype=jnp.int32)[:, None]).astype(F32)
    group_values = jnp.sum(onehot * scores, axis=1)
    row_scores = lax.dynamic_slice_in_dim(scores, me * rows_here, rows_here, axis=1).T
    return (grad_gate, grad_up, weight_grad, row_scores, group_values)


def solution(mesh):
    in_specs = (
        P("dp", "fsdp"),
        P("dp", "fsdp"),
        P("dp", "fsdp"),
        P("fsdp", None),
        P("dp", "fsdp"),
        P("dp", "fsdp"),
        P("dp"),
    )
    out_specs = (P("dp", "fsdp"), P("dp", "fsdp"), P("fsdp", "dp"), P("dp", None), P())
    n_dp, n_fs = mesh.shape["dp"], mesh.shape["fsdp"]
    fits = n_dp == 4 and n_fs == 2 * n_dp
    return jax.shard_map(
        per_device if fits else per_device_any,
        mesh=mesh, in_specs=in_specs, out_specs=out_specs, check_vma=False,
    )
```

```python
import functools

import jax
import jax.numpy as jnp
from jax import lax
from jax.experimental import pallas as pl
from jax.experimental.pallas import tpu as pltpu
from jax.sharding import PartitionSpec as P

D = 5120
FFW = 14336
L = 128
VAL = 256

F32 = jnp.float32
BF16 = jnp.bfloat16
MIB = 1024 * 1024


def dot_nt(a, b):
    return lax.dot_general(a, b, (((1,), (1,)), ((), ())), preferred_element_type=F32)


def dot_tn(a, b):
    return lax.dot_general(a, b, (((0,), (0,)), ((), ())), preferred_element_type=F32)


def swap(x, axis, k):
    n = lax.axis_size(axis)
    return lax.ppermute(x, axis, [(s, s ^ k) for s in range(n)])


def shift(x, axis, k):
    n = lax.axis_size(axis)
    return lax.ppermute(x, axis, [(s, (s + k) % n) for s in range(n)])


def whole(shape):
    return pl.BlockSpec(shape, lambda *_: (0,) * len(shape))


ANY = pl.BlockSpec(memory_space=pl.ANY)
HBM = pl.BlockSpec(memory_space=pltpu.HBM)
SMALL = pl.CostEstimate(flops=1024, bytes_accessed=1024, transcendentals=0)


def params(mib):
    return pltpu.CompilerParams(vmem_limit_bytes=mib * MIB)


def after_body(*refs):
    pass


def after(x, *order):
    return pl.pallas_call(
        after_body,
        in_specs=[ANY] * (1 + len(order)),
        out_specs=ANY,
        out_shape=jax.ShapeDtypeStruct(x.shape, x.dtype),
        input_output_aliases={0: 0},
        compiler_params=params(1),
        cost_estimate=SMALL,
        name="after",
    )(x, *order)


def hidden_body(gate_ref, up_ref, hid_ref, by_gate_ref, by_up_ref):
    gate = gate_ref[...].astype(F32)
    up = up_ref[...].astype(F32)
    sig = jax.nn.sigmoid(gate)
    act = gate * sig
    hid_ref[...] = (act * up).astype(BF16).T
    by_gate_ref[...] = (up * sig * (1.0 + gate * (1.0 - sig))).astype(BF16)
    by_up_ref[...] = act.astype(BF16)


def hidden_units(gate, up):
    toks, units = gate.shape
    tile = 256
    cols = pl.BlockSpec((toks, tile), lambda i: (0, i))
    return pl.pallas_call(
        hidden_body,
        grid=(units // tile,),
        in_specs=[cols, cols],
        out_specs=[pl.BlockSpec((tile, toks), lambda i: (i, 0)), cols, cols],
        out_shape=[
            jax.ShapeDtypeStruct((units, toks), BF16),
            jax.ShapeDtypeStruct((toks, units), BF16),
            jax.ShapeDtypeStruct((toks, units), BF16),
        ],
        compiler_params=params(12),
        cost_estimate=SMALL,
        name="hidden",
    )(gate, up)


def stack_body(n, at_ref, *refs):
    blocks, out_ref, sems = refs[:n], refs[-2], refs[-1]
    copies = [
        pltpu.make_async_copy(blocks[j], out_ref.at[at_ref[j]], sems.at[j]) for j in range(n)
    ]
    for copy in copies:
        copy.start()
    for copy in copies:
        copy.wait()


def stack(at, blocks, order, name):
    n = len(blocks)
    return pl.pallas_call(
        functools.partial(stack_body, n),
        in_specs=[pl.BlockSpec(memory_space=pltpu.SMEM)] + [ANY] * (n + len(order)),
        out_specs=pl.BlockSpec(memory_space=pltpu.VMEM),
        out_shape=jax.ShapeDtypeStruct((n,) + blocks[0].shape, BF16),
        scratch_shapes=[pltpu.SemaphoreType.DMA((n,))],
        compiler_params=params(8),
        cost_estimate=SMALL,
        name=name,
    )(at, *blocks, *order)


def arrange_body(n, to_ref, *refs):
    blocks, outs, sems = refs[:n], refs[-n - 1 : -1], refs[-1]
    for j in range(n):
        for k in range(n):

            @pl.when(to_ref[j] == k)
            def _():
                pltpu.make_async_copy(blocks[j], outs[k], sems.at[j]).start()

    for j in range(n):
        pltpu.make_async_copy(blocks[j], outs[0], sems.at[j]).wait()


def arrange(to, blocks, order, name):
    n = len(blocks)
    return pl.pallas_call(
        functools.partial(arrange_body, n),
        in_specs=[pl.BlockSpec(memory_space=pltpu.SMEM)] + [ANY] * (n + len(order)),
        out_specs=[pl.BlockSpec(memory_space=pltpu.VMEM)] * n,
        out_shape=[jax.ShapeDtypeStruct(blocks[0].shape, BF16)] * n,
        scratch_shapes=[pltpu.SemaphoreType.DMA((n,))],
        compiler_params=params(8),
        cost_estimate=SMALL,
        name=name,
    )(to, *blocks, *order)


def grads_body(n, offs_ref, *refs):
    blocks, (w_ref, by_gate_ref, by_up_ref, _, gg_ref, gu_ref, done_ref, piece) = refs[:n], refs[n:]
    width = blocks[0].shape[1]

    @pl.when(pl.program_id(0) == 0)
    def _():
        for j in range(n):
            piece[:, pl.ds(pl.multiple_of(offs_ref[j], 128), width)] = blocks[j][...]
        done_ref[...] = jnp.zeros_like(done_ref)

    total = dot_nt(piece[...], w_ref[...])
    gg_ref[...] = (total * by_gate_ref[...]).astype(BF16)
    gu_ref[...] = (total * by_up_ref[...]).astype(BF16)


def grads(offs, blocks, weight, by_gate, by_up, order):
    n = len(blocks)
    toks, width = blocks[0].shape
    units, feats = weight.shape
    tile = 256
    cols = pl.BlockSpec((toks, tile), lambda i, _: (0, i))
    out = jax.ShapeDtypeStruct((toks, units), BF16)
    return pl.pallas_call(
        functools.partial(grads_body, n),
        grid_spec=pltpu.PrefetchScalarGridSpec(
            num_scalar_prefetch=1,
            grid=(units // tile,),
            in_specs=[whole((toks, width))] * n
            + [pl.BlockSpec((tile, feats), lambda i, _: (i, 0)), cols, cols, ANY],
            out_specs=[cols, cols, whole((8, 128))],
            scratch_shapes=[pltpu.VMEM((toks, feats), BF16)],
        ),
        out_shape=(out, out, jax.ShapeDtypeStruct((8, 128), F32)),
        compiler_params=params(24),
        cost_estimate=SMALL,
        name="grads",
    )(offs, *blocks, weight, by_gate, by_up, order)


def wgrad_body(n, offs_ref, toks_ref, hid_ref, own_ref, *refs):
    others, (order_ref, out_ref, hid, cols, outs, hid_sems, col_sems, out_sems) = refs[:n], refs[n:]
    _, toks, width = own_ref.shape
    steps, tile, _ = hid.shape
    own, other = (pl.ds(pl.multiple_of(offs_ref[half], 128), width) for half in range(2))
    came = []
    for k in range(n):
        rows = pl.ds(pl.multiple_of(toks_ref[k], 128), toks)
        came.append((own_ref.at[k], cols.at[k * toks : (k + 1) * toks, own]))
        came.append((others[k], cols.at[rows, other]))
    came = [pltpu.make_async_copy(a, b, col_sems.at[j]) for j, (a, b) in enumerate(came)]
    came += [
        pltpu.make_async_copy(hid_ref.at[i * tile : (i + 1) * tile], hid.at[i], hid_sems.at[i])
        for i in range(steps)
    ]
    for copy in came:
        copy.start()
    for copy in came[:-steps]:
        copy.wait()
    gone = []
    for i in range(steps):
        came[i - steps].wait()
        outs[i] = lax.dot_general(
            hid[i], cols[...], (((1,), (0,)), ((), ())), preferred_element_type=F32
        ).astype(BF16)
        rows = out_ref.at[i * tile : (i + 1) * tile]
        gone.append(pltpu.make_async_copy(outs.at[i], rows, out_sems.at[i]))
        gone[-1].start()
    for copy in gone:
        copy.wait()


def wgrad(offs, tok_offs, hid, own, others, order):
    units, total = hid.shape
    n, toks, width = own.shape
    steps = 4
    tile = units // steps
    smem = pl.BlockSpec(memory_space=pltpu.SMEM)
    return pl.pallas_call(
        functools.partial(wgrad_body, n),
        in_specs=[smem, smem, HBM] + [ANY] * (n + 2),
        out_specs=HBM,
        out_shape=jax.ShapeDtypeStruct((units, 2 * width), BF16),
        scratch_shapes=[
            pltpu.VMEM((steps, tile, total), BF16),
            pltpu.VMEM((total, 2 * width), BF16),
            pltpu.VMEM((steps, tile, 2 * width), BF16),
            pltpu.SemaphoreType.DMA((steps,)),
            pltpu.SemaphoreType.DMA((2 * n,)),
            pltpu.SemaphoreType.DMA((steps,)),
        ],
        compiler_params=params(28),
        cost_estimate=pl.CostEstimate(
            flops=4 * total * units * width,
            bytes_accessed=2 * (total * (units + 2 * width) + 2 * units * width),
            transcendentals=0,
        ),
        name="wgrad",
    )(offs, tok_offs, hid, own, *others, order)


def put_slices(inner_ref, part, kept_ref, away_ref):
    outer, size, _ = kept_ref.shape
    for inner in range(2):

        @pl.when(inner_ref[0] == inner)
        def _():
            for p in range(2 * outer):
                out_ref = kept_ref if p % 2 == inner else away_ref
                out_ref[p // 2] = part[p * size : (p + 1) * size]


def grad_gram_body(inner_ref, offs_ref, *refs):
    toks_refs, (val_ref, order_ref, kept_ref, away_ref, wide) = refs[:-5], refs[-5:]
    for k, ref in enumerate(toks_refs):
        toks = ref.shape[0]
        wide[:, pl.ds(pl.multiple_of(offs_ref[k], 128), toks)] = dot_nt(val_ref[...], ref[...])
    put_slices(inner_ref, wide, kept_ref, away_ref)


def hidden_gram_body(inner_ref, offs_ref, *refs):
    hid, (val_ref, order_ref, kept_ref, away_ref, all_ref, wide, held, sem) = refs[:-8], refs[-8:]
    for k, ref in enumerate(hid):
        toks = ref.shape[1]
        held[:, pl.ds(pl.multiple_of(offs_ref[k], 128), toks)] = ref[...]
    copy = pltpu.make_async_copy(held, all_ref, sem)
    copy.start()
    wide[...] = lax.dot_general(
        val_ref[...], held[...], (((1,), (0,)), ((), ())), preferred_element_type=F32
    )
    put_slices(inner_ref, wide, kept_ref, away_ref)
    copy.wait()


def gram_call(body, inner, offs, operands, order, parts, extra, name):
    smem = pl.BlockSpec(memory_space=pltpu.SMEM)
    vmem = pl.BlockSpec(memory_space=pltpu.VMEM)
    *toks, vals = operands
    total = sum(x.size for x in toks) // vals.shape[1]
    half = jax.ShapeDtypeStruct((parts // 2, vals.shape[0] // parts, total), F32)
    shapes = [half, half, *extra]
    return pl.pallas_call(
        body,
        in_specs=[smem, smem] + [vmem] * len(operands) + [ANY],
        out_specs=[vmem, vmem] + [HBM] * len(extra),
        out_shape=shapes,
        scratch_shapes=[pltpu.VMEM((vals.shape[0], total), F32)]
        + [y for x in extra for y in (pltpu.VMEM(x.shape, x.dtype), pltpu.SemaphoreType.DMA)],
        compiler_params=params(20),
        cost_estimate=SMALL,
        name=name,
    )(inner, offs, *operands, order)


def pair_body(kept_ref, came_ref, *refs):
    refs[-1][...] = kept_ref[...] + came_ref[...]


def pair_sum(kept, came, order, name):
    vmem = pl.BlockSpec(memory_space=pltpu.VMEM)
    return pl.pallas_call(
        pair_body,
        in_specs=[vmem, vmem] + [ANY] * len(order),
        out_specs=vmem,
        out_shape=jax.ShapeDtypeStruct(kept.shape, F32),
        compiler_params=params(8),
        cost_estimate=SMALL,
        name=name,
    )(kept, came, *order)


def spread(pair):
    n_fs = lax.axis_size("fsdp")
    groups = [list(range(x, n_fs, 2)) for x in range(2)]
    return lax.all_to_all(
        pair, "fsdp", split_axis=0, concat_axis=0, axis_index_groups=groups, tiled=True
    )


def line_body(rows, assign_ref, hid_ref, grad_ref, *refs):
    out_ref = refs[-1]
    n = hid_ref.shape[0]
    hid_sum = sum(hid_ref[j] for j in range(n))
    grad_sum = sum(grad_ref[j] for j in range(n))
    by_tok = jnp.sum(hid_sum * grad_sum, axis=0, keepdims=True)
    size = by_tok.shape[1] // rows
    lane = lax.broadcasted_iota(jnp.int32, (1, 128), 1)
    line = jnp.zeros((1, 128), F32)
    for r in range(rows):
        row = jnp.sum(by_tok[:, r * size : (r + 1) * size], axis=1, keepdims=True)
        line = jnp.where(lane == r, row, line)
    for r in range(assign_ref.shape[0]):
        line = jnp.where(lane == rows + r, assign_ref[r].astype(F32), line)
    out_ref[...] = jnp.broadcast_to(line, out_ref.shape)


def score_line(assign, hid, grad, order, rows, copies):
    vmem = pl.BlockSpec(memory_space=pltpu.VMEM)
    return pl.pallas_call(
        functools.partial(line_body, rows),
        in_specs=[pl.BlockSpec(memory_space=pltpu.SMEM), vmem, vmem] + [ANY] * len(order),
        out_specs=vmem,
        out_shape=jax.ShapeDtypeStruct((copies, 128), F32),
        compiler_params=params(8),
        cost_estimate=SMALL,
        name="score_line",
    )(assign, hid, grad, *order)


def per_device(gate_act, up_act, out_grad, down_weight, val_hidden, val_grad, assign):
    n_dp = lax.axis_size("dp")
    n_fs = lax.axis_size("fsdp")
    d = lax.axis_index("dp")
    f = lax.axis_index("fsdp")
    rows_here = assign.shape[0]
    toks, width = out_grad.shape
    units = gate_act.shape[1]
    total = n_dp * toks
    n_out = n_fs // 2
    outer, inner = f // 2, f % 2

    at = (outer - jnp.arange(n_out, dtype=jnp.int32)) % n_out
    tok_offs = (d ^ jnp.arange(n_dp, dtype=jnp.int32)) * toks
    inner_at = inner.reshape(1).astype(jnp.int32)
    to = at ^ d

    first = shift(out_grad, "fsdp", 2)
    others = [swap(out_grad, "fsdp", 1)]
    far = swap(out_grad, "dp", 2)
    near = swap(out_grad, "dp", 1)
    first = after(first, others[0], far, near)
    hidden, by_gate, by_up = hidden_units(gate_act, up_act)
    hidden = after(hidden, first)
    grad_dp = [out_grad, near, far, swap(far, "dp", 1)]
    far = swap(hidden, "dp", 2)
    near = swap(hidden, "dp", 1)

    grad_kept, away = gram_call(
        grad_gram_body, inner_at, tok_offs, [*grad_dp, val_grad], first, n_fs, [], "grad_gram"
    )
    grad_came = swap(away, "fsdp", 1)
    ring = [out_grad, first]
    for _ in range(n_out - 2):
        others.append(swap(ring[-1], "fsdp", 1))
        order = away if len(ring) == 2 else near
        ring.append(after(shift(ring[-1], "fsdp", 2), others[-1], order))
    others.append(shift(others[-1], "fsdp", 2))

    def over_columns(blocks):
        return [x if k == 0 else swap(x, "dp", k) for k, x in enumerate(blocks)]

    far = after(far, ring[-1])
    hid_dp = [hidden, near, far, swap(far, "dp", 1)]
    own = stack(at, ring, [far], "own_features")
    own_cols = lax.all_to_all(own, "dp", split_axis=0, concat_axis=0, tiled=True)
    hid_kept, away, hid_all = gram_call(
        hidden_gram_body, inner_at, tok_offs, [*hid_dp, val_hidden], own, n_fs,
        [jax.ShapeDtypeStruct((units, total), BF16)], "hidden_gram",
    )
    hid_came = swap(away, "fsdp", 1)
    other = arrange(to, others, [away, grad_came], "other_features")
    other_cols = over_columns(other)
    grad_pair = pair_sum(grad_kept, grad_came, [other[0]], "grad_pair")
    grad_sums = spread(grad_pair)
    hid_pair = pair_sum(hid_kept, hid_came, [grad_pair, own_cols], "hidden_pair")
    hid_sums = spread(hid_pair)

    offs = (jnp.stack([inner, 1 - inner]) * width).astype(jnp.int32)
    places = (offs[:, None] + at[None, :] * (2 * width)).reshape(-1)
    grad_gate, grad_up, done = grads(
        places, [*ring, *others], down_weight, by_gate, by_up, hid_pair
    )

    mine = score_line(
        assign, hid_sums, grad_sums, [done, *other_cols], n_dp * rows_here, n_dp * n_fs
    )
    every = lax.all_to_all(
        mine, ("dp", "fsdp"), split_axis=0, concat_axis=0, tiled=True
    ).reshape(n_dp, n_fs, 128)
    weight_grad = wgrad(offs, tok_offs, hid_all, own_cols, other_cols, mine)

    rows = n_dp * rows_here
    scale = 1.0 / jnp.sqrt(F32(L) * VAL * FFW * D)
    scores = jnp.sum(every[:, :, :rows], axis=1) * scale
    groups = every[:, 0, rows : rows + rows_here].reshape(rows)
    onehot = (groups[None, :] == jnp.arange(n_dp, dtype=F32)[:, None]).astype(F32)
    group_values = jnp.sum(onehot * scores, axis=1)
    row_scores = lax.dynamic_slice_in_dim(scores, d * rows_here, rows_here, axis=1).T
    return (grad_gate, grad_up, weight_grad, row_scores, group_values)


def per_device_any(gate_act, up_act, out_grad, down_weight, val_hidden, val_grad, assign):
    n_dp = lax.axis_size("dp")
    me = lax.axis_index("dp")
    rows_here = assign.shape[0]
    toks = gate_act.shape[0]
    gate = gate_act.astype(F32)
    up = up_act.astype(F32)
    sig = jax.nn.sigmoid(gate)
    act = gate * sig
    hidden = (act * up).astype(BF16)
    grad_feat = lax.all_gather(out_grad, "dp", axis=0, tiled=True)
    piece = lax.all_gather(out_grad, "fsdp", axis=1, tiled=True)
    hidden_all = lax.all_gather(hidden, "dp", axis=0, tiled=True)
    grad_gram = lax.psum(dot_nt(grad_feat, val_grad), "fsdp")
    grad_cols = lax.all_to_all(piece, "dp", split_axis=1, concat_axis=0, tiled=True)
    grad_hidden = dot_nt(piece, down_weight)
    grad_gate = (grad_hidden * up * sig * (1.0 + gate * (1.0 - sig))).astype(BF16)
    grad_up = (grad_hidden * act).astype(BF16)
    product = dot_nt(hidden_all, val_hidden) * grad_gram
    part = jnp.sum(product.reshape(n_dp * rows_here, toks // rows_here * VAL), axis=1)
    weight_grad = dot_tn(hidden_all, grad_cols).astype(BF16)
    scale = 1.0 / jnp.sqrt(F32(L) * VAL * FFW * D)
    scores = lax.all_gather(lax.psum(part, "fsdp"), "dp") * scale
    groups = lax.all_gather(assign, "dp", tiled=True)
    onehot = (groups[None, :] == jnp.arange(n_dp, dtype=jnp.int32)[:, None]).astype(F32)
    group_values = jnp.sum(onehot * scores, axis=1)
    row_scores = lax.dynamic_slice_in_dim(scores, me * rows_here, rows_here, axis=1).T
    return (grad_gate, grad_up, weight_grad, row_scores, group_values)


def solution(mesh):
    in_specs = (
        P("dp", "fsdp"),
        P("dp", "fsdp"),
        P("dp", "fsdp"),
        P("fsdp", None),
        P("dp", "fsdp"),
        P("dp", "fsdp"),
        P("dp"),
    )
    out_specs = (P("dp", "fsdp"), P("dp", "fsdp"), P("fsdp", "dp"), P("dp", None), P())
    n_dp, n_fs = mesh.shape["dp"], mesh.shape["fsdp"]
    fits = n_dp == 4 and n_fs == 2 * n_dp
    return jax.shard_map(
        per_device if fits else per_device_any,
        mesh=mesh, in_specs=in_specs, out_specs=out_specs, check_vma=False,
    )
```

```python
import functools

import jax
import jax.numpy as jnp
from jax import lax
from jax.experimental import pallas as pl
from jax.experimental.pallas import tpu as pltpu
from jax.sharding import PartitionSpec as P

D = 5120
FFW = 14336
L = 128
VAL = 256

F32 = jnp.float32
BF16 = jnp.bfloat16
MIB = 1024 * 1024


def dot_nt(a, b):
    return lax.dot_general(a, b, (((1,), (1,)), ((), ())), preferred_element_type=F32)


def dot_tn(a, b):
    return lax.dot_general(a, b, (((0,), (0,)), ((), ())), preferred_element_type=F32)


def swap(x, axis, k):
    n = lax.axis_size(axis)
    return lax.ppermute(x, axis, [(s, s ^ k) for s in range(n)])


def shift(x, axis, k):
    n = lax.axis_size(axis)
    return lax.ppermute(x, axis, [(s, (s + k) % n) for s in range(n)])


def whole(shape):
    return pl.BlockSpec(shape, lambda *_: (0,) * len(shape))


def each(arrays):
    return [whole(x.shape) for x in arrays]


ANY = pl.BlockSpec(memory_space=pl.ANY)
HBM = pl.BlockSpec(memory_space=pltpu.HBM)
SMALL = pl.CostEstimate(flops=1024, bytes_accessed=1024, transcendentals=0)


def params(mib):
    return pltpu.CompilerParams(vmem_limit_bytes=mib * MIB)


def after_body(*refs):
    pass


def after(x, *order):
    return pl.pallas_call(
        after_body,
        in_specs=[ANY] * (1 + len(order)),
        out_specs=ANY,
        out_shape=jax.ShapeDtypeStruct(x.shape, x.dtype),
        input_output_aliases={0: 0},
        compiler_params=params(1),
        cost_estimate=SMALL,
        name="after",
    )(x, *order)


def hidden_body(gate_ref, up_ref, hid_ref, by_gate_ref, by_up_ref):
    gate = gate_ref[...].astype(F32)
    up = up_ref[...].astype(F32)
    sig = jax.nn.sigmoid(gate)
    act = gate * sig
    hid_ref[...] = (act * up).astype(BF16).T
    by_gate_ref[...] = (up * sig * (1.0 + gate * (1.0 - sig))).astype(BF16)
    by_up_ref[...] = act.astype(BF16)


def hidden_units(gate, up):
    toks, units = gate.shape
    tile = 256
    cols = pl.BlockSpec((toks, tile), lambda i: (0, i))
    return pl.pallas_call(
        hidden_body,
        grid=(units // tile,),
        in_specs=[cols, cols],
        out_specs=[pl.BlockSpec((tile, toks), lambda i: (i, 0)), cols, cols],
        out_shape=[
            jax.ShapeDtypeStruct((units, toks), BF16),
            jax.ShapeDtypeStruct((toks, units), BF16),
            jax.ShapeDtypeStruct((toks, units), BF16),
        ],
        compiler_params=params(12),
        cost_estimate=SMALL,
        name="hidden",
    )(gate, up)


def stack_body(n, at_ref, *refs):
    blocks, out_ref, sems = refs[:n], refs[-2], refs[-1]
    copies = [
        pltpu.make_async_copy(blocks[j], out_ref.at[at_ref[j]], sems.at[j]) for j in range(n)
    ]
    for copy in copies:
        copy.start()
    for copy in copies:
        copy.wait()


def stack(at, blocks, order, name):
    n = len(blocks)
    shape = (n,) + blocks[0].shape
    return pl.pallas_call(
        functools.partial(stack_body, n),
        grid=(1,),
        in_specs=[pl.BlockSpec(memory_space=pltpu.SMEM)] + [ANY] * (n + len(order)),
        out_specs=whole(shape),
        out_shape=jax.ShapeDtypeStruct(shape, BF16),
        scratch_shapes=[pltpu.SemaphoreType.DMA((n,))],
        compiler_params=params(8),
        cost_estimate=SMALL,
        name=name,
    )(at, *blocks, *order)


def arrange_body(n, to_ref, *refs):
    blocks, outs, sems = refs[:n], refs[-n - 1 : -1], refs[-1]
    for j in range(n):
        for k in range(n):

            @pl.when(to_ref[j] == k)
            def _():
                pltpu.make_async_copy(blocks[j], outs[k], sems.at[j]).start()

    for j in range(n):
        pltpu.make_async_copy(blocks[j], outs[0], sems.at[j]).wait()


def arrange(to, blocks, order, name):
    n = len(blocks)
    return pl.pallas_call(
        functools.partial(arrange_body, n),
        grid=(1,),
        in_specs=[pl.BlockSpec(memory_space=pltpu.SMEM)] + [ANY] * (n + len(order)),
        out_specs=each(blocks),
        out_shape=[jax.ShapeDtypeStruct(x.shape, BF16) for x in blocks],
        scratch_shapes=[pltpu.SemaphoreType.DMA((n,))],
        compiler_params=params(8),
        cost_estimate=SMALL,
        name=name,
    )(to, *blocks, *order)


def grads_body(n, offs_ref, *refs):
    blocks, (w_ref, by_gate_ref, by_up_ref, _, gg_ref, gu_ref, done_ref, piece) = refs[:n], refs[n:]
    width = blocks[0].shape[1]

    @pl.when(pl.program_id(0) == 0)
    def _():
        for j in range(n):
            piece[:, pl.ds(pl.multiple_of(offs_ref[j], 128), width)] = blocks[j][...]
        done_ref[...] = jnp.zeros_like(done_ref)

    total = dot_nt(piece[...], w_ref[...])
    gg_ref[...] = (total * by_gate_ref[...]).astype(BF16)
    gu_ref[...] = (total * by_up_ref[...]).astype(BF16)


def grads(offs, blocks, weight, by_gate, by_up, order):
    n = len(blocks)
    toks, width = blocks[0].shape
    units, feats = weight.shape
    tile = 256
    cols = pl.BlockSpec((toks, tile), lambda i, _: (0, i))
    out = jax.ShapeDtypeStruct((toks, units), BF16)
    return pl.pallas_call(
        functools.partial(grads_body, n),
        grid_spec=pltpu.PrefetchScalarGridSpec(
            num_scalar_prefetch=1,
            grid=(units // tile,),
            in_specs=[whole((toks, width))] * n
            + [pl.BlockSpec((tile, feats), lambda i, _: (i, 0)), cols, cols, ANY],
            out_specs=[cols, cols, whole((8, 128))],
            scratch_shapes=[pltpu.VMEM((toks, feats), BF16)],
        ),
        out_shape=(out, out, jax.ShapeDtypeStruct((8, 128), F32)),
        compiler_params=params(48),
        cost_estimate=SMALL,
        name="grads",
    )(offs, *blocks, weight, by_gate, by_up, order)


def wgrad_body(n, offs_ref, toks_ref, own_ref, *refs):
    others, hids = refs[:n], refs[n : 2 * n]
    out_ref, done_ref, hid, cols, outs, hid_sems, col_sems, out_sems = refs[-8:]
    done_ref[...] = jnp.zeros_like(done_ref)
    _, toks, width = own_ref.shape
    steps, tile, _ = outs.shape
    own, other = (pl.ds(pl.multiple_of(offs_ref[half], 128), width) for half in range(2))
    came = []
    for k in range(n):
        rows = pl.ds(pl.multiple_of(toks_ref[k], 128), toks)
        came.append((own_ref.at[k], cols.at[k * toks : (k + 1) * toks, own]))
        came.append((others[k], cols.at[rows, other]))
    came = [pltpu.make_async_copy(a, b, col_sems.at[j]) for j, (a, b) in enumerate(came)]
    units = []
    for i in range(steps):
        part = slice(i * tile, (i + 1) * tile)
        for k in range(n):
            place = pl.ds(pl.multiple_of(toks_ref[k], 128), toks)
            units.append(
                pltpu.make_async_copy(
                    hids[k].at[part], hid.at[part, place], hid_sems.at[i * n + k]
                )
            )
    for copy in [*units[:n], *came, *units[n:]]:
        copy.start()
    for copy in came:
        copy.wait()
    gone = []
    for i in range(steps):
        for copy in units[i * n : (i + 1) * n]:
            copy.wait()
        part = slice(i * tile, (i + 1) * tile)
        outs[i] = lax.dot_general(
            hid[part], cols[...], (((1,), (0,)), ((), ())), preferred_element_type=F32
        ).astype(BF16)
        gone.append(pltpu.make_async_copy(outs.at[i], out_ref.at[part], out_sems.at[i]))
        gone[-1].start()
    for copy in gone:
        copy.wait()


def wgrad(offs, tok_offs, own, others, hids, order):
    n, toks, width = own.shape
    units = hids[0].shape[0]
    total = n * toks
    steps = 4
    smem = pl.BlockSpec(memory_space=pltpu.SMEM)
    return pl.pallas_call(
        functools.partial(wgrad_body, n),
        in_specs=[smem, smem] + [ANY] * (2 * n + 1 + len(order)),
        out_specs=[ANY, pl.BlockSpec(memory_space=pltpu.VMEM)],
        out_shape=[
            jax.ShapeDtypeStruct((units, 2 * width), BF16),
            jax.ShapeDtypeStruct((8, 128), F32),
        ],
        scratch_shapes=[
            pltpu.VMEM((units, total), BF16),
            pltpu.VMEM((total, 2 * width), BF16),
            pltpu.VMEM((steps, units // steps, 2 * width), BF16),
            pltpu.SemaphoreType.DMA((steps * n,)),
            pltpu.SemaphoreType.DMA((2 * n,)),
            pltpu.SemaphoreType.DMA((steps,)),
        ],
        compiler_params=params(24),
        cost_estimate=SMALL,
        name="wgrad",
    )(offs, tok_offs, own, *others, *hids, *order)


def put_slices(inner_ref, part, kept_ref, away_refs):
    outer, size, total = kept_ref.shape
    half = total // 2
    for inner in range(2):

        @pl.when(inner_ref[0] == inner)
        def _():
            for p in range(2 * outer):
                rows = part[p * size : (p + 1) * size]
                if p % 2 == inner:
                    kept_ref[p // 2] = rows
                else:
                    for h in range(2):
                        away_refs[h][p // 2] = rows[:, h * half : (h + 1) * half]


def grad_gram_body(inner_ref, offs_ref, *refs):
    n = len(refs) - 6
    toks_refs, (val_ref, _, kept_ref, *away_refs, wide) = refs[:n], refs[n:]
    for k, ref in enumerate(toks_refs):
        toks = ref.shape[0]
        wide[:, pl.ds(pl.multiple_of(offs_ref[k], 128), toks)] = dot_nt(val_ref[...], ref[...])
    put_slices(inner_ref, wide, kept_ref, away_refs)


def hidden_gram_body(inner_ref, offs_ref, *refs):
    n = len(refs) - 6
    hid, (val_ref, _, kept_ref, *away_refs, wide) = refs[:n], refs[n:]
    for k, ref in enumerate(hid):
        toks = ref.shape[1]
        wide[:, pl.ds(pl.multiple_of(offs_ref[k], 128), toks)] = lax.dot_general(
            val_ref[...], ref[...], (((1,), (0,)), ((), ())), preferred_element_type=F32
        )
    put_slices(inner_ref, wide, kept_ref, away_refs)


def gram(body, inner, offs, operands, order, parts, name):
    smem = pl.BlockSpec(memory_space=pltpu.SMEM)
    *toks, vals = operands
    total = sum(x.size for x in toks) // vals.shape[1]
    kept = jax.ShapeDtypeStruct((parts // 2, vals.shape[0] // parts, total), F32)
    away = jax.ShapeDtypeStruct((parts // 2, vals.shape[0] // parts, total // 2), F32)
    shapes = [kept, away, away]
    kept, *away = pl.pallas_call(
        body,
        grid=(1,),
        in_specs=[smem, smem] + each(operands) + [ANY],
        out_specs=each(shapes),
        out_shape=shapes,
        scratch_shapes=[pltpu.VMEM((vals.shape[0], total), F32)],
        compiler_params=params(28),
        cost_estimate=SMALL,
        name=name,
    )(inner, offs, *operands, order)
    return kept, away, [swap(x, "fsdp", 1) for x in away]


def pair_body(kept_ref, *refs):
    came_refs, out_ref = refs[:2], refs[-1]
    half = came_refs[0].shape[2]
    for h in range(2):
        cols = slice(h * half, (h + 1) * half)
        out_ref[:, :, cols] = kept_ref[:, :, cols] + came_refs[h][...]


def pair_sum(kept, came, order, name):
    return pl.pallas_call(
        pair_body,
        grid=(1,),
        in_specs=each([kept, *came]) + [ANY] * len(order),
        out_specs=whole(kept.shape),
        out_shape=jax.ShapeDtypeStruct(kept.shape, F32),
        compiler_params=params(16),
        cost_estimate=SMALL,
        name=name,
    )(kept, *came, *order)


def spread(pair):
    n_fs = lax.axis_size("fsdp")
    groups = [list(range(x, n_fs, 2)) for x in range(2)]
    return lax.all_to_all(
        pair, "fsdp", split_axis=0, concat_axis=0, axis_index_groups=groups, tiled=True
    )


def line_body(rows, assign_ref, hid_ref, grad_ref, *refs):
    out_ref = refs[-1]
    n = hid_ref.shape[0]
    hid_sum = sum(hid_ref[j] for j in range(n))
    grad_sum = sum(grad_ref[j] for j in range(n))
    by_tok = jnp.sum(hid_sum * grad_sum, axis=0, keepdims=True)
    size = by_tok.shape[1] // rows
    lane = lax.broadcasted_iota(jnp.int32, (1, 128), 1)
    line = jnp.zeros((1, 128), F32)
    for r in range(rows):
        row = jnp.sum(by_tok[:, r * size : (r + 1) * size], axis=1, keepdims=True)
        line = jnp.where(lane == r, row, line)
    for r in range(assign_ref.shape[0]):
        line = jnp.where(lane == rows + r, assign_ref[r].astype(F32), line)
    out_ref[...] = jnp.broadcast_to(line, out_ref.shape)


def score_line(assign, hid, grad, order, rows, copies):
    return pl.pallas_call(
        functools.partial(line_body, rows),
        grid=(1,),
        in_specs=[pl.BlockSpec(memory_space=pltpu.SMEM)] + each([hid, grad]) + [ANY] * len(order),
        out_specs=whole((copies, 128)),
        out_shape=jax.ShapeDtypeStruct((copies, 128), F32),
        compiler_params=params(8),
        cost_estimate=SMALL,
        name="score_line",
    )(assign, hid, grad, *order)


def per_device(gate_act, up_act, out_grad, down_weight, val_hidden, val_grad, assign):
    n_dp = lax.axis_size("dp")
    n_fs = lax.axis_size("fsdp")
    d = lax.axis_index("dp")
    f = lax.axis_index("fsdp")
    rows_here = assign.shape[0]
    toks, width = out_grad.shape
    units = gate_act.shape[1]
    total = n_dp * toks
    n_out = n_fs // 2
    outer, inner = f // 2, f % 2

    at = (outer - jnp.arange(n_out, dtype=jnp.int32)) % n_out
    tok_offs = (d ^ jnp.arange(n_dp, dtype=jnp.int32)) * toks
    inner_at = inner.reshape(1).astype(jnp.int32)
    to = at ^ d

    first = shift(out_grad, "fsdp", 2)
    others = [swap(out_grad, "fsdp", 1)]
    far = swap(out_grad, "dp", 2)
    near = swap(out_grad, "dp", 1)
    first = after(first, others[0], far, near)
    hidden, by_gate, by_up = hidden_units(gate_act, up_act)
    hidden = after(hidden, first)
    grad_dp = [out_grad, near, far, swap(far, "dp", 1)]
    far = swap(hidden, "dp", 2)
    near = swap(hidden, "dp", 1)

    grad_kept, away, grad_came = gram(
        grad_gram_body, inner_at, tok_offs, [*grad_dp, val_grad], first, n_fs, "grad_gram"
    )
    ring = [out_grad, first]
    others.append(swap(ring[1], "fsdp", 1))
    ring.append(after(shift(ring[1], "fsdp", 2), others[1], grad_came[0]))
    others.append(swap(ring[2], "fsdp", 1))
    ring.append(after(shift(ring[2], "fsdp", 2), near))
    others.append(shift(others[2], "fsdp", 2))

    def over_columns(blocks):
        return [x if k == 0 else swap(x, "dp", k) for k, x in enumerate(blocks)]

    far = after(far, ring[3])
    hid_dp = [hidden, near, far, swap(far, "dp", 1)]
    own = stack(at, ring, [far], "own_features")
    own_cols = lax.all_to_all(own, "dp", split_axis=0, concat_axis=0, tiled=True)
    hid_kept, away, hid_came = gram(
        hidden_gram_body, inner_at, tok_offs, [*hid_dp, val_hidden], own, n_fs, "hidden_gram"
    )
    grad_pair = pair_sum(grad_kept, grad_came, away, "grad_pair")
    other = arrange(to, others, [grad_pair, hid_came[0]], "other_features")
    other_cols = over_columns(other)
    grad_sums = spread(grad_pair)

    offs = (jnp.stack([inner, 1 - inner]) * width).astype(jnp.int32)
    places = (offs[:, None] + at[None, :] * (2 * width)).reshape(-1)
    grad_gate, grad_up, done = grads(
        places, [*ring, *others], down_weight, by_gate, by_up, other[0]
    )
    hid_pair = pair_sum(hid_kept, hid_came, [done, own_cols], "hidden_pair")
    hid_sums = spread(hid_pair)
    weight_grad, done = wgrad(offs, tok_offs, own_cols, other_cols, hid_dp, [hid_pair])

    mine = score_line(
        assign, hid_sums, grad_sums, [done], n_dp * rows_here, n_dp * n_fs
    )
    every = lax.all_to_all(
        mine, ("dp", "fsdp"), split_axis=0, concat_axis=0, tiled=True
    ).reshape(n_dp, n_fs, 128)

    rows = n_dp * rows_here
    scale = 1.0 / jnp.sqrt(F32(L) * VAL * FFW * D)
    scores = jnp.sum(every[:, :, :rows], axis=1) * scale
    groups = every[:, 0, rows : rows + rows_here].reshape(rows)
    onehot = (groups[None, :] == jnp.arange(n_dp, dtype=F32)[:, None]).astype(F32)
    group_values = jnp.sum(onehot * scores, axis=1)
    row_scores = lax.dynamic_slice_in_dim(scores, d * rows_here, rows_here, axis=1).T
    return (grad_gate, grad_up, weight_grad, row_scores, group_values)


def per_device_any(gate_act, up_act, out_grad, down_weight, val_hidden, val_grad, assign):
    n_dp = lax.axis_size("dp")
    me = lax.axis_index("dp")
    rows_here = assign.shape[0]
    toks = gate_act.shape[0]
    gate = gate_act.astype(F32)
    up = up_act.astype(F32)
    sig = jax.nn.sigmoid(gate)
    act = gate * sig
    hidden = (act * up).astype(BF16)
    grad_feat = lax.all_gather(out_grad, "dp", axis=0, tiled=True)
    piece = lax.all_gather(out_grad, "fsdp", axis=1, tiled=True)
    hidden_all = lax.all_gather(hidden, "dp", axis=0, tiled=True)
    grad_gram = lax.psum(dot_nt(grad_feat, val_grad), "fsdp")
    grad_cols = lax.all_to_all(piece, "dp", split_axis=1, concat_axis=0, tiled=True)
    grad_hidden = dot_nt(piece, down_weight)
    grad_gate = (grad_hidden * up * sig * (1.0 + gate * (1.0 - sig))).astype(BF16)
    grad_up = (grad_hidden * act).astype(BF16)
    product = dot_nt(hidden_all, val_hidden) * grad_gram
    part = jnp.sum(product.reshape(n_dp * rows_here, toks // rows_here * VAL), axis=1)
    weight_grad = dot_tn(hidden_all, grad_cols).astype(BF16)
    scale = 1.0 / jnp.sqrt(F32(L) * VAL * FFW * D)
    scores = lax.all_gather(lax.psum(part, "fsdp"), "dp") * scale
    groups = lax.all_gather(assign, "dp", tiled=True)
    onehot = (groups[None, :] == jnp.arange(n_dp, dtype=jnp.int32)[:, None]).astype(F32)
    group_values = jnp.sum(onehot * scores, axis=1)
    row_scores = lax.dynamic_slice_in_dim(scores, me * rows_here, rows_here, axis=1).T
    return (grad_gate, grad_up, weight_grad, row_scores, group_values)


def solution(mesh):
    in_specs = (
        P("dp", "fsdp"),
        P("dp", "fsdp"),
        P("dp", "fsdp"),
        P("fsdp", None),
        P("dp", "fsdp"),
        P("dp", "fsdp"),
        P("dp"),
    )
    out_specs = (P("dp", "fsdp"), P("dp", "fsdp"), P("fsdp", "dp"), P("dp", None), P())
    n_dp, n_fs = mesh.shape["dp"], mesh.shape["fsdp"]
    fits = n_dp == 4 and n_fs == 2 * n_dp
    return jax.shard_map(
        per_device if fits else per_device_any,
        mesh=mesh, in_specs=in_specs, out_specs=out_specs, check_vma=False,
    )
```

```python
import functools

import jax
import jax.numpy as jnp
from jax import lax
from jax.experimental import pallas as pl
from jax.experimental.pallas import tpu as pltpu
from jax.sharding import PartitionSpec as P

D = 5120
FFW = 14336
L = 128
VAL = 256

F32 = jnp.float32
BF16 = jnp.bfloat16
VMEM_LIMIT = 63 * 1024 * 1024


def dot_nt(a, b):
    return lax.dot_general(a, b, (((1,), (1,)), ((), ())), preferred_element_type=F32)


def dot_tn(a, b):
    return lax.dot_general(a, b, (((0,), (0,)), ((), ())), preferred_element_type=F32)


def swap(x, axis, k):
    n = lax.axis_size(axis)
    return lax.ppermute(x, axis, [(s, s ^ k) for s in range(n)])


def shift(x, axis, k):
    n = lax.axis_size(axis)
    return lax.ppermute(x, axis, [(s, (s + k) % n) for s in range(n)])


def whole(shape):
    return pl.BlockSpec(shape, lambda *_: (0,) * len(shape))


def each(arrays):
    return [whole(x.shape) for x in arrays]


ANY = pl.BlockSpec(memory_space=pl.ANY)
HBM = pl.BlockSpec(memory_space=pltpu.HBM)
SMALL = pl.CostEstimate(flops=1024, bytes_accessed=1024, transcendentals=0)


def params():
    return pltpu.CompilerParams(vmem_limit_bytes=VMEM_LIMIT)


def after_body(*refs):
    pass


def after(x, *order):
    return pl.pallas_call(
        after_body,
        in_specs=[ANY] * (1 + len(order)),
        out_specs=ANY,
        out_shape=jax.ShapeDtypeStruct(x.shape, x.dtype),
        input_output_aliases={0: 0},
        compiler_params=params(),
        cost_estimate=SMALL,
        name="after",
    )(x, *order)


def hidden_body(gate_ref, up_ref, hid_ref, by_gate_ref, by_up_ref):
    gate = gate_ref[...].astype(F32)
    up = up_ref[...].astype(F32)
    sig = jax.nn.sigmoid(gate)
    act = gate * sig
    hid_ref[...] = (act * up).astype(BF16).T
    by_gate_ref[...] = (up * sig * (1.0 + gate * (1.0 - sig))).astype(BF16)
    by_up_ref[...] = act.astype(BF16)


def hidden_units(gate, up):
    toks, units = gate.shape
    tile = 256
    cols = pl.BlockSpec((toks, tile), lambda i: (0, i))
    return pl.pallas_call(
        hidden_body,
        grid=(units // tile,),
        in_specs=[cols, cols],
        out_specs=[pl.BlockSpec((tile, toks), lambda i: (i, 0)), cols, cols],
        out_shape=[
            jax.ShapeDtypeStruct((units, toks), BF16),
            jax.ShapeDtypeStruct((toks, units), BF16),
            jax.ShapeDtypeStruct((toks, units), BF16),
        ],
        compiler_params=params(),
        cost_estimate=SMALL,
        name="hidden",
    )(gate, up)


def stack_body(n, at_ref, *refs):
    blocks, out_ref, sems = refs[:n], refs[-2], refs[-1]
    copies = [
        pltpu.make_async_copy(blocks[j], out_ref.at[at_ref[j]], sems.at[j]) for j in range(n)
    ]
    for copy in copies:
        copy.start()
    for copy in copies:
        copy.wait()


def stack(at, blocks, order, name):
    n = len(blocks)
    shape = (n,) + blocks[0].shape
    return pl.pallas_call(
        functools.partial(stack_body, n),
        grid=(1,),
        in_specs=[pl.BlockSpec(memory_space=pltpu.SMEM)] + [ANY] * (n + len(order)),
        out_specs=whole(shape),
        out_shape=jax.ShapeDtypeStruct(shape, BF16),
        scratch_shapes=[pltpu.SemaphoreType.DMA((n,))],
        compiler_params=params(),
        cost_estimate=SMALL,
        name=name,
    )(at, *blocks, *order)


def arrange_body(n, to_ref, *refs):
    blocks, outs, sems = refs[:n], refs[-n - 1 : -1], refs[-1]
    for j in range(n):
        for k in range(n):

            @pl.when(to_ref[j] == k)
            def _():
                pltpu.make_async_copy(blocks[j], outs[k], sems.at[j]).start()

    for j in range(n):
        pltpu.make_async_copy(blocks[j], outs[0], sems.at[j]).wait()


def arrange(to, blocks, order, name):
    n = len(blocks)
    return pl.pallas_call(
        functools.partial(arrange_body, n),
        grid=(1,),
        in_specs=[pl.BlockSpec(memory_space=pltpu.SMEM)] + [ANY] * (n + len(order)),
        out_specs=each(blocks),
        out_shape=[jax.ShapeDtypeStruct(x.shape, BF16) for x in blocks],
        scratch_shapes=[pltpu.SemaphoreType.DMA((n,))],
        compiler_params=params(),
        cost_estimate=SMALL,
        name=name,
    )(to, *blocks, *order)


def grads_body(n, offs_ref, *refs):
    blocks, (w_ref, by_gate_ref, by_up_ref), (gg_ref, gu_ref, done_ref, piece) = (
        refs[:n], refs[n : n + 3], refs[-4:]
    )
    width = blocks[0].shape[1]

    @pl.when(pl.program_id(0) == 0)
    def _():
        for j in range(n):
            piece[:, pl.ds(pl.multiple_of(offs_ref[j], 128), width)] = blocks[j][...]
        done_ref[...] = jnp.zeros_like(done_ref)

    total = dot_nt(piece[...], w_ref[...])
    gg_ref[...] = (total * by_gate_ref[...]).astype(BF16)
    gu_ref[...] = (total * by_up_ref[...]).astype(BF16)


def grads(offs, blocks, weight, by_gate, by_up, order, tiles, made, name):
    n = len(blocks)
    toks, width = blocks[0].shape
    units, feats = weight.shape
    tile = 256
    first, count = tiles
    cols = pl.BlockSpec((toks, tile), lambda i, _: (0, first + i))
    out = jax.ShapeDtypeStruct((toks, units), BF16)
    operands = [offs, *blocks, weight, by_gate, by_up, *order, *made]
    return pl.pallas_call(
        functools.partial(grads_body, n),
        grid_spec=pltpu.PrefetchScalarGridSpec(
            num_scalar_prefetch=1,
            grid=(count,),
            in_specs=[whole((toks, width))] * n
            + [pl.BlockSpec((tile, feats), lambda i, _: (first + i, 0)), cols, cols]
            + [ANY] * (len(order) + len(made)),
            out_specs=[cols, cols, whole((8, 128))],
            scratch_shapes=[pltpu.VMEM((toks, feats), BF16)],
        ),
        out_shape=(out, out, jax.ShapeDtypeStruct((8, 128), F32)),
        input_output_aliases={len(operands) - len(made) + k: k for k in range(len(made))},
        compiler_params=params(),
        cost_estimate=pl.CostEstimate(
            flops=2 * toks * tile * count * feats,
            bytes_accessed=2 * (tile * count * feats + toks * feats + 4 * toks * tile * count),
            transcendentals=0,
        ),
        name=name,
    )(*operands)


def wgrad_body(n, first, offs_ref, toks_ref, own_ref, *refs):
    others, hids = refs[:n], refs[n : 2 * n]
    out_ref, done_ref, hid, cols, outs, hid_sems, col_sems, out_sems = refs[-8:]
    done_ref[...] = jnp.zeros_like(done_ref)
    _, toks, width = own_ref.shape
    steps, tile, _ = outs.shape
    base = first * tile
    own, other = (pl.ds(pl.multiple_of(offs_ref[half], 128), width) for half in range(2))
    came = []
    for k in range(n):
        rows = pl.ds(pl.multiple_of(toks_ref[k], 128), toks)
        came.append((own_ref.at[k], cols.at[k * toks : (k + 1) * toks, own]))
        came.append((others[k], cols.at[rows, other]))
    came = [pltpu.make_async_copy(a, b, col_sems.at[j]) for j, (a, b) in enumerate(came)]
    units = []
    for i in range(steps):
        part = slice(i * tile, (i + 1) * tile)
        taken = slice(base + i * tile, base + (i + 1) * tile)
        for k in range(n):
            place = pl.ds(pl.multiple_of(toks_ref[k], 128), toks)
            units.append(
                pltpu.make_async_copy(
                    hids[k].at[taken], hid.at[part, place], hid_sems.at[i * n + k]
                )
            )
    for copy in [*units[:n], *came, *units[n:]]:
        copy.start()
    for copy in came:
        copy.wait()
    gone = []
    for i in range(steps):
        for copy in units[i * n : (i + 1) * n]:
            copy.wait()
        part = slice(i * tile, (i + 1) * tile)
        outs[i] = lax.dot_general(
            hid[part], cols[...], (((1,), (0,)), ((), ())), preferred_element_type=F32
        ).astype(BF16)
        made = out_ref.at[base + i * tile : base + (i + 1) * tile]
        gone.append(pltpu.make_async_copy(outs.at[i], made, out_sems.at[i]))
        gone[-1].start()
    for copy in gone:
        copy.wait()


def wgrad(offs, tok_offs, own, others, hids, order, parts, made, name):
    n, toks, width = own.shape
    units = hids[0].shape[0]
    total = n * toks
    first, steps = parts
    tile = units // 4
    smem = pl.BlockSpec(memory_space=pltpu.SMEM)
    operands = [offs, tok_offs, own, *others, *hids, *order, *made]
    return pl.pallas_call(
        functools.partial(wgrad_body, n, first),
        in_specs=[smem, smem] + [ANY] * (len(operands) - 2),
        out_specs=[ANY, pl.BlockSpec(memory_space=pltpu.VMEM)],
        out_shape=[
            jax.ShapeDtypeStruct((units, 2 * width), BF16),
            jax.ShapeDtypeStruct((8, 128), F32),
        ],
        scratch_shapes=[
            pltpu.VMEM((steps * tile, total), BF16),
            pltpu.VMEM((total, 2 * width), BF16),
            pltpu.VMEM((steps, tile, 2 * width), BF16),
            pltpu.SemaphoreType.DMA((steps * n,)),
            pltpu.SemaphoreType.DMA((2 * n,)),
            pltpu.SemaphoreType.DMA((steps,)),
        ],
        input_output_aliases={len(operands) - len(made) + k: k for k in range(len(made))},
        compiler_params=params(),
        cost_estimate=pl.CostEstimate(
            flops=4 * total * steps * tile * width,
            bytes_accessed=2 * (total * (steps * tile + 2 * width) + 2 * steps * tile * width),
            transcendentals=0,
        ),
        name=name,
    )(*operands)


def put_slices(inner_ref, part, kept_ref, away_refs):
    outer, size, total = kept_ref.shape
    cut = total // len(away_refs)
    for inner in range(2):

        @pl.when(inner_ref[0] == inner)
        def _():
            for p in range(2 * outer):
                rows = part[p * size : (p + 1) * size]
                if p % 2 == inner:
                    kept_ref[p // 2] = rows
                else:
                    for h, away_ref in enumerate(away_refs):
                        away_ref[p // 2] = rows[:, h * cut : (h + 1) * cut]


def grad_gram_body(n, cuts, inner_ref, offs_ref, *refs):
    toks_refs, val_ref, (kept_ref, *away_refs, wide) = refs[:n], refs[n], refs[-2 - cuts :]
    for k, ref in enumerate(toks_refs):
        toks = ref.shape[0]
        wide[:, pl.ds(pl.multiple_of(offs_ref[k], 128), toks)] = dot_nt(val_ref[...], ref[...])
    put_slices(inner_ref, wide, kept_ref, away_refs)


def hidden_gram_body(n, cuts, inner_ref, offs_ref, *refs):
    hid, val_ref, (kept_ref, *away_refs, wide) = refs[:n], refs[n], refs[-2 - cuts :]
    for k, ref in enumerate(hid):
        toks = ref.shape[1]
        wide[:, pl.ds(pl.multiple_of(offs_ref[k], 128), toks)] = lax.dot_general(
            val_ref[...], ref[...], (((1,), (0,)), ((), ())), preferred_element_type=F32
        )
    put_slices(inner_ref, wide, kept_ref, away_refs)


def gram(body, inner, offs, operands, order, parts, cuts, name):
    smem = pl.BlockSpec(memory_space=pltpu.SMEM)
    *toks, vals = operands
    total = sum(x.size for x in toks) // vals.shape[1]
    kept = jax.ShapeDtypeStruct((parts // 2, vals.shape[0] // parts, total), F32)
    away = jax.ShapeDtypeStruct((parts // 2, vals.shape[0] // parts, total // cuts), F32)
    shapes = [kept] + [away] * cuts
    kept, *away = pl.pallas_call(
        functools.partial(body, len(toks), cuts),
        grid=(1,),
        in_specs=[smem, smem] + each(operands) + [ANY] * len(order),
        out_specs=each(shapes),
        out_shape=shapes,
        scratch_shapes=[pltpu.VMEM((vals.shape[0], total), F32)],
        compiler_params=params(),
        cost_estimate=SMALL,
        name=name,
    )(inner, offs, *operands, *order)
    return kept, away, [swap(x, "fsdp", 1) for x in away]


def pair_body(cuts, kept_ref, *refs):
    came_refs, out_ref = refs[:cuts], refs[-1]
    cut = kept_ref.shape[2] // cuts
    for h in range(cuts):
        cols = slice(h * cut, (h + 1) * cut)
        out_ref[:, :, cols] = kept_ref[:, :, cols] + came_refs[h][...]


def pair_sum(kept, came, order, name):
    return pl.pallas_call(
        functools.partial(pair_body, len(came)),
        grid=(1,),
        in_specs=each([kept, *came]) + [ANY] * len(order),
        out_specs=whole(kept.shape),
        out_shape=jax.ShapeDtypeStruct(kept.shape, F32),
        compiler_params=params(),
        cost_estimate=SMALL,
        name=name,
    )(kept, *came, *order)


def spread(pair):
    n_fs = lax.axis_size("fsdp")
    groups = [list(range(x, n_fs, 2)) for x in range(2)]
    return lax.all_to_all(
        pair, "fsdp", split_axis=0, concat_axis=0, axis_index_groups=groups, tiled=True
    )


def line_body(rows, assign_ref, hid_ref, grad_ref, *refs):
    out_ref = refs[-1]
    n = hid_ref.shape[0]
    hid_sum = sum(hid_ref[j] for j in range(n))
    grad_sum = sum(grad_ref[j] for j in range(n))
    by_tok = jnp.sum(hid_sum * grad_sum, axis=0, keepdims=True)
    size = by_tok.shape[1] // rows
    lane = lax.broadcasted_iota(jnp.int32, (1, 128), 1)
    line = jnp.zeros((1, 128), F32)
    for r in range(rows):
        row = jnp.sum(by_tok[:, r * size : (r + 1) * size], axis=1, keepdims=True)
        line = jnp.where(lane == r, row, line)
    for r in range(assign_ref.shape[0]):
        line = jnp.where(lane == rows + r, assign_ref[r].astype(F32), line)
    out_ref[...] = jnp.broadcast_to(line, out_ref.shape)


def score_line(assign, hid, grad, order, rows, copies):
    return pl.pallas_call(
        functools.partial(line_body, rows),
        grid=(1,),
        in_specs=[pl.BlockSpec(memory_space=pltpu.SMEM)] + each([hid, grad]) + [ANY] * len(order),
        out_specs=whole((copies, 128)),
        out_shape=jax.ShapeDtypeStruct((copies, 128), F32),
        compiler_params=params(),
        cost_estimate=SMALL,
        name="score_line",
    )(assign, hid, grad, *order)


def per_device(gate_act, up_act, out_grad, down_weight, val_hidden, val_grad, assign):
    n_dp = lax.axis_size("dp")
    n_fs = lax.axis_size("fsdp")
    d = lax.axis_index("dp")
    f = lax.axis_index("fsdp")
    rows_here = assign.shape[0]
    toks, width = out_grad.shape
    units = gate_act.shape[1]
    total = n_dp * toks
    n_out = n_fs // 2
    outer, inner = f // 2, f % 2

    at = (outer - jnp.arange(n_out, dtype=jnp.int32)) % n_out
    tok_offs = (d ^ jnp.arange(n_dp, dtype=jnp.int32)) * toks
    inner_at = inner.reshape(1).astype(jnp.int32)
    to = at ^ d

    first = shift(out_grad, "fsdp", 2)
    others = [swap(out_grad, "fsdp", 1)]
    far = swap(out_grad, "dp", 2)
    near = swap(out_grad, "dp", 1)
    first = after(first, others[0], far, near)
    hidden, by_gate, by_up = hidden_units(gate_act, up_act)
    hidden = after(hidden, first)
    grad_dp = [out_grad, near, far, swap(far, "dp", 1)]
    far = swap(hidden, "dp", 2)
    near = swap(hidden, "dp", 1)

    grad_kept, away, grad_came = gram(
        grad_gram_body, inner_at, tok_offs, [*grad_dp, val_grad], [first], n_fs, 1, "grad_gram"
    )
    ring = [out_grad, first]
    others.append(swap(ring[1], "fsdp", 1))
    ring.append(after(shift(ring[1], "fsdp", 2), others[1], *away))
    others.append(swap(ring[2], "fsdp", 1))
    ring.append(after(shift(ring[2], "fsdp", 2), others[2], near))
    others.append(shift(others[2], "fsdp", 2))

    def over_columns(blocks):
        return [x if k == 0 else swap(x, "dp", k) for k, x in enumerate(blocks)]

    far = after(far, ring[3])
    hid_dp = [hidden, near, far, swap(far, "dp", 1)]
    own = stack(at, ring, [far], "own_features")
    own_cols = lax.all_to_all(own, "dp", split_axis=0, concat_axis=0, tiled=True)
    hid_kept, away, hid_came = gram(
        hidden_gram_body, inner_at, tok_offs, [*hid_dp, val_hidden], [own, others[3]], n_fs, 2,
        "hidden_gram",
    )
    offs = (jnp.stack([inner, 1 - inner]) * width).astype(jnp.int32)
    places = (offs[:, None] + at[None, :] * (2 * width)).reshape(-1)
    tiles = units // 256
    *made, done = grads(
        places, [*ring, *others], down_weight, by_gate, by_up, away, (0, tiles // 2 + 1), [],
        "grads_first",
    )
    grad_pair = pair_sum(grad_kept, grad_came, [done, hid_came[0]], "grad_pair")
    grad_sums = spread(grad_pair)
    other = arrange(to, others, [grad_pair], "other_features")
    other_cols = over_columns(other)
    grad_gate, grad_up, done = grads(
        places, [*ring, *others], down_weight, by_gate, by_up, [other[0]],
        (tiles // 2 + 1, tiles - tiles // 2 - 1), made, "grads_last",
    )
    hid_pair = pair_sum(hid_kept, hid_came, [done, *other_cols[1:3]], "hidden_pair")
    hid_sums = spread(hid_pair)
    made, done = wgrad(
        offs, tok_offs, own_cols, other_cols, hid_dp, [hid_pair], (0, 2), [], "wgrad_first"
    )

    mine = score_line(
        assign, hid_sums, grad_sums, [done], n_dp * rows_here, n_dp * n_fs
    )
    every = lax.all_to_all(
        mine, ("dp", "fsdp"), split_axis=0, concat_axis=0, tiled=True
    ).reshape(n_dp, n_fs, 128)
    weight_grad, _ = wgrad(
        offs, tok_offs, own_cols, other_cols, hid_dp, [mine], (2, 2), [made], "wgrad_last"
    )

    rows = n_dp * rows_here
    scale = 1.0 / jnp.sqrt(F32(L) * VAL * FFW * D)
    scores = jnp.sum(every[:, :, :rows], axis=1) * scale
    groups = every[:, 0, rows : rows + rows_here].reshape(rows)
    onehot = (groups[None, :] == jnp.arange(n_dp, dtype=F32)[:, None]).astype(F32)
    group_values = jnp.sum(onehot * scores, axis=1)
    row_scores = lax.dynamic_slice_in_dim(scores, d * rows_here, rows_here, axis=1).T
    return (grad_gate, grad_up, weight_grad, row_scores, group_values)


def per_device_any(gate_act, up_act, out_grad, down_weight, val_hidden, val_grad, assign):
    n_dp = lax.axis_size("dp")
    me = lax.axis_index("dp")
    rows_here = assign.shape[0]
    toks = gate_act.shape[0]
    gate = gate_act.astype(F32)
    up = up_act.astype(F32)
    sig = jax.nn.sigmoid(gate)
    act = gate * sig
    hidden = (act * up).astype(BF16)
    grad_feat = lax.all_gather(out_grad, "dp", axis=0, tiled=True)
    piece = lax.all_gather(out_grad, "fsdp", axis=1, tiled=True)
    hidden_all = lax.all_gather(hidden, "dp", axis=0, tiled=True)
    grad_gram = lax.psum(dot_nt(grad_feat, val_grad), "fsdp")
    grad_cols = lax.all_to_all(piece, "dp", split_axis=1, concat_axis=0, tiled=True)
    grad_hidden = dot_nt(piece, down_weight)
    grad_gate = (grad_hidden * up * sig * (1.0 + gate * (1.0 - sig))).astype(BF16)
    grad_up = (grad_hidden * act).astype(BF16)
    product = dot_nt(hidden_all, val_hidden) * grad_gram
    part = jnp.sum(product.reshape(n_dp * rows_here, toks // rows_here * VAL), axis=1)
    weight_grad = dot_tn(hidden_all, grad_cols).astype(BF16)
    scale = 1.0 / jnp.sqrt(F32(L) * VAL * FFW * D)
    scores = lax.all_gather(lax.psum(part, "fsdp"), "dp") * scale
    groups = lax.all_gather(assign, "dp", tiled=True)
    onehot = (groups[None, :] == jnp.arange(n_dp, dtype=jnp.int32)[:, None]).astype(F32)
    group_values = jnp.sum(onehot * scores, axis=1)
    row_scores = lax.dynamic_slice_in_dim(scores, me * rows_here, rows_here, axis=1).T
    return (grad_gate, grad_up, weight_grad, row_scores, group_values)


def solution(mesh):
    in_specs = (
        P("dp", "fsdp"),
        P("dp", "fsdp"),
        P("dp", "fsdp"),
        P("fsdp", None),
        P("dp", "fsdp"),
        P("dp", "fsdp"),
        P("dp"),
    )
    out_specs = (P("dp", "fsdp"), P("dp", "fsdp"), P("fsdp", "dp"), P("dp", None), P())
    n_dp, n_fs = mesh.shape["dp"], mesh.shape["fsdp"]
    fits = n_dp == 4 and n_fs == 2 * n_dp
    return jax.shard_map(
        per_device if fits else per_device_any,
        mesh=mesh, in_specs=in_specs, out_specs=out_specs, check_vma=False,
    )
```

```python
import functools

import jax
import jax.numpy as jnp
from jax import lax
from jax.experimental import pallas as pl
from jax.experimental.pallas import tpu as pltpu
from jax.sharding import PartitionSpec as P

D = 5120
FFW = 14336
L = 128
VAL = 256

F32 = jnp.float32
BF16 = jnp.bfloat16
TILE = 256
VMEM_LIMIT = 63 * 1024 * 1024


def dot_nt(a, b):
    return lax.dot_general(a, b, (((1,), (1,)), ((), ())), preferred_element_type=F32)


def dot_tn(a, b):
    return lax.dot_general(a, b, (((0,), (0,)), ((), ())), preferred_element_type=F32)


def swap(x, axis, k):
    n = lax.axis_size(axis)
    return lax.ppermute(x, axis, [(s, s ^ k) for s in range(n)])


def shift(x, axis, k):
    n = lax.axis_size(axis)
    return lax.ppermute(x, axis, [(s, (s + k) % n) for s in range(n)])


def whole(shape):
    return pl.BlockSpec(shape, lambda *_: (0,) * len(shape))


def each(arrays):
    return [whole(x.shape) for x in arrays]


ANY = pl.BlockSpec(memory_space=pl.ANY)
HBM = pl.BlockSpec(memory_space=pltpu.HBM)
SMALL = pl.CostEstimate(flops=1024, bytes_accessed=1024, transcendentals=0)


def params():
    return pltpu.CompilerParams(vmem_limit_bytes=VMEM_LIMIT)


def after_body(*refs):
    pass


def after(x, *order):
    return pl.pallas_call(
        after_body,
        in_specs=[ANY] * (1 + len(order)),
        out_specs=ANY,
        out_shape=jax.ShapeDtypeStruct(x.shape, x.dtype),
        input_output_aliases={0: 0},
        compiler_params=params(),
        cost_estimate=SMALL,
        name="after",
    )(x, *order)


def hidden_body(gate_ref, up_ref, hid_ref):
    gate = gate_ref[...].astype(F32)
    hid_ref[...] = (gate * jax.nn.sigmoid(gate) * up_ref[...].astype(F32)).astype(BF16).T


def hidden_units(gate, up, first, count, name):
    toks = gate.shape[0]
    cols = pl.BlockSpec((toks, TILE), lambda i: (0, first + i))
    return pl.pallas_call(
        hidden_body,
        grid=(count,),
        in_specs=[cols, cols],
        out_specs=pl.BlockSpec((TILE, toks), lambda i: (i, 0)),
        out_shape=jax.ShapeDtypeStruct((count * TILE, toks), BF16),
        compiler_params=params(),
        cost_estimate=SMALL,
        name=name,
    )(gate, up)


def factors_body(gate_ref, up_ref, order_ref, by_gate_ref, by_up_ref):
    gate = gate_ref[...].astype(F32)
    sig = jax.nn.sigmoid(gate)
    up = up_ref[...].astype(F32)
    by_gate_ref[...] = (up * sig * (1.0 + gate * (1.0 - sig))).astype(BF16)
    by_up_ref[...] = (gate * sig).astype(BF16)


def factors(gate, up, order):
    toks, units = gate.shape
    cols = pl.BlockSpec((toks, TILE), lambda i: (0, i))
    return pl.pallas_call(
        factors_body,
        grid=(units // TILE,),
        in_specs=[cols, cols, ANY],
        out_specs=[cols, cols],
        out_shape=[jax.ShapeDtypeStruct((toks, units), BF16)] * 2,
        compiler_params=params(),
        cost_estimate=SMALL,
        name="factors",
    )(gate, up, order)


def stack_body(n, at_ref, *refs):
    blocks, out_ref, sems = refs[:n], refs[-2], refs[-1]
    copies = [
        pltpu.make_async_copy(blocks[j], out_ref.at[at_ref[j]], sems.at[j]) for j in range(n)
    ]
    for copy in copies:
        copy.start()
    for copy in copies:
        copy.wait()


def stack(at, blocks, order, name):
    n = len(blocks)
    shape = (n,) + blocks[0].shape
    return pl.pallas_call(
        functools.partial(stack_body, n),
        grid=(1,),
        in_specs=[pl.BlockSpec(memory_space=pltpu.SMEM)] + [ANY] * (n + len(order)),
        out_specs=whole(shape),
        out_shape=jax.ShapeDtypeStruct(shape, BF16),
        scratch_shapes=[pltpu.SemaphoreType.DMA((n,))],
        compiler_params=params(),
        cost_estimate=SMALL,
        name=name,
    )(at, *blocks, *order)


def arrange_body(n, to_ref, *refs):
    blocks, outs, sems = refs[:n], refs[-n - 1 : -1], refs[-1]
    for j in range(n):
        for k in range(n):

            @pl.when(to_ref[j] == k)
            def _():
                pltpu.make_async_copy(blocks[j], outs[k], sems.at[j]).start()

    for j in range(n):
        pltpu.make_async_copy(blocks[j], outs[0], sems.at[j]).wait()


def arrange(to, blocks, order, name):
    n = len(blocks)
    return pl.pallas_call(
        functools.partial(arrange_body, n),
        grid=(1,),
        in_specs=[pl.BlockSpec(memory_space=pltpu.SMEM)] + [ANY] * (n + len(order)),
        out_specs=each(blocks),
        out_shape=[jax.ShapeDtypeStruct(x.shape, BF16) for x in blocks],
        scratch_shapes=[pltpu.SemaphoreType.DMA((n,))],
        compiler_params=params(),
        cost_estimate=SMALL,
        name=name,
    )(to, *blocks, *order)


def grads_body(n, last, offs_ref, *refs):
    blocks, (w_ref, *rest) = refs[:n], refs[n:]
    width = blocks[0].shape[1]
    piece = refs[-1]

    @pl.when(pl.program_id(0) == 0)
    def _():
        for j in range(n):
            piece[:, j * width : (j + 1) * width] = blocks[j][...]

    weight = jnp.concatenate(
        [w_ref[:, pl.ds(pl.multiple_of(offs_ref[j], 128), width)] for j in range(n)], axis=1
    )
    total = dot_nt(piece[...], weight)
    if last:
        sum_ref, by_gate_ref, by_up_ref = rest[:3]
        gg_ref, gu_ref, done_ref = refs[-4:-1]
        total += sum_ref[...]
        gg_ref[...] = (total * by_gate_ref[...]).astype(BF16)
        gu_ref[...] = (total * by_up_ref[...]).astype(BF16)
        done_ref[...] = jnp.zeros_like(done_ref)
    else:
        refs[-2][...] = total


def grads(offs, blocks, weight, more, order, name):
    n = len(blocks)
    last = len(more) > 0
    toks, width = blocks[0].shape
    units, feats = weight.shape
    cols = pl.BlockSpec((toks, TILE), lambda i, _: (0, i))
    out = jax.ShapeDtypeStruct((toks, units), BF16)
    if last:
        out_specs = [cols, cols, whole((8, 128))]
        out_shape = [out, out, jax.ShapeDtypeStruct((8, 128), F32)]
    else:
        out_specs, out_shape = cols, jax.ShapeDtypeStruct((toks, units), F32)
    return pl.pallas_call(
        functools.partial(grads_body, n, last),
        grid_spec=pltpu.PrefetchScalarGridSpec(
            num_scalar_prefetch=1,
            grid=(units // TILE,),
            in_specs=[whole((toks, width))] * n
            + [pl.BlockSpec((TILE, feats), lambda i, _: (i, 0))]
            + [cols] * len(more)
            + [ANY] * len(order),
            out_specs=out_specs,
            scratch_shapes=[pltpu.VMEM((toks, n * width), BF16)],
        ),
        out_shape=out_shape,
        compiler_params=params(),
        cost_estimate=pl.CostEstimate(
            flops=2 * toks * units * n * width,
            bytes_accessed=2 * (units * feats + toks * n * width + 4 * toks * units),
            transcendentals=0,
        ),
        name=name,
    )(offs, *blocks, weight, *more, *order)


def wgrad_body(n, starts, offs_ref, toks_ref, own_ref, *refs):
    steps = len(starts) - 1
    others, hids = refs[:n], refs[n : (1 + steps) * n]
    out_ref, done_ref, hid, cols, outs, hid_sems, col_sems, out_sems = refs[-8:]
    done_ref[...] = jnp.zeros_like(done_ref)
    _, toks, width = own_ref.shape
    own, other = (pl.ds(pl.multiple_of(offs_ref[half], 128), width) for half in range(2))
    came = []
    for k in range(n):
        rows = pl.ds(pl.multiple_of(toks_ref[k], 128), toks)
        came.append((own_ref.at[k], cols.at[k * toks : (k + 1) * toks, own]))
        came.append((others[k], cols.at[rows, other]))
    came = [pltpu.make_async_copy(a, b, col_sems.at[j]) for j, (a, b) in enumerate(came)]
    units = []
    for i in range(steps):
        part = slice(starts[i], starts[i + 1])
        for k in range(n):
            place = pl.ds(pl.multiple_of(toks_ref[k], 128), toks)
            copy = (hids[i * n + k], hid.at[part, place], hid_sems.at[i * n + k])
            units.append(pltpu.make_async_copy(*copy))
    for copy in [*units[:n], *came, *units[n:]]:
        copy.start()
    for copy in came:
        copy.wait()
    gone = []
    for i in range(steps):
        for copy in units[i * n : (i + 1) * n]:
            copy.wait()
        part = slice(starts[i], starts[i + 1])
        outs[part] = lax.dot_general(
            hid[part], cols[...], (((1,), (0,)), ((), ())), preferred_element_type=F32
        ).astype(BF16)
        gone.append(pltpu.make_async_copy(outs.at[part], out_ref.at[part], out_sems.at[i]))
        gone[-1].start()
    for copy in gone:
        copy.wait()


def wgrad(offs, tok_offs, own, others, hids, order):
    n, toks, width = own.shape
    total = n * toks
    starts = [0]
    for part in hids:
        starts.append(starts[-1] + part[0].shape[0])
    units = starts[-1]
    operands = [offs, tok_offs, own, *others, *(x for part in hids for x in part), *order]
    return pl.pallas_call(
        functools.partial(wgrad_body, n, tuple(starts)),
        in_specs=[pl.BlockSpec(memory_space=pltpu.SMEM)] * 2 + [ANY] * (len(operands) - 2),
        out_specs=[ANY, pl.BlockSpec(memory_space=pltpu.VMEM)],
        out_shape=[
            jax.ShapeDtypeStruct((units, 2 * width), BF16),
            jax.ShapeDtypeStruct((8, 128), F32),
        ],
        scratch_shapes=[
            pltpu.VMEM((units, total), BF16),
            pltpu.VMEM((total, 2 * width), BF16),
            pltpu.VMEM((units, 2 * width), BF16),
            pltpu.SemaphoreType.DMA((len(hids) * n,)),
            pltpu.SemaphoreType.DMA((2 * n,)),
            pltpu.SemaphoreType.DMA((len(hids),)),
        ],
        compiler_params=params(),
        cost_estimate=pl.CostEstimate(
            flops=4 * total * units * width,
            bytes_accessed=2 * (total * (units + 2 * width) + 2 * units * width),
            transcendentals=0,
        ),
        name="wgrad",
    )(*operands)


def put_slices(inner_ref, part, kept_ref, away_refs):
    outer, size, total = kept_ref.shape
    cut = total // len(away_refs)
    for inner in range(2):

        @pl.when(inner_ref[0] == inner)
        def _():
            for p in range(2 * outer):
                rows = part[p * size : (p + 1) * size]
                if p % 2 == inner:
                    kept_ref[p // 2] = rows
                else:
                    for h, away_ref in enumerate(away_refs):
                        away_ref[p // 2] = rows[:, h * cut : (h + 1) * cut]


def grad_gram_body(n, cuts, inner_ref, offs_ref, *refs):
    toks_refs, val_ref, (kept_ref, *away_refs, wide) = refs[:n], refs[n], refs[-2 - cuts :]
    for k, ref in enumerate(toks_refs):
        toks = ref.shape[0]
        wide[:, pl.ds(pl.multiple_of(offs_ref[k], 128), toks)] = dot_nt(val_ref[...], ref[...])
    put_slices(inner_ref, wide, kept_ref, away_refs)


def hidden_gram_body(n, cuts, inner_ref, offs_ref, *refs):
    hid, val_ref, (kept_ref, *away_refs, wide) = refs[:n], refs[n], refs[-2 - cuts :]
    dp_count = offs_ref.shape[0]
    for k in range(dp_count):
        start, total = 0, None
        for ref in hid[k::dp_count]:
            count, toks = ref.shape
            term = lax.dot_general(
                val_ref[:, start : start + count], ref[...], (((1,), (0,)), ((), ())),
                preferred_element_type=F32,
            )
            start, total = start + count, term if total is None else total + term
        wide[:, pl.ds(pl.multiple_of(offs_ref[k], 128), toks)] = total
    put_slices(inner_ref, wide, kept_ref, away_refs)


def gram(body, inner, offs, operands, order, parts, cuts, name):
    smem = pl.BlockSpec(memory_space=pltpu.SMEM)
    *toks, vals = operands
    total = sum(x.size for x in toks) // vals.shape[1]
    kept = jax.ShapeDtypeStruct((parts // 2, vals.shape[0] // parts, total), F32)
    away = jax.ShapeDtypeStruct((parts // 2, vals.shape[0] // parts, total // cuts), F32)
    shapes = [kept] + [away] * cuts
    kept, *away = pl.pallas_call(
        functools.partial(body, len(toks), cuts),
        grid=(1,),
        in_specs=[smem, smem] + each(operands) + [ANY] * len(order),
        out_specs=each(shapes),
        out_shape=shapes,
        scratch_shapes=[pltpu.VMEM((vals.shape[0], total), F32)],
        compiler_params=params(),
        cost_estimate=SMALL,
        name=name,
    )(inner, offs, *operands, *order)
    return kept, away, [swap(x, "fsdp", 1) for x in away]


def pair_body(cuts, kept_ref, *refs):
    came_refs, out_ref = refs[:cuts], refs[-1]
    cut = kept_ref.shape[2] // cuts
    for h in range(cuts):
        cols = slice(h * cut, (h + 1) * cut)
        out_ref[:, :, cols] = kept_ref[:, :, cols] + came_refs[h][...]


def pair_sum(kept, came, order, name):
    return pl.pallas_call(
        functools.partial(pair_body, len(came)),
        grid=(1,),
        in_specs=each([kept, *came]) + [ANY] * len(order),
        out_specs=whole(kept.shape),
        out_shape=jax.ShapeDtypeStruct(kept.shape, F32),
        compiler_params=params(),
        cost_estimate=SMALL,
        name=name,
    )(kept, *came, *order)


def spread(pair):
    n_fs = lax.axis_size("fsdp")
    groups = [list(range(x, n_fs, 2)) for x in range(2)]
    return lax.all_to_all(
        pair, "fsdp", split_axis=0, concat_axis=0, axis_index_groups=groups, tiled=True
    )


def line_body(rows, assign_ref, hid_ref, grad_ref, *refs):
    out_ref = refs[-1]
    n = hid_ref.shape[0]
    hid_sum = sum(hid_ref[j] for j in range(n))
    grad_sum = sum(grad_ref[j] for j in range(n))
    by_tok = jnp.sum(hid_sum * grad_sum, axis=0, keepdims=True)
    size = by_tok.shape[1] // rows
    lane = lax.broadcasted_iota(jnp.int32, (1, 128), 1)
    line = jnp.zeros((1, 128), F32)
    for r in range(rows):
        row = jnp.sum(by_tok[:, r * size : (r + 1) * size], axis=1, keepdims=True)
        line = jnp.where(lane == r, row, line)
    for r in range(assign_ref.shape[0]):
        line = jnp.where(lane == rows + r, assign_ref[r].astype(F32), line)
    out_ref[...] = jnp.broadcast_to(line, out_ref.shape)


def score_line(assign, hid, grad, order, rows, copies):
    return pl.pallas_call(
        functools.partial(line_body, rows),
        grid=(1,),
        in_specs=[pl.BlockSpec(memory_space=pltpu.SMEM)] + each([hid, grad]) + [ANY] * len(order),
        out_specs=whole((copies, 128)),
        out_shape=jax.ShapeDtypeStruct((copies, 128), F32),
        compiler_params=params(),
        cost_estimate=SMALL,
        name="score_line",
    )(assign, hid, grad, *order)


def per_device(gate_act, up_act, out_grad, down_weight, val_hidden, val_grad, assign):
    n_dp = lax.axis_size("dp")
    n_fs = lax.axis_size("fsdp")
    d = lax.axis_index("dp")
    f = lax.axis_index("fsdp")
    rows_here = assign.shape[0]
    toks, width = out_grad.shape
    units = gate_act.shape[1]
    total = n_dp * toks
    n_out = n_fs // 2
    outer, inner = f // 2, f % 2

    at = (outer - jnp.arange(n_out, dtype=jnp.int32)) % n_out
    tok_offs = (d ^ jnp.arange(n_dp, dtype=jnp.int32)) * toks
    inner_at = inner.reshape(1).astype(jnp.int32)
    to = at ^ d

    def over_dp(x):
        far = swap(x, "dp", 2)
        return [x, swap(x, "dp", 1), far, None]

    tiles = units // TILE
    cuts = [0, tiles // 3, tiles - tiles // 3, tiles]
    hids = [
        over_dp(hidden_units(gate_act, up_act, a, b - a, f"hidden_{a}"))
        for a, b in zip(cuts, cuts[1:])
    ]

    ring, others = [out_grad], [swap(out_grad, "fsdp", 1)]
    for step in range(2):
        came = shift(ring[-1], "fsdp", 2)
        ring.append(after(came, others[-1], hids[step][2]))
        others.append(swap(ring[-1], "fsdp", 1))
    for part in hids:
        part[3] = swap(part[2], "dp", 1)

    offs = (jnp.stack([inner, 1 - inner]) * width).astype(jnp.int32)
    places = (offs[None, :] + at[:, None] * (2 * width)).reshape(-1)
    by_gate, by_up = factors(gate_act, up_act, ring[1])
    blocks = [x for pair in zip(ring, others) for x in pair]
    half_sum = grads(places[:4], blocks[:4], down_weight, [], [ring[2], by_up], "grads_first")
    ring.append(after(shift(ring[2], "fsdp", 2), others[2], hids[2][2], half_sum))
    others.append(shift(others[2], "fsdp", 2))

    hid_kept, away, hid_came = gram(
        hidden_gram_body, inner_at, tok_offs, [*(x for part in hids for x in part), val_hidden],
        [half_sum], n_fs, 1, "hidden_gram",
    )
    far = swap(out_grad, "dp", 2)
    own = stack(at, ring, [*away, far], "own_features")
    own_cols = lax.all_to_all(own, "dp", split_axis=0, concat_axis=0, tiled=True)

    grad_dp = [out_grad, swap(out_grad, "dp", 1), far, swap(far, "dp", 1)]
    grad_kept, away, grad_came = gram(
        grad_gram_body, inner_at, tok_offs, [*grad_dp, val_grad], [own], n_fs, 1, "grad_gram"
    )
    hid_pair = pair_sum(hid_kept, hid_came, [*away, others[3]], "hidden_pair")
    hid_sums = spread(hid_pair)
    other = arrange(to, others, [hid_pair], "other_features")
    other_cols = [x if k == 0 else swap(x, "dp", k) for k, x in enumerate(other)]
    grad_gate, grad_up, done = grads(
        places[4:], [ring[2], others[2], ring[3], others[3]], down_weight,
        [half_sum, by_gate, by_up], [other[0]], "grads_last",
    )
    grad_pair = pair_sum(grad_kept, grad_came, [done, *other_cols[1:3]], "grad_pair")
    grad_sums = spread(grad_pair)
    weight_grad, done = wgrad(offs, tok_offs, own_cols, other_cols, hids, [grad_pair])

    mine = score_line(assign, hid_sums, grad_sums, [done], n_dp * rows_here, n_dp * n_fs)
    every = lax.all_to_all(
        mine, ("dp", "fsdp"), split_axis=0, concat_axis=0, tiled=True
    ).reshape(n_dp, n_fs, 128)

    rows = n_dp * rows_here
    scale = 1.0 / jnp.sqrt(F32(L) * VAL * FFW * D)
    scores = jnp.sum(every[:, :, :rows], axis=1) * scale
    groups = every[:, 0, rows : rows + rows_here].reshape(rows)
    onehot = (groups[None, :] == jnp.arange(n_dp, dtype=F32)[:, None]).astype(F32)
    group_values = jnp.sum(onehot * scores, axis=1)
    row_scores = lax.dynamic_slice_in_dim(scores, d * rows_here, rows_here, axis=1).T
    return (grad_gate, grad_up, weight_grad, row_scores, group_values)


def per_device_any(gate_act, up_act, out_grad, down_weight, val_hidden, val_grad, assign):
    n_dp = lax.axis_size("dp")
    me = lax.axis_index("dp")
    rows_here = assign.shape[0]
    toks = gate_act.shape[0]
    gate = gate_act.astype(F32)
    up = up_act.astype(F32)
    sig = jax.nn.sigmoid(gate)
    act = gate * sig
    hidden = (act * up).astype(BF16)
    grad_feat = lax.all_gather(out_grad, "dp", axis=0, tiled=True)
    piece = lax.all_gather(out_grad, "fsdp", axis=1, tiled=True)
    hidden_all = lax.all_gather(hidden, "dp", axis=0, tiled=True)
    grad_gram = lax.psum(dot_nt(grad_feat, val_grad), "fsdp")
    grad_cols = lax.all_to_all(piece, "dp", split_axis=1, concat_axis=0, tiled=True)
    grad_hidden = dot_nt(piece, down_weight)
    grad_gate = (grad_hidden * up * sig * (1.0 + gate * (1.0 - sig))).astype(BF16)
    grad_up = (grad_hidden * act).astype(BF16)
    product = dot_nt(hidden_all, val_hidden) * grad_gram
    part = jnp.sum(product.reshape(n_dp * rows_here, toks // rows_here * VAL), axis=1)
    weight_grad = dot_tn(hidden_all, grad_cols).astype(BF16)
    scale = 1.0 / jnp.sqrt(F32(L) * VAL * FFW * D)
    scores = lax.all_gather(lax.psum(part, "fsdp"), "dp") * scale
    groups = lax.all_gather(assign, "dp", tiled=True)
    onehot = (groups[None, :] == jnp.arange(n_dp, dtype=jnp.int32)[:, None]).astype(F32)
    group_values = jnp.sum(onehot * scores, axis=1)
    row_scores = lax.dynamic_slice_in_dim(scores, me * rows_here, rows_here, axis=1).T
    return (grad_gate, grad_up, weight_grad, row_scores, group_values)


def solution(mesh):
    in_specs = (
        P("dp", "fsdp"),
        P("dp", "fsdp"),
        P("dp", "fsdp"),
        P("fsdp", None),
        P("dp", "fsdp"),
        P("dp", "fsdp"),
        P("dp"),
    )
    out_specs = (P("dp", "fsdp"), P("dp", "fsdp"), P("fsdp", "dp"), P("dp", None), P())
    n_dp, n_fs = mesh.shape["dp"], mesh.shape["fsdp"]
    fits = n_dp == 4 and n_fs == 2 * n_dp
    return jax.shard_map(
        per_device if fits else per_device_any,
        mesh=mesh, in_specs=in_specs, out_specs=out_specs, check_vma=False,
    )
```

```python
import functools

import jax
import jax.numpy as jnp
from jax import lax
from jax.experimental import pallas as pl
from jax.experimental.pallas import tpu as pltpu
from jax.sharding import PartitionSpec as P

D = 5120
FFW = 14336
L = 128
VAL = 256

F32 = jnp.float32
BF16 = jnp.bfloat16
TILE = 256
VMEM_LIMIT = 63 * 1024 * 1024


def dot_nt(a, b):
    return lax.dot_general(a, b, (((1,), (1,)), ((), ())), preferred_element_type=F32)


def dot_tn(a, b):
    return lax.dot_general(a, b, (((0,), (0,)), ((), ())), preferred_element_type=F32)


def swap(x, axis, k):
    n = lax.axis_size(axis)
    return lax.ppermute(x, axis, [(s, s ^ k) for s in range(n)])


def shift(x, axis, k):
    n = lax.axis_size(axis)
    return lax.ppermute(x, axis, [(s, (s + k) % n) for s in range(n)])


def whole(shape):
    return pl.BlockSpec(shape, lambda *_: (0,) * len(shape))


def each(arrays):
    return [whole(x.shape) for x in arrays]


ANY = pl.BlockSpec(memory_space=pl.ANY)
HBM = pl.BlockSpec(memory_space=pltpu.HBM)
SMALL = pl.CostEstimate(flops=1024, bytes_accessed=1024, transcendentals=0)


def params():
    return pltpu.CompilerParams(vmem_limit_bytes=VMEM_LIMIT)


def after_body(*refs):
    pass


def after(x, *order):
    return pl.pallas_call(
        after_body,
        in_specs=[ANY] * (1 + len(order)),
        out_specs=ANY,
        out_shape=jax.ShapeDtypeStruct(x.shape, x.dtype),
        input_output_aliases={0: 0},
        compiler_params=params(),
        cost_estimate=SMALL,
        name="after",
    )(x, *order)


def hidden_body(gate_ref, up_ref, hid_ref):
    gate = gate_ref[...].astype(F32)
    hid_ref[...] = (gate * jax.nn.sigmoid(gate) * up_ref[...].astype(F32)).astype(BF16).T


def hidden_units(gate, up, first, count, name):
    toks = gate.shape[0]
    cols = pl.BlockSpec((toks, TILE), lambda i: (0, first + i))
    return pl.pallas_call(
        hidden_body,
        grid=(count,),
        in_specs=[cols, cols],
        out_specs=pl.BlockSpec((TILE, toks), lambda i: (i, 0)),
        out_shape=jax.ShapeDtypeStruct((count * TILE, toks), BF16),
        compiler_params=params(),
        cost_estimate=SMALL,
        name=name,
    )(gate, up)


def stack_body(n, at_ref, *refs):
    blocks, out_ref, sems = refs[:n], refs[-2], refs[-1]
    copies = [
        pltpu.make_async_copy(blocks[j], out_ref.at[at_ref[j]], sems.at[j]) for j in range(n)
    ]
    for copy in copies:
        copy.start()
    for copy in copies:
        copy.wait()


def stack(at, blocks, order, name):
    n = len(blocks)
    shape = (n,) + blocks[0].shape
    return pl.pallas_call(
        functools.partial(stack_body, n),
        grid=(1,),
        in_specs=[pl.BlockSpec(memory_space=pltpu.SMEM)] + [ANY] * (n + len(order)),
        out_specs=whole(shape),
        out_shape=jax.ShapeDtypeStruct(shape, BF16),
        scratch_shapes=[pltpu.SemaphoreType.DMA((n,))],
        compiler_params=params(),
        cost_estimate=SMALL,
        name=name,
    )(at, *blocks, *order)


def arrange_body(n, to_ref, *refs):
    blocks, outs, sems = refs[:n], refs[-n - 1 : -1], refs[-1]
    for j in range(n):
        for k in range(n):

            @pl.when(to_ref[j] == k)
            def _():
                pltpu.make_async_copy(blocks[j], outs[k], sems.at[j]).start()

    for j in range(n):
        pltpu.make_async_copy(blocks[j], outs[0], sems.at[j]).wait()


def arrange(to, blocks, order, name):
    n = len(blocks)
    return pl.pallas_call(
        functools.partial(arrange_body, n),
        grid=(1,),
        in_specs=[pl.BlockSpec(memory_space=pltpu.SMEM)] + [ANY] * (n + len(order)),
        out_specs=each(blocks),
        out_shape=[jax.ShapeDtypeStruct(x.shape, BF16) for x in blocks],
        scratch_shapes=[pltpu.SemaphoreType.DMA((n,))],
        compiler_params=params(),
        cost_estimate=SMALL,
        name=name,
    )(to, *blocks, *order)


def grads_body(n, offs_ref, *refs):
    blocks, (w_ref, gate_ref, up_ref), (gg_ref, gu_ref, done_ref, piece) = (
        refs[:n], refs[n : n + 3], refs[-4:]
    )
    width = blocks[0].shape[1]

    @pl.when(pl.program_id(0) == 0)
    def _():
        for j in range(n):
            piece[:, pl.ds(pl.multiple_of(offs_ref[j], 128), width)] = blocks[j][...]
        done_ref[...] = jnp.zeros_like(done_ref)

    total = dot_nt(piece[...], w_ref[...])
    gate = gate_ref[...].astype(F32)
    up = up_ref[...].astype(F32)
    sig = jax.nn.sigmoid(gate)
    gg_ref[...] = (total * up * sig * (1.0 + gate * (1.0 - sig))).astype(BF16)
    gu_ref[...] = (total * (gate * sig)).astype(BF16)


def grads(offs, blocks, weight, gate, up, order):
    n = len(blocks)
    toks, width = blocks[0].shape
    units, feats = weight.shape
    cols = pl.BlockSpec((toks, TILE), lambda i, _: (0, i))
    out = jax.ShapeDtypeStruct((toks, units), BF16)
    return pl.pallas_call(
        functools.partial(grads_body, n),
        grid_spec=pltpu.PrefetchScalarGridSpec(
            num_scalar_prefetch=1,
            grid=(units // TILE,),
            in_specs=[whole((toks, width))] * n
            + [pl.BlockSpec((TILE, feats), lambda i, _: (i, 0)), cols, cols]
            + [ANY] * len(order),
            out_specs=[cols, cols, whole((8, 128))],
            scratch_shapes=[pltpu.VMEM((toks, feats), BF16)],
        ),
        out_shape=(out, out, jax.ShapeDtypeStruct((8, 128), F32)),
        compiler_params=params(),
        cost_estimate=pl.CostEstimate(
            flops=2 * toks * units * feats,
            bytes_accessed=2 * (units * feats + toks * feats + 4 * toks * units),
            transcendentals=toks * units,
        ),
        name="grads",
    )(offs, *blocks, weight, gate, up, *order)


def wgrad_body(n, starts, offs_ref, toks_ref, own_ref, *refs):
    steps = len(starts) - 1
    others, hids = refs[:n], refs[n : (1 + steps) * n]
    out_ref, done_ref, hid, cols, outs, hid_sems, col_sems, out_sems = refs[-8:]
    done_ref[...] = jnp.zeros_like(done_ref)
    _, toks, width = own_ref.shape
    own, other = (pl.ds(pl.multiple_of(offs_ref[half], 128), width) for half in range(2))
    came = []
    for k in range(n):
        rows = pl.ds(pl.multiple_of(toks_ref[k], 128), toks)
        came.append((own_ref.at[k], cols.at[k * toks : (k + 1) * toks, own]))
        came.append((others[k], cols.at[rows, other]))
    came = [pltpu.make_async_copy(a, b, col_sems.at[j]) for j, (a, b) in enumerate(came)]
    units = []
    for i in range(steps):
        part = slice(starts[i], starts[i + 1])
        for k in range(n):
            place = pl.ds(pl.multiple_of(toks_ref[k], 128), toks)
            copy = (hids[i * n + k], hid.at[part, place], hid_sems.at[i * n + k])
            units.append(pltpu.make_async_copy(*copy))
    for copy in [*units[:n], *came, *units[n:]]:
        copy.start()
    for copy in came:
        copy.wait()
    gone = []
    for i in range(steps):
        for copy in units[i * n : (i + 1) * n]:
            copy.wait()
        part = slice(starts[i], starts[i + 1])
        outs[part] = lax.dot_general(
            hid[part], cols[...], (((1,), (0,)), ((), ())), preferred_element_type=F32
        ).astype(BF16)
        gone.append(pltpu.make_async_copy(outs.at[part], out_ref.at[part], out_sems.at[i]))
        gone[-1].start()
    for copy in gone:
        copy.wait()


def wgrad(offs, tok_offs, own, others, hids, order):
    n, toks, width = own.shape
    total = n * toks
    starts = [0]
    for part in hids:
        starts.append(starts[-1] + part[0].shape[0])
    units = starts[-1]
    operands = [offs, tok_offs, own, *others, *(x for part in hids for x in part), *order]
    return pl.pallas_call(
        functools.partial(wgrad_body, n, tuple(starts)),
        in_specs=[pl.BlockSpec(memory_space=pltpu.SMEM)] * 2 + [ANY] * (len(operands) - 2),
        out_specs=[ANY, pl.BlockSpec(memory_space=pltpu.VMEM)],
        out_shape=[
            jax.ShapeDtypeStruct((units, 2 * width), BF16),
            jax.ShapeDtypeStruct((8, 128), F32),
        ],
        scratch_shapes=[
            pltpu.VMEM((units, total), BF16),
            pltpu.VMEM((total, 2 * width), BF16),
            pltpu.VMEM((units, 2 * width), BF16),
            pltpu.SemaphoreType.DMA((len(hids) * n,)),
            pltpu.SemaphoreType.DMA((2 * n,)),
            pltpu.SemaphoreType.DMA((len(hids),)),
        ],
        compiler_params=params(),
        cost_estimate=pl.CostEstimate(
            flops=4 * total * units * width,
            bytes_accessed=2 * (total * (units + 2 * width) + 2 * units * width),
            transcendentals=0,
        ),
        name="wgrad",
    )(*operands)


def put_slices(inner_ref, part, kept_ref, away_refs):
    outer, size, total = kept_ref.shape
    cut = total // len(away_refs)
    for inner in range(2):

        @pl.when(inner_ref[0] == inner)
        def _():
            for p in range(2 * outer):
                rows = part[p * size : (p + 1) * size]
                if p % 2 == inner:
                    kept_ref[p // 2] = rows
                else:
                    for h, away_ref in enumerate(away_refs):
                        away_ref[p // 2] = rows[:, h * cut : (h + 1) * cut]


def grad_gram_body(n, cuts, inner_ref, offs_ref, *refs):
    toks_refs, val_ref, (kept_ref, *away_refs, wide) = refs[:n], refs[n], refs[-2 - cuts :]
    for k, ref in enumerate(toks_refs):
        toks = ref.shape[0]
        wide[:, pl.ds(pl.multiple_of(offs_ref[k], 128), toks)] = dot_nt(val_ref[...], ref[...])
    put_slices(inner_ref, wide, kept_ref, away_refs)


def hidden_gram_body(n, cuts, inner_ref, offs_ref, *refs):
    hid, val_ref, (kept_ref, *away_refs, wide) = refs[:n], refs[n], refs[-2 - cuts :]
    dp_count = offs_ref.shape[0]
    for k in range(dp_count):
        start, total = 0, None
        for ref in hid[k::dp_count]:
            count, toks = ref.shape
            term = lax.dot_general(
                val_ref[:, start : start + count], ref[...], (((1,), (0,)), ((), ())),
                preferred_element_type=F32,
            )
            start, total = start + count, term if total is None else total + term
        wide[:, pl.ds(pl.multiple_of(offs_ref[k], 128), toks)] = total
    put_slices(inner_ref, wide, kept_ref, away_refs)


def gram(body, inner, offs, operands, order, parts, cuts, name):
    smem = pl.BlockSpec(memory_space=pltpu.SMEM)
    *toks, vals = operands
    total = sum(x.size for x in toks) // vals.shape[1]
    kept = jax.ShapeDtypeStruct((parts // 2, vals.shape[0] // parts, total), F32)
    away = jax.ShapeDtypeStruct((parts // 2, vals.shape[0] // parts, total // cuts), F32)
    shapes = [kept] + [away] * cuts
    kept, *away = pl.pallas_call(
        functools.partial(body, len(toks), cuts),
        grid=(1,),
        in_specs=[smem, smem] + each(operands) + [ANY] * len(order),
        out_specs=each(shapes),
        out_shape=shapes,
        scratch_shapes=[pltpu.VMEM((vals.shape[0], total), F32)],
        compiler_params=params(),
        cost_estimate=SMALL,
        name=name,
    )(inner, offs, *operands, *order)
    return kept, away, [swap(x, "fsdp", 1) for x in away]


def pair_body(cuts, kept_ref, *refs):
    came_refs, out_ref = refs[:cuts], refs[-1]
    cut = kept_ref.shape[2] // cuts
    for h in range(cuts):
        cols = slice(h * cut, (h + 1) * cut)
        out_ref[:, :, cols] = kept_ref[:, :, cols] + came_refs[h][...]


def pair_sum(kept, came, order, name):
    return pl.pallas_call(
        functools.partial(pair_body, len(came)),
        grid=(1,),
        in_specs=each([kept, *came]) + [ANY] * len(order),
        out_specs=whole(kept.shape),
        out_shape=jax.ShapeDtypeStruct(kept.shape, F32),
        compiler_params=params(),
        cost_estimate=SMALL,
        name=name,
    )(kept, *came, *order)


def spread(pair):
    n_fs = lax.axis_size("fsdp")
    groups = [list(range(x, n_fs, 2)) for x in range(2)]
    return lax.all_to_all(
        pair, "fsdp", split_axis=0, concat_axis=0, axis_index_groups=groups, tiled=True
    )


def line_body(rows, assign_ref, hid_ref, grad_ref, *refs):
    out_ref = refs[-1]
    n = hid_ref.shape[0]
    hid_sum = sum(hid_ref[j] for j in range(n))
    grad_sum = sum(grad_ref[j] for j in range(n))
    by_tok = jnp.sum(hid_sum * grad_sum, axis=0, keepdims=True)
    size = by_tok.shape[1] // rows
    lane = lax.broadcasted_iota(jnp.int32, (1, 128), 1)
    line = jnp.zeros((1, 128), F32)
    for r in range(rows):
        row = jnp.sum(by_tok[:, r * size : (r + 1) * size], axis=1, keepdims=True)
        line = jnp.where(lane == r, row, line)
    for r in range(assign_ref.shape[0]):
        line = jnp.where(lane == rows + r, assign_ref[r].astype(F32), line)
    out_ref[...] = jnp.broadcast_to(line, out_ref.shape)


def score_line(assign, hid, grad, order, rows, copies):
    return pl.pallas_call(
        functools.partial(line_body, rows),
        grid=(1,),
        in_specs=[pl.BlockSpec(memory_space=pltpu.SMEM)] + each([hid, grad]) + [ANY] * len(order),
        out_specs=whole((copies, 128)),
        out_shape=jax.ShapeDtypeStruct((copies, 128), F32),
        compiler_params=params(),
        cost_estimate=SMALL,
        name="score_line",
    )(assign, hid, grad, *order)


def per_device(gate_act, up_act, out_grad, down_weight, val_hidden, val_grad, assign):
    n_dp = lax.axis_size("dp")
    n_fs = lax.axis_size("fsdp")
    d = lax.axis_index("dp")
    f = lax.axis_index("fsdp")
    rows_here = assign.shape[0]
    toks, width = out_grad.shape
    units = gate_act.shape[1]
    total = n_dp * toks
    n_out = n_fs // 2
    outer, inner = f // 2, f % 2

    at = (outer - jnp.arange(n_out, dtype=jnp.int32)) % n_out
    tok_offs = (d ^ jnp.arange(n_dp, dtype=jnp.int32)) * toks
    inner_at = inner.reshape(1).astype(jnp.int32)
    to = at ^ d

    def over_dp(x):
        far = swap(x, "dp", 2)
        return [x, swap(x, "dp", 1), far, None]

    tiles = units // TILE
    cuts = [0, tiles // 3, tiles - tiles // 3, tiles]
    hids = [
        over_dp(hidden_units(gate_act, up_act, a, b - a, f"hidden_{a}"))
        for a, b in zip(cuts, cuts[1:])
    ]

    ring, others = [out_grad], [swap(out_grad, "fsdp", 1)]
    for step in range(2):
        came = shift(ring[-1], "fsdp", 2)
        ring.append(after(came, others[-1], hids[step][2]))
        others.append(swap(ring[-1], "fsdp", 1))
    for part in hids:
        part[3] = swap(part[2], "dp", 1)
    hid_kept, away, hid_came = gram(
        hidden_gram_body, inner_at, tok_offs, [*(x for part in hids for x in part), val_hidden],
        [ring[2]], n_fs, 1, "hidden_gram",
    )
    ring.append(after(shift(ring[2], "fsdp", 2), others[2], *away))
    others.append(shift(others[2], "fsdp", 2))

    far = swap(out_grad, "dp", 2)
    own = stack(at, ring, [far], "own_features")
    own_cols = lax.all_to_all(own, "dp", split_axis=0, concat_axis=0, tiled=True)

    grad_dp = [out_grad, swap(out_grad, "dp", 1), far, swap(far, "dp", 1)]
    grad_kept, away, grad_came = gram(
        grad_gram_body, inner_at, tok_offs, [*grad_dp, val_grad], [own], n_fs, 1, "grad_gram"
    )
    other = arrange(to, others, away, "other_features")
    other_cols = [x if k == 0 else swap(x, "dp", k) for k, x in enumerate(other)]
    hid_pair = pair_sum(hid_kept, hid_came, [other[0]], "hidden_pair")
    hid_sums = spread(hid_pair)
    offs = (jnp.stack([inner, 1 - inner]) * width).astype(jnp.int32)
    places = (offs[:, None] + at[None, :] * (2 * width)).reshape(-1)
    grad_gate, grad_up, done = grads(
        places, [*ring, *others], down_weight, gate_act, up_act, [hid_pair]
    )
    grad_pair = pair_sum(grad_kept, grad_came, [done, *other_cols[1:]], "grad_pair")
    grad_sums = spread(grad_pair)
    weight_grad, done = wgrad(offs, tok_offs, own_cols, other_cols, hids, [grad_pair])

    mine = score_line(assign, hid_sums, grad_sums, [done], n_dp * rows_here, n_dp * n_fs)
    every = lax.all_to_all(
        mine, ("dp", "fsdp"), split_axis=0, concat_axis=0, tiled=True
    ).reshape(n_dp, n_fs, 128)

    rows = n_dp * rows_here
    scale = 1.0 / jnp.sqrt(F32(L) * VAL * FFW * D)
    scores = jnp.sum(every[:, :, :rows], axis=1) * scale
    groups = every[:, 0, rows : rows + rows_here].reshape(rows)
    onehot = (groups[None, :] == jnp.arange(n_dp, dtype=F32)[:, None]).astype(F32)
    group_values = jnp.sum(onehot * scores, axis=1)
    row_scores = lax.dynamic_slice_in_dim(scores, d * rows_here, rows_here, axis=1).T
    return (grad_gate, grad_up, weight_grad, row_scores, group_values)


def per_device_any(gate_act, up_act, out_grad, down_weight, val_hidden, val_grad, assign):
    n_dp = lax.axis_size("dp")
    me = lax.axis_index("dp")
    rows_here = assign.shape[0]
    toks = gate_act.shape[0]
    gate = gate_act.astype(F32)
    up = up_act.astype(F32)
    sig = jax.nn.sigmoid(gate)
    act = gate * sig
    hidden = (act * up).astype(BF16)
    grad_feat = lax.all_gather(out_grad, "dp", axis=0, tiled=True)
    piece = lax.all_gather(out_grad, "fsdp", axis=1, tiled=True)
    hidden_all = lax.all_gather(hidden, "dp", axis=0, tiled=True)
    grad_gram = lax.psum(dot_nt(grad_feat, val_grad), "fsdp")
    grad_cols = lax.all_to_all(piece, "dp", split_axis=1, concat_axis=0, tiled=True)
    grad_hidden = dot_nt(piece, down_weight)
    grad_gate = (grad_hidden * up * sig * (1.0 + gate * (1.0 - sig))).astype(BF16)
    grad_up = (grad_hidden * act).astype(BF16)
    product = dot_nt(hidden_all, val_hidden) * grad_gram
    part = jnp.sum(product.reshape(n_dp * rows_here, toks // rows_here * VAL), axis=1)
    weight_grad = dot_tn(hidden_all, grad_cols).astype(BF16)
    scale = 1.0 / jnp.sqrt(F32(L) * VAL * FFW * D)
    scores = lax.all_gather(lax.psum(part, "fsdp"), "dp") * scale
    groups = lax.all_gather(assign, "dp", tiled=True)
    onehot = (groups[None, :] == jnp.arange(n_dp, dtype=jnp.int32)[:, None]).astype(F32)
    group_values = jnp.sum(onehot * scores, axis=1)
    row_scores = lax.dynamic_slice_in_dim(scores, me * rows_here, rows_here, axis=1).T
    return (grad_gate, grad_up, weight_grad, row_scores, group_values)


def solution(mesh):
    in_specs = (
        P("dp", "fsdp"),
        P("dp", "fsdp"),
        P("dp", "fsdp"),
        P("fsdp", None),
        P("dp", "fsdp"),
        P("dp", "fsdp"),
        P("dp"),
    )
    out_specs = (P("dp", "fsdp"), P("dp", "fsdp"), P("fsdp", "dp"), P("dp", None), P())
    n_dp, n_fs = mesh.shape["dp"], mesh.shape["fsdp"]
    fits = n_dp == 4 and n_fs == 2 * n_dp
    return jax.shard_map(
        per_device if fits else per_device_any,
        mesh=mesh, in_specs=in_specs, out_specs=out_specs, check_vma=False,
    )
```

```python
import functools

import jax
import jax.numpy as jnp
from jax import lax
from jax.experimental import pallas as pl
from jax.experimental.pallas import tpu as pltpu
from jax.sharding import PartitionSpec as P

D = 5120
FFW = 14336
L = 128
VAL = 256

F32 = jnp.float32
BF16 = jnp.bfloat16
TILE = 256
VMEM_LIMIT = 63 * 1024 * 1024


def dot_nt(a, b):
    return lax.dot_general(a, b, (((1,), (1,)), ((), ())), preferred_element_type=F32)


def dot_tn(a, b):
    return lax.dot_general(a, b, (((0,), (0,)), ((), ())), preferred_element_type=F32)


def swap(x, axis, k):
    n = lax.axis_size(axis)
    return lax.ppermute(x, axis, [(s, s ^ k) for s in range(n)])


def shift(x, axis, k):
    n = lax.axis_size(axis)
    return lax.ppermute(x, axis, [(s, (s + k) % n) for s in range(n)])


def whole(shape):
    return pl.BlockSpec(shape, lambda *_: (0,) * len(shape))


def each(arrays):
    return [whole(x.shape) for x in arrays]


ANY = pl.BlockSpec(memory_space=pl.ANY)
HBM = pl.BlockSpec(memory_space=pltpu.HBM)
SMALL = pl.CostEstimate(flops=1024, bytes_accessed=1024, transcendentals=0)


def params():
    return pltpu.CompilerParams(vmem_limit_bytes=VMEM_LIMIT)


def after_body(*refs):
    pass


def after(x, *order):
    return pl.pallas_call(
        after_body,
        in_specs=[ANY] * (1 + len(order)),
        out_specs=ANY,
        out_shape=jax.ShapeDtypeStruct(x.shape, x.dtype),
        input_output_aliases={0: 0},
        compiler_params=params(),
        cost_estimate=SMALL,
        name="after",
    )(x, *order)


def hidden_body(gate_ref, up_ref, hid_ref):
    gate = gate_ref[...].astype(F32)
    hid_ref[...] = (gate * jax.nn.sigmoid(gate) * up_ref[...].astype(F32)).astype(BF16).T


def hidden_units(gate, up, first, count, name):
    toks = gate.shape[0]
    cols = pl.BlockSpec((toks, TILE), lambda i: (0, first + i))
    return pl.pallas_call(
        hidden_body,
        grid=(count,),
        in_specs=[cols, cols],
        out_specs=pl.BlockSpec((TILE, toks), lambda i: (i, 0)),
        out_shape=jax.ShapeDtypeStruct((count * TILE, toks), BF16),
        compiler_params=params(),
        cost_estimate=SMALL,
        name=name,
    )(gate, up)


def stack_body(n, at_ref, *refs):
    blocks, out_ref, sems = refs[:n], refs[-2], refs[-1]
    copies = [
        pltpu.make_async_copy(blocks[j], out_ref.at[at_ref[j]], sems.at[j]) for j in range(n)
    ]
    for copy in copies:
        copy.start()
    for copy in copies:
        copy.wait()


def stack(at, blocks, order, name):
    n = len(blocks)
    shape = (n,) + blocks[0].shape
    return pl.pallas_call(
        functools.partial(stack_body, n),
        grid=(1,),
        in_specs=[pl.BlockSpec(memory_space=pltpu.SMEM)] + [ANY] * (n + len(order)),
        out_specs=whole(shape),
        out_shape=jax.ShapeDtypeStruct(shape, BF16),
        scratch_shapes=[pltpu.SemaphoreType.DMA((n,))],
        compiler_params=params(),
        cost_estimate=SMALL,
        name=name,
    )(at, *blocks, *order)


def arrange_body(n, to_ref, *refs):
    blocks, outs, sems = refs[:n], refs[-n - 1 : -1], refs[-1]
    for j in range(n):
        for k in range(n):

            @pl.when(to_ref[j] == k)
            def _():
                pltpu.make_async_copy(blocks[j], outs[k], sems.at[j]).start()

    for j in range(n):
        pltpu.make_async_copy(blocks[j], outs[0], sems.at[j]).wait()


def arrange(to, blocks, order, name):
    n = len(blocks)
    return pl.pallas_call(
        functools.partial(arrange_body, n),
        grid=(1,),
        in_specs=[pl.BlockSpec(memory_space=pltpu.SMEM)] + [ANY] * (n + len(order)),
        out_specs=each(blocks),
        out_shape=[jax.ShapeDtypeStruct(x.shape, BF16) for x in blocks],
        scratch_shapes=[pltpu.SemaphoreType.DMA((n,))],
        compiler_params=params(),
        cost_estimate=SMALL,
        name=name,
    )(to, *blocks, *order)


def grads_body(n, offs_ref, *refs):
    blocks, (w_ref, gate_ref, up_ref), (gg_ref, gu_ref, done_ref, piece) = (
        refs[:n], refs[n : n + 3], refs[-4:]
    )
    width = blocks[0].shape[1]

    @pl.when(pl.program_id(0) == 0)
    def _():
        for j in range(n):
            piece[:, pl.ds(pl.multiple_of(offs_ref[j], 128), width)] = blocks[j][...]
        done_ref[...] = jnp.zeros_like(done_ref)

    total = dot_nt(piece[...], w_ref[...])
    gate = gate_ref[...].astype(F32)
    up = up_ref[...].astype(F32)
    sig = jax.nn.sigmoid(gate)
    gg_ref[...] = (total * up * sig * (1.0 + gate * (1.0 - sig))).astype(BF16)
    gu_ref[...] = (total * (gate * sig)).astype(BF16)


def grads(offs, blocks, weight, gate, up, order):
    n = len(blocks)
    toks, width = blocks[0].shape
    units, feats = weight.shape
    cols = pl.BlockSpec((toks, TILE), lambda i, _: (0, i))
    out = jax.ShapeDtypeStruct((toks, units), BF16)
    return pl.pallas_call(
        functools.partial(grads_body, n),
        grid_spec=pltpu.PrefetchScalarGridSpec(
            num_scalar_prefetch=1,
            grid=(units // TILE,),
            in_specs=[whole((toks, width))] * n
            + [pl.BlockSpec((TILE, feats), lambda i, _: (i, 0)), cols, cols]
            + [ANY] * len(order),
            out_specs=[cols, cols, whole((8, 128))],
            scratch_shapes=[pltpu.VMEM((toks, feats), BF16)],
        ),
        out_shape=(out, out, jax.ShapeDtypeStruct((8, 128), F32)),
        compiler_params=params(),
        cost_estimate=pl.CostEstimate(
            flops=2 * toks * units * feats,
            bytes_accessed=2 * (units * feats + toks * feats + 4 * toks * units),
            transcendentals=toks * units,
        ),
        name="grads",
    )(offs, *blocks, weight, gate, up, *order)


def wgrad_body(n, starts, offs_ref, toks_ref, own_ref, *refs):
    steps = len(starts) - 1
    others, hids = refs[:n], refs[n : (1 + steps) * n]
    out_ref, done_ref, hid, cols, outs, hid_sems, col_sems, out_sems = refs[-8:]
    done_ref[...] = jnp.zeros_like(done_ref)
    _, toks, width = own_ref.shape
    own, other = (pl.ds(pl.multiple_of(offs_ref[half], 128), width) for half in range(2))
    came = []
    for k in range(n):
        rows = pl.ds(pl.multiple_of(toks_ref[k], 128), toks)
        came.append((own_ref.at[k], cols.at[k * toks : (k + 1) * toks, own]))
        came.append((others[k], cols.at[rows, other]))
    came = [pltpu.make_async_copy(a, b, col_sems.at[j]) for j, (a, b) in enumerate(came)]
    units = []
    for i in range(steps):
        part = slice(starts[i], starts[i + 1])
        for k in range(n):
            place = pl.ds(pl.multiple_of(toks_ref[k], 128), toks)
            copy = (hids[i * n + k], hid.at[part, place], hid_sems.at[i * n + k])
            units.append(pltpu.make_async_copy(*copy))
    for copy in [*units[:n], *came, *units[n:]]:
        copy.start()
    for copy in came:
        copy.wait()
    gone = []
    for i in range(steps):
        for copy in units[i * n : (i + 1) * n]:
            copy.wait()
        part = slice(starts[i], starts[i + 1])
        outs[part] = lax.dot_general(
            hid[part], cols[...], (((1,), (0,)), ((), ())), preferred_element_type=F32
        ).astype(BF16)
        gone.append(pltpu.make_async_copy(outs.at[part], out_ref.at[part], out_sems.at[i]))
        gone[-1].start()
    for copy in gone:
        copy.wait()


def wgrad(offs, tok_offs, own, others, hids, order):
    n, toks, width = own.shape
    total = n * toks
    starts = [0]
    for part in hids:
        starts.append(starts[-1] + part[0].shape[0])
    units = starts[-1]
    operands = [offs, tok_offs, own, *others, *(x for part in hids for x in part), *order]
    return pl.pallas_call(
        functools.partial(wgrad_body, n, tuple(starts)),
        in_specs=[pl.BlockSpec(memory_space=pltpu.SMEM)] * 2 + [ANY] * (len(operands) - 2),
        out_specs=[ANY, pl.BlockSpec(memory_space=pltpu.VMEM)],
        out_shape=[
            jax.ShapeDtypeStruct((units, 2 * width), BF16),
            jax.ShapeDtypeStruct((8, 128), F32),
        ],
        scratch_shapes=[
            pltpu.VMEM((units, total), BF16),
            pltpu.VMEM((total, 2 * width), BF16),
            pltpu.VMEM((units, 2 * width), BF16),
            pltpu.SemaphoreType.DMA((len(hids) * n,)),
            pltpu.SemaphoreType.DMA((2 * n,)),
            pltpu.SemaphoreType.DMA((len(hids),)),
        ],
        compiler_params=params(),
        cost_estimate=pl.CostEstimate(
            flops=16 * total * units * width,
            bytes_accessed=2 * (total * (units + 2 * width) + 2 * units * width),
            transcendentals=0,
        ),
        name="wgrad",
    )(*operands)


def put_slices(inner_ref, part, kept_ref, away_refs):
    outer, size, total = kept_ref.shape
    cut = total // len(away_refs)
    for inner in range(2):

        @pl.when(inner_ref[0] == inner)
        def _():
            for p in range(2 * outer):
                rows = part[p * size : (p + 1) * size]
                if p % 2 == inner:
                    kept_ref[p // 2] = rows
                else:
                    for h, away_ref in enumerate(away_refs):
                        away_ref[p // 2] = rows[:, h * cut : (h + 1) * cut]


def grad_gram_body(n, cuts, inner_ref, offs_ref, *refs):
    toks_refs, val_ref, (kept_ref, *away_refs, wide) = refs[:n], refs[n], refs[-2 - cuts :]
    for k, ref in enumerate(toks_refs):
        toks = ref.shape[0]
        wide[:, pl.ds(pl.multiple_of(offs_ref[k], 128), toks)] = dot_nt(val_ref[...], ref[...])
    put_slices(inner_ref, wide, kept_ref, away_refs)


def hidden_gram_body(n, cuts, inner_ref, offs_ref, *refs):
    hid, val_ref, (kept_ref, *away_refs, wide) = refs[:n], refs[n], refs[-2 - cuts :]
    dp_count = offs_ref.shape[0]
    for k in range(dp_count):
        start, total = 0, None
        for ref in hid[k::dp_count]:
            count, toks = ref.shape
            term = lax.dot_general(
                val_ref[:, start : start + count], ref[...], (((1,), (0,)), ((), ())),
                preferred_element_type=F32,
            )
            start, total = start + count, term if total is None else total + term
        wide[:, pl.ds(pl.multiple_of(offs_ref[k], 128), toks)] = total
    put_slices(inner_ref, wide, kept_ref, away_refs)


def gram(body, inner, offs, operands, order, parts, cuts, name):
    smem = pl.BlockSpec(memory_space=pltpu.SMEM)
    *toks, vals = operands
    total = sum(x.size for x in toks) // vals.shape[1]
    kept = jax.ShapeDtypeStruct((parts // 2, vals.shape[0] // parts, total), F32)
    away = jax.ShapeDtypeStruct((parts // 2, vals.shape[0] // parts, total // cuts), F32)
    shapes = [kept] + [away] * cuts
    kept, *away = pl.pallas_call(
        functools.partial(body, len(toks), cuts),
        grid=(1,),
        in_specs=[smem, smem] + each(operands) + [ANY] * len(order),
        out_specs=each(shapes),
        out_shape=shapes,
        scratch_shapes=[pltpu.VMEM((vals.shape[0], total), F32)],
        compiler_params=params(),
        cost_estimate=SMALL,
        name=name,
    )(inner, offs, *operands, *order)
    return kept, away, [swap(x, "fsdp", 1) for x in away]


def pair_body(cuts, kept_ref, *refs):
    came_refs, out_ref = refs[:cuts], refs[-1]
    cut = kept_ref.shape[2] // cuts
    for h in range(cuts):
        cols = slice(h * cut, (h + 1) * cut)
        out_ref[:, :, cols] = kept_ref[:, :, cols] + came_refs[h][...]


def pair_sum(kept, came, order, name):
    return pl.pallas_call(
        functools.partial(pair_body, len(came)),
        grid=(1,),
        in_specs=each([kept, *came]) + [ANY] * len(order),
        out_specs=whole(kept.shape),
        out_shape=jax.ShapeDtypeStruct(kept.shape, F32),
        compiler_params=params(),
        cost_estimate=SMALL,
        name=name,
    )(kept, *came, *order)


def spread(pair):
    n_fs = lax.axis_size("fsdp")
    groups = [list(range(x, n_fs, 2)) for x in range(2)]
    return lax.all_to_all(
        pair, "fsdp", split_axis=0, concat_axis=0, axis_index_groups=groups, tiled=True
    )


def line_body(rows, assign_ref, hid_ref, grad_ref, *refs):
    out_ref = refs[-1]
    n = hid_ref.shape[0]
    hid_sum = sum(hid_ref[j] for j in range(n))
    grad_sum = sum(grad_ref[j] for j in range(n))
    by_tok = jnp.sum(hid_sum * grad_sum, axis=0, keepdims=True)
    size = by_tok.shape[1] // rows
    lane = lax.broadcasted_iota(jnp.int32, (1, 128), 1)
    line = jnp.zeros((1, 128), F32)
    for r in range(rows):
        row = jnp.sum(by_tok[:, r * size : (r + 1) * size], axis=1, keepdims=True)
        line = jnp.where(lane == r, row, line)
    for r in range(assign_ref.shape[0]):
        line = jnp.where(lane == rows + r, assign_ref[r].astype(F32), line)
    out_ref[...] = jnp.broadcast_to(line, out_ref.shape)


def score_line(assign, hid, grad, order, rows, copies):
    return pl.pallas_call(
        functools.partial(line_body, rows),
        grid=(1,),
        in_specs=[pl.BlockSpec(memory_space=pltpu.SMEM)] + each([hid, grad]) + [ANY] * len(order),
        out_specs=whole((copies, 128)),
        out_shape=jax.ShapeDtypeStruct((copies, 128), F32),
        compiler_params=params(),
        cost_estimate=SMALL,
        name="score_line",
    )(assign, hid, grad, *order)


def per_device(gate_act, up_act, out_grad, down_weight, val_hidden, val_grad, assign):
    n_dp = lax.axis_size("dp")
    n_fs = lax.axis_size("fsdp")
    d = lax.axis_index("dp")
    f = lax.axis_index("fsdp")
    rows_here = assign.shape[0]
    toks, width = out_grad.shape
    units = gate_act.shape[1]
    total = n_dp * toks
    n_out = n_fs // 2
    outer, inner = f // 2, f % 2

    at = (outer - jnp.arange(n_out, dtype=jnp.int32)) % n_out
    tok_offs = (d ^ jnp.arange(n_dp, dtype=jnp.int32)) * toks
    inner_at = inner.reshape(1).astype(jnp.int32)
    to = at ^ d

    def over_dp(x):
        far = swap(x, "dp", 2)
        return [x, swap(x, "dp", 1), far, None]

    tiles = units // TILE
    cuts = [0, tiles // 3, tiles - tiles // 3, tiles]
    hids = [
        over_dp(hidden_units(gate_act, up_act, a, b - a, f"hidden_{a}"))
        for a, b in zip(cuts, cuts[1:])
    ]

    ring, others = [out_grad], [swap(out_grad, "fsdp", 1)]
    for step in range(2):
        came = shift(ring[-1], "fsdp", 2)
        ring.append(after(came, others[-1], hids[step][2]))
        others.append(swap(ring[-1], "fsdp", 1))
    for part in hids:
        part[3] = swap(part[2], "dp", 1)
    hid_kept, away, hid_came = gram(
        hidden_gram_body, inner_at, tok_offs, [*(x for part in hids for x in part), val_hidden],
        [ring[2]], n_fs, 1, "hidden_gram",
    )
    ring.append(after(shift(ring[2], "fsdp", 2), others[2], *away))
    others.append(shift(others[2], "fsdp", 2))

    far = swap(out_grad, "dp", 2)
    own = stack(at, ring, [far], "own_features")
    own_cols = lax.all_to_all(own, "dp", split_axis=0, concat_axis=0, tiled=True)

    grad_dp = [out_grad, swap(out_grad, "dp", 1), far, swap(far, "dp", 1)]
    grad_kept, away, grad_came = gram(
        grad_gram_body, inner_at, tok_offs, [*grad_dp, val_grad], [own], n_fs, 1, "grad_gram"
    )
    other = arrange(to, others, away, "other_features")
    other_cols = [x if k == 0 else swap(x, "dp", k) for k, x in enumerate(other)]
    hid_pair = pair_sum(hid_kept, hid_came, [other[0]], "hidden_pair")
    hid_sums = spread(hid_pair)
    offs = (jnp.stack([inner, 1 - inner]) * width).astype(jnp.int32)
    places = (offs[:, None] + at[None, :] * (2 * width)).reshape(-1)
    grad_gate, grad_up, done = grads(
        places, [*ring, *others], down_weight, gate_act, up_act, [hid_pair]
    )
    grad_pair = pair_sum(grad_kept, grad_came, [done], "grad_pair")
    grad_sums = spread(grad_pair)
    weight_grad, done = wgrad(offs, tok_offs, own_cols, other_cols, hids, [grad_pair])

    mine = score_line(assign, hid_sums, grad_sums, [done], n_dp * rows_here, n_dp * n_fs)
    every = lax.all_to_all(
        mine, ("dp", "fsdp"), split_axis=0, concat_axis=0, tiled=True
    ).reshape(n_dp, n_fs, 128)

    rows = n_dp * rows_here
    scale = 1.0 / jnp.sqrt(F32(L) * VAL * FFW * D)
    scores = jnp.sum(every[:, :, :rows], axis=1) * scale
    groups = every[:, 0, rows : rows + rows_here].reshape(rows)
    onehot = (groups[None, :] == jnp.arange(n_dp, dtype=F32)[:, None]).astype(F32)
    group_values = jnp.sum(onehot * scores, axis=1)
    row_scores = lax.dynamic_slice_in_dim(scores, d * rows_here, rows_here, axis=1).T
    return (grad_gate, grad_up, weight_grad, row_scores, group_values)


def per_device_any(gate_act, up_act, out_grad, down_weight, val_hidden, val_grad, assign):
    n_dp = lax.axis_size("dp")
    me = lax.axis_index("dp")
    rows_here = assign.shape[0]
    toks = gate_act.shape[0]
    gate = gate_act.astype(F32)
    up = up_act.astype(F32)
    sig = jax.nn.sigmoid(gate)
    act = gate * sig
    hidden = (act * up).astype(BF16)
    grad_feat = lax.all_gather(out_grad, "dp", axis=0, tiled=True)
    piece = lax.all_gather(out_grad, "fsdp", axis=1, tiled=True)
    hidden_all = lax.all_gather(hidden, "dp", axis=0, tiled=True)
    grad_gram = lax.psum(dot_nt(grad_feat, val_grad), "fsdp")
    grad_cols = lax.all_to_all(piece, "dp", split_axis=1, concat_axis=0, tiled=True)
    grad_hidden = dot_nt(piece, down_weight)
    grad_gate = (grad_hidden * up * sig * (1.0 + gate * (1.0 - sig))).astype(BF16)
    grad_up = (grad_hidden * act).astype(BF16)
    product = dot_nt(hidden_all, val_hidden) * grad_gram
    part = jnp.sum(product.reshape(n_dp * rows_here, toks // rows_here * VAL), axis=1)
    weight_grad = dot_tn(hidden_all, grad_cols).astype(BF16)
    scale = 1.0 / jnp.sqrt(F32(L) * VAL * FFW * D)
    scores = lax.all_gather(lax.psum(part, "fsdp"), "dp") * scale
    groups = lax.all_gather(assign, "dp", tiled=True)
    onehot = (groups[None, :] == jnp.arange(n_dp, dtype=jnp.int32)[:, None]).astype(F32)
    group_values = jnp.sum(onehot * scores, axis=1)
    row_scores = lax.dynamic_slice_in_dim(scores, me * rows_here, rows_here, axis=1).T
    return (grad_gate, grad_up, weight_grad, row_scores, group_values)


def solution(mesh):
    in_specs = (
        P("dp", "fsdp"),
        P("dp", "fsdp"),
        P("dp", "fsdp"),
        P("fsdp", None),
        P("dp", "fsdp"),
        P("dp", "fsdp"),
        P("dp"),
    )
    out_specs = (P("dp", "fsdp"), P("dp", "fsdp"), P("fsdp", "dp"), P("dp", None), P())
    n_dp, n_fs = mesh.shape["dp"], mesh.shape["fsdp"]
    fits = n_dp == 4 and n_fs == 2 * n_dp
    return jax.shard_map(
        per_device if fits else per_device_any,
        mesh=mesh, in_specs=in_specs, out_specs=out_specs, check_vma=False,
    )
```

```python
import functools

import jax
import jax.numpy as jnp
from jax import lax
from jax.experimental import pallas as pl
from jax.experimental.pallas import tpu as pltpu
from jax.sharding import PartitionSpec as P

D = 5120
FFW = 14336
L = 128
VAL = 256

F32 = jnp.float32
BF16 = jnp.bfloat16
TILE = 256
VMEM_LIMIT = 63 * 1024 * 1024


def dot_nt(a, b):
    return lax.dot_general(a, b, (((1,), (1,)), ((), ())), preferred_element_type=F32)


def dot_tn(a, b):
    return lax.dot_general(a, b, (((0,), (0,)), ((), ())), preferred_element_type=F32)


def swap(x, axis, k):
    n = lax.axis_size(axis)
    return lax.ppermute(x, axis, [(s, s ^ k) for s in range(n)])


def shift(x, axis, k):
    n = lax.axis_size(axis)
    return lax.ppermute(x, axis, [(s, (s + k) % n) for s in range(n)])


def whole(shape):
    return pl.BlockSpec(shape, lambda *_: (0,) * len(shape))


def each(arrays):
    return [whole(x.shape) for x in arrays]


ANY = pl.BlockSpec(memory_space=pl.ANY)
HBM = pl.BlockSpec(memory_space=pltpu.HBM)
SMALL = pl.CostEstimate(flops=1024, bytes_accessed=1024, transcendentals=0)


def params():
    return pltpu.CompilerParams(vmem_limit_bytes=VMEM_LIMIT)


def after_body(*refs):
    pass


def after(x, *order):
    return pl.pallas_call(
        after_body,
        in_specs=[ANY] * (1 + len(order)),
        out_specs=ANY,
        out_shape=jax.ShapeDtypeStruct(x.shape, x.dtype),
        input_output_aliases={0: 0},
        compiler_params=params(),
        cost_estimate=SMALL,
        name="after",
    )(x, *order)


def hidden_body(gate_ref, up_ref, hid_ref):
    gate = gate_ref[...].astype(F32)
    hid_ref[...] = (gate * jax.nn.sigmoid(gate) * up_ref[...].astype(F32)).astype(BF16).T


def hidden_units(gate, up, first, count, name):
    toks = gate.shape[0]
    cols = pl.BlockSpec((toks, TILE), lambda i: (0, first + i))
    return pl.pallas_call(
        hidden_body,
        grid=(count,),
        in_specs=[cols, cols],
        out_specs=pl.BlockSpec((TILE, toks), lambda i: (i, 0)),
        out_shape=jax.ShapeDtypeStruct((count * TILE, toks), BF16),
        compiler_params=params(),
        cost_estimate=SMALL,
        name=name,
    )(gate, up)


def stack_body(n, at_ref, *refs):
    blocks, out_ref, sems = refs[:n], refs[-2], refs[-1]
    copies = [
        pltpu.make_async_copy(blocks[j], out_ref.at[at_ref[j]], sems.at[j]) for j in range(n)
    ]
    for copy in copies:
        copy.start()
    for copy in copies:
        copy.wait()


def stack(at, blocks, order, name):
    n = len(blocks)
    shape = (n,) + blocks[0].shape
    return pl.pallas_call(
        functools.partial(stack_body, n),
        grid=(1,),
        in_specs=[pl.BlockSpec(memory_space=pltpu.SMEM)] + [ANY] * (n + len(order)),
        out_specs=whole(shape),
        out_shape=jax.ShapeDtypeStruct(shape, BF16),
        scratch_shapes=[pltpu.SemaphoreType.DMA((n,))],
        compiler_params=params(),
        cost_estimate=SMALL,
        name=name,
    )(at, *blocks, *order)


def arrange_body(n, to_ref, *refs):
    blocks, outs, sems = refs[:n], refs[-n - 1 : -1], refs[-1]
    for j in range(n):
        for k in range(n):

            @pl.when(to_ref[j] == k)
            def _():
                pltpu.make_async_copy(blocks[j], outs[k], sems.at[j]).start()

    for j in range(n):
        pltpu.make_async_copy(blocks[j], outs[0], sems.at[j]).wait()


def arrange(to, blocks, order, name):
    n = len(blocks)
    return pl.pallas_call(
        functools.partial(arrange_body, n),
        grid=(1,),
        in_specs=[pl.BlockSpec(memory_space=pltpu.SMEM)] + [ANY] * (n + len(order)),
        out_specs=each(blocks),
        out_shape=[jax.ShapeDtypeStruct(x.shape, BF16) for x in blocks],
        scratch_shapes=[pltpu.SemaphoreType.DMA((n,))],
        compiler_params=params(),
        cost_estimate=SMALL,
        name=name,
    )(to, *blocks, *order)


def grads_body(n, tiles, offs_ref, *refs):
    blocks, (w_ref, gate_ref, up_ref), (gg_ref, gu_ref, done_ref, piece, sums, sems) = (
        refs[:n], refs[n : n + 3], refs[-6:]
    )
    width = blocks[0].shape[1]
    step = pl.program_id(0)

    def work_off(total):
        gate = gate_ref[...].astype(F32)
        up = up_ref[...].astype(F32)
        sig = jax.nn.sigmoid(gate)
        gg_ref[...] = (total * up * sig * (1.0 + gate * (1.0 - sig))).astype(BF16)
        gu_ref[...] = (total * (gate * sig)).astype(BF16)

    @pl.when(step == 0)
    def _():
        copies = []
        for j in range(n):
            place = pl.ds(pl.multiple_of(offs_ref[j], 128), width)
            copies.append(pltpu.make_async_copy(blocks[j], piece.at[:, place], sems.at[j]))
        for copy in copies:
            copy.start()
        done_ref[...] = jnp.zeros_like(done_ref)
        sums[1] = jnp.zeros(sums.shape[1:], F32)
        for copy in copies:
            copy.wait()

    for odd in range(2):

        @pl.when((step < tiles) & (step % 2 == odd))
        def _():
            work_off(sums[1 - odd])
            sums[odd] = dot_nt(piece[...], w_ref[...])

    @pl.when(step == tiles)
    def _():
        work_off(sums[(tiles - 1) % 2])


def grads(offs, blocks, weight, gate, up, order):
    n = len(blocks)
    toks, width = blocks[0].shape
    units, feats = weight.shape
    tiles = units // TILE
    cols = pl.BlockSpec((toks, TILE), lambda i, _: (0, jnp.maximum(i - 1, 0)))
    out = jax.ShapeDtypeStruct((toks, units), BF16)
    return pl.pallas_call(
        functools.partial(grads_body, n, tiles),
        grid_spec=pltpu.PrefetchScalarGridSpec(
            num_scalar_prefetch=1,
            grid=(tiles + 1,),
            in_specs=[ANY] * n
            + [pl.BlockSpec((TILE, feats), lambda i, _: (jnp.minimum(i, tiles - 1), 0)), cols, cols]
            + [ANY] * len(order),
            out_specs=[cols, cols, whole((8, 128))],
            scratch_shapes=[
                pltpu.VMEM((toks, feats), BF16),
                pltpu.VMEM((2, toks, TILE), F32),
                pltpu.SemaphoreType.DMA((n,)),
            ],
        ),
        out_shape=(out, out, jax.ShapeDtypeStruct((8, 128), F32)),
        compiler_params=params(),
        cost_estimate=pl.CostEstimate(
            flops=2 * toks * units * feats,
            bytes_accessed=2 * (units * feats + toks * feats + 4 * toks * units),
            transcendentals=toks * units,
        ),
        name="grads",
    )(offs, *blocks, weight, gate, up, *order)


def wgrad_body(n, starts, offs_ref, toks_ref, own_ref, *refs):
    steps = len(starts) - 1
    others, hids = refs[:n], refs[n : (1 + steps) * n]
    out_ref, done_ref, hid, cols, outs, hid_sems, col_sems, out_sems = refs[-8:]
    done_ref[...] = jnp.zeros_like(done_ref)
    _, toks, width = own_ref.shape
    own, other = (pl.ds(pl.multiple_of(offs_ref[half], 128), width) for half in range(2))
    came = []
    for k in range(n):
        rows = pl.ds(pl.multiple_of(toks_ref[k], 128), toks)
        came.append((own_ref.at[k], cols.at[k * toks : (k + 1) * toks, own]))
        came.append((others[k], cols.at[rows, other]))
    came = [pltpu.make_async_copy(a, b, col_sems.at[j]) for j, (a, b) in enumerate(came)]
    units = []
    for i in range(steps):
        part = slice(starts[i], starts[i + 1])
        for k in range(n):
            place = pl.ds(pl.multiple_of(toks_ref[k], 128), toks)
            copy = (hids[i * n + k], hid.at[part, place], hid_sems.at[i * n + k])
            units.append(pltpu.make_async_copy(*copy))
    for copy in [*units[:n], *came, *units[n:]]:
        copy.start()
    for copy in came:
        copy.wait()
    gone = []
    for i in range(steps):
        for copy in units[i * n : (i + 1) * n]:
            copy.wait()
        part = slice(starts[i], starts[i + 1])
        outs[part] = lax.dot_general(
            hid[part], cols[...], (((1,), (0,)), ((), ())), preferred_element_type=F32
        ).astype(BF16)
        gone.append(pltpu.make_async_copy(outs.at[part], out_ref.at[part], out_sems.at[i]))
        gone[-1].start()
    for copy in gone:
        copy.wait()


def wgrad(offs, tok_offs, own, others, hids, order):
    n, toks, width = own.shape
    total = n * toks
    starts = [0]
    for part in hids:
        starts.append(starts[-1] + part[0].shape[0])
    units = starts[-1]
    operands = [offs, tok_offs, own, *others, *(x for part in hids for x in part), *order]
    return pl.pallas_call(
        functools.partial(wgrad_body, n, tuple(starts)),
        in_specs=[pl.BlockSpec(memory_space=pltpu.SMEM)] * 2 + [ANY] * (len(operands) - 2),
        out_specs=[ANY, pl.BlockSpec(memory_space=pltpu.VMEM)],
        out_shape=[
            jax.ShapeDtypeStruct((units, 2 * width), BF16),
            jax.ShapeDtypeStruct((8, 128), F32),
        ],
        scratch_shapes=[
            pltpu.VMEM((units, total), BF16),
            pltpu.VMEM((total, 2 * width), BF16),
            pltpu.VMEM((units, 2 * width), BF16),
            pltpu.SemaphoreType.DMA((len(hids) * n,)),
            pltpu.SemaphoreType.DMA((2 * n,)),
            pltpu.SemaphoreType.DMA((len(hids),)),
        ],
        compiler_params=params(),
        cost_estimate=pl.CostEstimate(
            flops=16 * total * units * width,
            bytes_accessed=2 * (total * (units + 2 * width) + 2 * units * width),
            transcendentals=0,
        ),
        name="wgrad",
    )(*operands)


def put_slices(inner_ref, part, kept_ref, away_refs):
    outer, size, total = kept_ref.shape
    cut = total // len(away_refs)
    for inner in range(2):

        @pl.when(inner_ref[0] == inner)
        def _():
            for p in range(2 * outer):
                rows = part[p * size : (p + 1) * size]
                if p % 2 == inner:
                    kept_ref[p // 2] = rows
                else:
                    for h, away_ref in enumerate(away_refs):
                        away_ref[p // 2] = rows[:, h * cut : (h + 1) * cut]


def grad_gram_body(n, cuts, inner_ref, offs_ref, *refs):
    toks_refs, val_ref, (kept_ref, *away_refs, wide) = refs[:n], refs[n], refs[-2 - cuts :]
    for k, ref in enumerate(toks_refs):
        toks = ref.shape[0]
        wide[:, pl.ds(pl.multiple_of(offs_ref[k], 128), toks)] = dot_nt(val_ref[...], ref[...])
    put_slices(inner_ref, wide, kept_ref, away_refs)


def hidden_gram_body(n, cuts, inner_ref, offs_ref, *refs):
    hid, val_ref, (kept_ref, *away_refs, wide) = refs[:n], refs[n], refs[-2 - cuts :]
    dp_count = offs_ref.shape[0]
    for k in range(dp_count):
        start, total = 0, None
        for ref in hid[k::dp_count]:
            count, toks = ref.shape
            term = lax.dot_general(
                val_ref[:, start : start + count], ref[...], (((1,), (0,)), ((), ())),
                preferred_element_type=F32,
            )
            start, total = start + count, term if total is None else total + term
        wide[:, pl.ds(pl.multiple_of(offs_ref[k], 128), toks)] = total
    put_slices(inner_ref, wide, kept_ref, away_refs)


def gram(body, inner, offs, operands, order, parts, cuts, name):
    smem = pl.BlockSpec(memory_space=pltpu.SMEM)
    *toks, vals = operands
    total = sum(x.size for x in toks) // vals.shape[1]
    kept = jax.ShapeDtypeStruct((parts // 2, vals.shape[0] // parts, total), F32)
    away = jax.ShapeDtypeStruct((parts // 2, vals.shape[0] // parts, total // cuts), F32)
    shapes = [kept] + [away] * cuts
    kept, *away = pl.pallas_call(
        functools.partial(body, len(toks), cuts),
        grid=(1,),
        in_specs=[smem, smem] + each(operands) + [ANY] * len(order),
        out_specs=each(shapes),
        out_shape=shapes,
        scratch_shapes=[pltpu.VMEM((vals.shape[0], total), F32)],
        compiler_params=params(),
        cost_estimate=SMALL,
        name=name,
    )(inner, offs, *operands, *order)
    return kept, away, [swap(x, "fsdp", 1) for x in away]


def pair_body(cuts, kept_ref, *refs):
    came_refs, out_ref = refs[:cuts], refs[-1]
    cut = kept_ref.shape[2] // cuts
    for h in range(cuts):
        cols = slice(h * cut, (h + 1) * cut)
        out_ref[:, :, cols] = kept_ref[:, :, cols] + came_refs[h][...]


def pair_sum(kept, came, order, name):
    return pl.pallas_call(
        functools.partial(pair_body, len(came)),
        grid=(1,),
        in_specs=each([kept, *came]) + [ANY] * len(order),
        out_specs=whole(kept.shape),
        out_shape=jax.ShapeDtypeStruct(kept.shape, F32),
        compiler_params=params(),
        cost_estimate=SMALL,
        name=name,
    )(kept, *came, *order)


def spread(pair):
    n_fs = lax.axis_size("fsdp")
    groups = [list(range(x, n_fs, 2)) for x in range(2)]
    return lax.all_to_all(
        pair, "fsdp", split_axis=0, concat_axis=0, axis_index_groups=groups, tiled=True
    )


def line_body(rows, assign_ref, hid_ref, grad_ref, *refs):
    out_ref = refs[-1]
    n = hid_ref.shape[0]
    hid_sum = sum(hid_ref[j] for j in range(n))
    grad_sum = sum(grad_ref[j] for j in range(n))
    by_tok = jnp.sum(hid_sum * grad_sum, axis=0, keepdims=True)
    size = by_tok.shape[1] // rows
    lane = lax.broadcasted_iota(jnp.int32, (1, 128), 1)
    line = jnp.zeros((1, 128), F32)
    for r in range(rows):
        row = jnp.sum(by_tok[:, r * size : (r + 1) * size], axis=1, keepdims=True)
        line = jnp.where(lane == r, row, line)
    for r in range(assign_ref.shape[0]):
        line = jnp.where(lane == rows + r, assign_ref[r].astype(F32), line)
    out_ref[...] = jnp.broadcast_to(line, out_ref.shape)


def score_line(assign, hid, grad, order, rows, copies):
    return pl.pallas_call(
        functools.partial(line_body, rows),
        grid=(1,),
        in_specs=[pl.BlockSpec(memory_space=pltpu.SMEM)] + each([hid, grad]) + [ANY] * len(order),
        out_specs=whole((copies, 128)),
        out_shape=jax.ShapeDtypeStruct((copies, 128), F32),
        compiler_params=params(),
        cost_estimate=SMALL,
        name="score_line",
    )(assign, hid, grad, *order)


def per_device(gate_act, up_act, out_grad, down_weight, val_hidden, val_grad, assign):
    n_dp = lax.axis_size("dp")
    n_fs = lax.axis_size("fsdp")
    d = lax.axis_index("dp")
    f = lax.axis_index("fsdp")
    rows_here = assign.shape[0]
    toks, width = out_grad.shape
    units = gate_act.shape[1]
    total = n_dp * toks
    n_out = n_fs // 2
    outer, inner = f // 2, f % 2

    at = (outer - jnp.arange(n_out, dtype=jnp.int32)) % n_out
    tok_offs = (d ^ jnp.arange(n_dp, dtype=jnp.int32)) * toks
    inner_at = inner.reshape(1).astype(jnp.int32)
    to = at ^ d

    def over_dp(x):
        far = swap(x, "dp", 2)
        return [x, swap(x, "dp", 1), far, None]

    tiles = units // TILE
    cuts = [0, tiles // 3, tiles - tiles // 3, tiles]
    hids = [
        over_dp(hidden_units(gate_act, up_act, a, b - a, f"hidden_{a}"))
        for a, b in zip(cuts, cuts[1:])
    ]

    ring, others = [out_grad], [swap(out_grad, "fsdp", 1)]
    for step in range(2):
        came = shift(ring[-1], "fsdp", 2)
        ring.append(after(came, others[-1], hids[step][2]))
        others.append(swap(ring[-1], "fsdp", 1))
    for part in hids:
        part[3] = swap(part[2], "dp", 1)
    hid_kept, away, hid_came = gram(
        hidden_gram_body, inner_at, tok_offs, [*(x for part in hids for x in part), val_hidden],
        [ring[2]], n_fs, 1, "hidden_gram",
    )
    ring.append(after(shift(ring[2], "fsdp", 2), others[2], *away))
    others.append(shift(others[2], "fsdp", 2))

    far = swap(out_grad, "dp", 2)
    own = stack(at, ring, [far], "own_features")
    own_cols = lax.all_to_all(own, "dp", split_axis=0, concat_axis=0, tiled=True)

    grad_dp = [out_grad, swap(out_grad, "dp", 1), far, swap(far, "dp", 1)]
    grad_kept, away, grad_came = gram(
        grad_gram_body, inner_at, tok_offs, [*grad_dp, val_grad], [own], n_fs, 1, "grad_gram"
    )
    other = arrange(to, others, away, "other_features")
    other_cols = [x if k == 0 else swap(x, "dp", k) for k, x in enumerate(other)]
    hid_pair = pair_sum(hid_kept, hid_came, [other[0]], "hidden_pair")
    hid_sums = spread(hid_pair)
    offs = (jnp.stack([inner, 1 - inner]) * width).astype(jnp.int32)
    places = (offs[:, None] + at[None, :] * (2 * width)).reshape(-1)
    grad_gate, grad_up, done = grads(
        places, [*ring, *others], down_weight, gate_act, up_act, [hid_pair]
    )
    grad_pair = pair_sum(grad_kept, grad_came, [done], "grad_pair")
    grad_sums = spread(grad_pair)
    weight_grad, done = wgrad(offs, tok_offs, own_cols, other_cols, hids, [grad_pair])

    mine = score_line(assign, hid_sums, grad_sums, [done], n_dp * rows_here, n_dp * n_fs)
    every = lax.all_to_all(
        mine, ("dp", "fsdp"), split_axis=0, concat_axis=0, tiled=True
    ).reshape(n_dp, n_fs, 128)

    rows = n_dp * rows_here
    scale = 1.0 / jnp.sqrt(F32(L) * VAL * FFW * D)
    scores = jnp.sum(every[:, :, :rows], axis=1) * scale
    groups = every[:, 0, rows : rows + rows_here].reshape(rows)
    onehot = (groups[None, :] == jnp.arange(n_dp, dtype=F32)[:, None]).astype(F32)
    group_values = jnp.sum(onehot * scores, axis=1)
    row_scores = lax.dynamic_slice_in_dim(scores, d * rows_here, rows_here, axis=1).T
    return (grad_gate, grad_up, weight_grad, row_scores, group_values)


def per_device_any(gate_act, up_act, out_grad, down_weight, val_hidden, val_grad, assign):
    n_dp = lax.axis_size("dp")
    me = lax.axis_index("dp")
    rows_here = assign.shape[0]
    toks = gate_act.shape[0]
    gate = gate_act.astype(F32)
    up = up_act.astype(F32)
    sig = jax.nn.sigmoid(gate)
    act = gate * sig
    hidden = (act * up).astype(BF16)
    grad_feat = lax.all_gather(out_grad, "dp", axis=0, tiled=True)
    piece = lax.all_gather(out_grad, "fsdp", axis=1, tiled=True)
    hidden_all = lax.all_gather(hidden, "dp", axis=0, tiled=True)
    grad_gram = lax.psum(dot_nt(grad_feat, val_grad), "fsdp")
    grad_cols = lax.all_to_all(piece, "dp", split_axis=1, concat_axis=0, tiled=True)
    grad_hidden = dot_nt(piece, down_weight)
    grad_gate = (grad_hidden * up * sig * (1.0 + gate * (1.0 - sig))).astype(BF16)
    grad_up = (grad_hidden * act).astype(BF16)
    product = dot_nt(hidden_all, val_hidden) * grad_gram
    part = jnp.sum(product.reshape(n_dp * rows_here, toks // rows_here * VAL), axis=1)
    weight_grad = dot_tn(hidden_all, grad_cols).astype(BF16)
    scale = 1.0 / jnp.sqrt(F32(L) * VAL * FFW * D)
    scores = lax.all_gather(lax.psum(part, "fsdp"), "dp") * scale
    groups = lax.all_gather(assign, "dp", tiled=True)
    onehot = (groups[None, :] == jnp.arange(n_dp, dtype=jnp.int32)[:, None]).astype(F32)
    group_values = jnp.sum(onehot * scores, axis=1)
    row_scores = lax.dynamic_slice_in_dim(scores, me * rows_here, rows_here, axis=1).T
    return (grad_gate, grad_up, weight_grad, row_scores, group_values)


def solution(mesh):
    in_specs = (
        P("dp", "fsdp"),
        P("dp", "fsdp"),
        P("dp", "fsdp"),
        P("fsdp", None),
        P("dp", "fsdp"),
        P("dp", "fsdp"),
        P("dp"),
    )
    out_specs = (P("dp", "fsdp"), P("dp", "fsdp"), P("fsdp", "dp"), P("dp", None), P())
    n_dp, n_fs = mesh.shape["dp"], mesh.shape["fsdp"]
    fits = n_dp == 4 and n_fs == 2 * n_dp
    return jax.shard_map(
        per_device if fits else per_device_any,
        mesh=mesh, in_specs=in_specs, out_specs=out_specs, check_vma=False,
    )
```

```python
import functools

import jax
import jax.numpy as jnp
from jax import lax
from jax.experimental import pallas as pl
from jax.experimental.pallas import tpu as pltpu
from jax.sharding import PartitionSpec as P

D = 5120
FFW = 14336
L = 128
VAL = 256

F32 = jnp.float32
BF16 = jnp.bfloat16
TILE = 256
VMEM_LIMIT = 63 * 1024 * 1024


def dot_nt(a, b):
    return lax.dot_general(a, b, (((1,), (1,)), ((), ())), preferred_element_type=F32)


def dot_tn(a, b):
    return lax.dot_general(a, b, (((0,), (0,)), ((), ())), preferred_element_type=F32)


def swap(x, axis, k):
    n = lax.axis_size(axis)
    return lax.ppermute(x, axis, [(s, s ^ k) for s in range(n)])


def shift(x, axis, k):
    n = lax.axis_size(axis)
    return lax.ppermute(x, axis, [(s, (s + k) % n) for s in range(n)])


def whole(shape):
    return pl.BlockSpec(shape, lambda *_: (0,) * len(shape))


def each(arrays):
    return [whole(x.shape) for x in arrays]


ANY = pl.BlockSpec(memory_space=pl.ANY)
HBM = pl.BlockSpec(memory_space=pltpu.HBM)
SMALL = pl.CostEstimate(flops=1024, bytes_accessed=1024, transcendentals=0)


def params():
    return pltpu.CompilerParams(vmem_limit_bytes=VMEM_LIMIT)


def after_body(*refs):
    pass


def after(x, *order):
    return pl.pallas_call(
        after_body,
        in_specs=[ANY] * (1 + len(order)),
        out_specs=ANY,
        out_shape=jax.ShapeDtypeStruct(x.shape, x.dtype),
        input_output_aliases={0: 0},
        compiler_params=params(),
        cost_estimate=SMALL,
        name="after",
    )(x, *order)


def hidden_body(gate_ref, up_ref, hid_ref):
    gate = gate_ref[...].astype(F32)
    hid_ref[...] = (gate * jax.nn.sigmoid(gate) * up_ref[...].astype(F32)).astype(BF16).T


def hidden_units(gate, up, first, count, name):
    toks = gate.shape[0]
    cols = pl.BlockSpec((toks, TILE), lambda i: (0, first + i))
    return pl.pallas_call(
        hidden_body,
        grid=(count,),
        in_specs=[cols, cols],
        out_specs=pl.BlockSpec((TILE, toks), lambda i: (i, 0)),
        out_shape=jax.ShapeDtypeStruct((count * TILE, toks), BF16),
        compiler_params=params(),
        cost_estimate=SMALL,
        name=name,
    )(gate, up)


def stack_body(n, at_ref, *refs):
    blocks, out_ref, sems = refs[:n], refs[-2], refs[-1]
    copies = [
        pltpu.make_async_copy(blocks[j], out_ref.at[at_ref[j]], sems.at[j]) for j in range(n)
    ]
    for copy in copies:
        copy.start()
    for copy in copies:
        copy.wait()


def stack(at, blocks, order, name):
    n = len(blocks)
    shape = (n,) + blocks[0].shape
    return pl.pallas_call(
        functools.partial(stack_body, n),
        grid=(1,),
        in_specs=[pl.BlockSpec(memory_space=pltpu.SMEM)] + [ANY] * (n + len(order)),
        out_specs=whole(shape),
        out_shape=jax.ShapeDtypeStruct(shape, BF16),
        scratch_shapes=[pltpu.SemaphoreType.DMA((n,))],
        compiler_params=params(),
        cost_estimate=SMALL,
        name=name,
    )(at, *blocks, *order)


def arrange_body(n, to_ref, *refs):
    blocks, outs, sems = refs[:n], refs[-n - 1 : -1], refs[-1]
    for j in range(n):
        for k in range(n):

            @pl.when(to_ref[j] == k)
            def _():
                pltpu.make_async_copy(blocks[j], outs[k], sems.at[j]).start()

    for j in range(n):
        pltpu.make_async_copy(blocks[j], outs[0], sems.at[j]).wait()


def arrange(to, blocks, order, name):
    n = len(blocks)
    return pl.pallas_call(
        functools.partial(arrange_body, n),
        grid=(1,),
        in_specs=[pl.BlockSpec(memory_space=pltpu.SMEM)] + [ANY] * (n + len(order)),
        out_specs=each(blocks),
        out_shape=[jax.ShapeDtypeStruct(x.shape, BF16) for x in blocks],
        scratch_shapes=[pltpu.SemaphoreType.DMA((n,))],
        compiler_params=params(),
        cost_estimate=SMALL,
        name=name,
    )(to, *blocks, *order)


def grads_body(n, offs_ref, *refs):
    blocks, (w_ref, gate_ref, up_ref), (gg_ref, gu_ref, done_ref, piece) = (
        refs[:n], refs[n : n + 3], refs[-4:]
    )
    width = blocks[0].shape[1]

    @pl.when(pl.program_id(0) == 0)
    def _():
        for j in range(n):
            piece[:, pl.ds(pl.multiple_of(offs_ref[j], 128), width)] = blocks[j][...]
        done_ref[...] = jnp.zeros_like(done_ref)

    total = dot_nt(piece[...], w_ref[...])
    gate = gate_ref[...].astype(F32)
    up = up_ref[...].astype(F32)
    sig = jax.nn.sigmoid(gate)
    gg_ref[...] = (total * up * sig * (1.0 + gate * (1.0 - sig))).astype(BF16)
    gu_ref[...] = (total * (gate * sig)).astype(BF16)


def grads(offs, blocks, weight, gate, up, order):
    n = len(blocks)
    toks, width = blocks[0].shape
    units, feats = weight.shape
    cols = pl.BlockSpec((toks, TILE), lambda i, _: (0, i))
    out = jax.ShapeDtypeStruct((toks, units), BF16)
    return pl.pallas_call(
        functools.partial(grads_body, n),
        grid_spec=pltpu.PrefetchScalarGridSpec(
            num_scalar_prefetch=1,
            grid=(units // TILE,),
            in_specs=[whole((toks, width))] * n
            + [pl.BlockSpec((TILE, feats), lambda i, _: (i, 0)), cols, cols]
            + [ANY] * len(order),
            out_specs=[cols, cols, whole((8, 128))],
            scratch_shapes=[pltpu.VMEM((toks, feats), BF16)],
        ),
        out_shape=(out, out, jax.ShapeDtypeStruct((8, 128), F32)),
        compiler_params=params(),
        cost_estimate=pl.CostEstimate(
            flops=2 * toks * units * feats,
            bytes_accessed=2 * (units * feats + toks * feats + 4 * toks * units),
            transcendentals=toks * units,
        ),
        name="grads",
    )(offs, *blocks, weight, gate, up, *order)


def wgrad_body(n, starts, offs_ref, toks_ref, own_ref, *refs):
    steps = len(starts) - 1
    others, hids = refs[:n], refs[n : (1 + steps) * n]
    out_ref, done_ref, hid, cols, outs, hid_sems, col_sems, out_sems = refs[-8:]
    done_ref[...] = jnp.zeros_like(done_ref)
    _, toks, width = own_ref.shape
    own, other = (pl.ds(pl.multiple_of(offs_ref[half], 128), width) for half in range(2))
    came = []
    for k in range(n):
        rows = pl.ds(pl.multiple_of(toks_ref[k], 128), toks)
        came.append((own_ref.at[k], cols.at[k * toks : (k + 1) * toks, own]))
        came.append((others[k], cols.at[rows, other]))
    came = [pltpu.make_async_copy(a, b, col_sems.at[j]) for j, (a, b) in enumerate(came)]
    units = []
    for i in range(steps):
        part = slice(starts[i], starts[i + 1])
        for k in range(n):
            place = pl.ds(pl.multiple_of(toks_ref[k], 128), toks)
            copy = (hids[i * n + k], hid.at[part, place], hid_sems.at[i * n + k])
            units.append(pltpu.make_async_copy(*copy))
    for copy in [*units[:n], *came, *units[n:]]:
        copy.start()
    for copy in came:
        copy.wait()
    gone = []
    for i in range(steps):
        for copy in units[i * n : (i + 1) * n]:
            copy.wait()
        part = slice(starts[i], starts[i + 1])
        outs[part] = lax.dot_general(
            hid[part], cols[...], (((1,), (0,)), ((), ())), preferred_element_type=F32
        ).astype(BF16)
        gone.append(pltpu.make_async_copy(outs.at[part], out_ref.at[part], out_sems.at[i]))
        gone[-1].start()
    for copy in gone:
        copy.wait()


def wgrad(offs, tok_offs, own, others, hids, order):
    n, toks, width = own.shape
    total = n * toks
    starts = [0]
    for part in hids:
        starts.append(starts[-1] + part[0].shape[0])
    units = starts[-1]
    operands = [offs, tok_offs, own, *others, *(x for part in hids for x in part), *order]
    return pl.pallas_call(
        functools.partial(wgrad_body, n, tuple(starts)),
        in_specs=[pl.BlockSpec(memory_space=pltpu.SMEM)] * 2 + [ANY] * (len(operands) - 2),
        out_specs=[ANY, pl.BlockSpec(memory_space=pltpu.VMEM)],
        out_shape=[
            jax.ShapeDtypeStruct((units, 2 * width), BF16),
            jax.ShapeDtypeStruct((8, 128), F32),
        ],
        scratch_shapes=[
            pltpu.VMEM((units, total), BF16),
            pltpu.VMEM((total, 2 * width), BF16),
            pltpu.VMEM((units, 2 * width), BF16),
            pltpu.SemaphoreType.DMA((len(hids) * n,)),
            pltpu.SemaphoreType.DMA((2 * n,)),
            pltpu.SemaphoreType.DMA((len(hids),)),
        ],
        compiler_params=params(),
        cost_estimate=pl.CostEstimate(
            flops=16 * total * units * width,
            bytes_accessed=2 * (total * (units + 2 * width) + 2 * units * width),
            transcendentals=0,
        ),
        name="wgrad",
    )(*operands)


def put_slices(inner_ref, part, kept_ref, away_refs):
    outer, size, total = kept_ref.shape
    cut = total // len(away_refs)
    for inner in range(2):

        @pl.when(inner_ref[0] == inner)
        def _():
            for p in range(2 * outer):
                rows = part[p * size : (p + 1) * size]
                if p % 2 == inner:
                    kept_ref[p // 2] = rows
                else:
                    for h, away_ref in enumerate(away_refs):
                        away_ref[p // 2] = rows[:, h * cut : (h + 1) * cut]


def grad_gram_body(n, cuts, inner_ref, offs_ref, *refs):
    toks_refs, val_ref, (kept_ref, *away_refs, wide) = refs[:n], refs[n], refs[-2 - cuts :]
    for k, ref in enumerate(toks_refs):
        toks = ref.shape[0]
        wide[:, pl.ds(pl.multiple_of(offs_ref[k], 128), toks)] = dot_nt(val_ref[...], ref[...])
    put_slices(inner_ref, wide, kept_ref, away_refs)


def hidden_gram_body(n, cuts, inner_ref, offs_ref, *refs):
    hid, val_ref, (kept_ref, *away_refs, wide) = refs[:n], refs[n], refs[-2 - cuts :]
    dp_count = offs_ref.shape[0]
    for k in range(dp_count):
        start, total = 0, None
        for ref in hid[k::dp_count]:
            count, toks = ref.shape
            term = lax.dot_general(
                val_ref[:, start : start + count], ref[...], (((1,), (0,)), ((), ())),
                preferred_element_type=F32,
            )
            start, total = start + count, term if total is None else total + term
        wide[:, pl.ds(pl.multiple_of(offs_ref[k], 128), toks)] = total
    put_slices(inner_ref, wide, kept_ref, away_refs)


def gram(body, inner, offs, operands, order, parts, cuts, name):
    smem = pl.BlockSpec(memory_space=pltpu.SMEM)
    *toks, vals = operands
    total = sum(x.size for x in toks) // vals.shape[1]
    kept = jax.ShapeDtypeStruct((parts // 2, vals.shape[0] // parts, total), F32)
    away = jax.ShapeDtypeStruct((parts // 2, vals.shape[0] // parts, total // cuts), F32)
    shapes = [kept] + [away] * cuts
    kept, *away = pl.pallas_call(
        functools.partial(body, len(toks), cuts),
        grid=(1,),
        in_specs=[smem, smem] + each(operands) + [ANY] * len(order),
        out_specs=each(shapes),
        out_shape=shapes,
        scratch_shapes=[pltpu.VMEM((vals.shape[0], total), F32)],
        compiler_params=params(),
        cost_estimate=SMALL,
        name=name,
    )(inner, offs, *operands, *order)
    return kept, away, [swap(x, "fsdp", 1) for x in away]


def pair_body(cuts, kept_ref, *refs):
    came_refs, out_ref = refs[:cuts], refs[-1]
    cut = kept_ref.shape[2] // cuts
    for h in range(cuts):
        cols = slice(h * cut, (h + 1) * cut)
        out_ref[:, :, cols] = kept_ref[:, :, cols] + came_refs[h][...]


def pair_sum(kept, came, order, name):
    return pl.pallas_call(
        functools.partial(pair_body, len(came)),
        grid=(1,),
        in_specs=each([kept, *came]) + [ANY] * len(order),
        out_specs=whole(kept.shape),
        out_shape=jax.ShapeDtypeStruct(kept.shape, F32),
        compiler_params=params(),
        cost_estimate=SMALL,
        name=name,
    )(kept, *came, *order)


def slices_body(n, cuts, outer_ref, kept_ref, *refs):
    came_refs, outs = refs[:cuts], refs[-n:]
    cut = kept_ref.shape[2] // cuts
    for step, out_ref in enumerate(outs):
        at = lax.rem(outer_ref[0] + step, n)
        for h in range(cuts):
            cols = slice(h * cut, (h + 1) * cut)
            out_ref[:, cols] = kept_ref[at, :, cols] + came_refs[h][at]


def pair_slices(outer, kept, came, order, name):
    n, *size = kept.shape
    outs = [jax.ShapeDtypeStruct(size, F32)] * n
    return pl.pallas_call(
        functools.partial(slices_body, n, len(came)),
        grid=(1,),
        in_specs=[pl.BlockSpec(memory_space=pltpu.SMEM)]
        + each([kept, *came])
        + [ANY] * len(order),
        out_specs=each(outs),
        out_shape=outs,
        compiler_params=params(),
        cost_estimate=SMALL,
        name=name,
    )(outer, kept, *came, *order)


def spread(pair):
    n_fs = lax.axis_size("fsdp")
    groups = [list(range(x, n_fs, 2)) for x in range(2)]
    return lax.all_to_all(
        pair, "fsdp", split_axis=0, concat_axis=0, axis_index_groups=groups, tiled=True
    )


def line_body(rows, n, assign_ref, hid_ref, *refs):
    grad, out_ref = refs[:n], refs[-1]
    hid_sum = sum(hid_ref[j] for j in range(n))
    grad_sum = sum(ref[...] for ref in grad)
    by_tok = jnp.sum(hid_sum * grad_sum, axis=0, keepdims=True)
    size = by_tok.shape[1] // rows
    lane = lax.broadcasted_iota(jnp.int32, (1, 128), 1)
    line = jnp.zeros((1, 128), F32)
    for r in range(rows):
        row = jnp.sum(by_tok[:, r * size : (r + 1) * size], axis=1, keepdims=True)
        line = jnp.where(lane == r, row, line)
    for r in range(assign_ref.shape[0]):
        line = jnp.where(lane == rows + r, assign_ref[r].astype(F32), line)
    out_ref[...] = jnp.broadcast_to(line, out_ref.shape)


def score_line(assign, hid, grad, order, rows, copies):
    return pl.pallas_call(
        functools.partial(line_body, rows, len(grad)),
        grid=(1,),
        in_specs=[pl.BlockSpec(memory_space=pltpu.SMEM)] + each([hid, *grad]) + [ANY] * len(order),
        out_specs=whole((copies, 128)),
        out_shape=jax.ShapeDtypeStruct((copies, 128), F32),
        compiler_params=params(),
        cost_estimate=SMALL,
        name="score_line",
    )(assign, hid, *grad, *order)


def per_device(gate_act, up_act, out_grad, down_weight, val_hidden, val_grad, assign):
    n_dp = lax.axis_size("dp")
    n_fs = lax.axis_size("fsdp")
    d = lax.axis_index("dp")
    f = lax.axis_index("fsdp")
    rows_here = assign.shape[0]
    toks, width = out_grad.shape
    units = gate_act.shape[1]
    total = n_dp * toks
    n_out = n_fs // 2
    outer, inner = f // 2, f % 2

    at = (outer - jnp.arange(n_out, dtype=jnp.int32)) % n_out
    tok_offs = (d ^ jnp.arange(n_dp, dtype=jnp.int32)) * toks
    inner_at = inner.reshape(1).astype(jnp.int32)
    to = at ^ d
    outer_at = outer.reshape(1).astype(jnp.int32)

    def over_dp(x):
        far = swap(x, "dp", 2)
        return [x, swap(x, "dp", 1), far, None]

    tiles = units // TILE
    cuts = [0, tiles // 3, tiles - tiles // 3, tiles]
    hids = [
        over_dp(hidden_units(gate_act, up_act, a, b - a, f"hidden_{a}"))
        for a, b in zip(cuts, cuts[1:])
    ]

    ring, others = [out_grad], [swap(out_grad, "fsdp", 1)]
    for step in range(2):
        came = shift(ring[-1], "fsdp", 2)
        ring.append(after(came, others[-1], hids[step][2]))
        others.append(swap(ring[-1], "fsdp", 1))
    for part in hids:
        part[3] = swap(part[2], "dp", 1)
    hid_kept, away, hid_came = gram(
        hidden_gram_body, inner_at, tok_offs, [*(x for part in hids for x in part), val_hidden],
        [ring[2]], n_fs, 1, "hidden_gram",
    )
    ring.append(after(shift(ring[2], "fsdp", 2), others[2], *away))
    others.append(shift(others[2], "fsdp", 2))

    far = swap(out_grad, "dp", 2)
    own = stack(at, ring, [far], "own_features")
    own_cols = lax.all_to_all(own, "dp", split_axis=0, concat_axis=0, tiled=True)

    grad_dp = [out_grad, swap(out_grad, "dp", 1), far, swap(far, "dp", 1)]
    grad_kept, away, grad_came = gram(
        grad_gram_body, inner_at, tok_offs, [*grad_dp, val_grad], [own], n_fs, 1, "grad_gram"
    )
    other = arrange(to, others, away, "other_features")
    other_cols = [x if k == 0 else swap(x, "dp", k) for k, x in enumerate(other)]
    hid_pair = pair_sum(hid_kept, hid_came, [other[0], own_cols], "hidden_pair")
    hid_sums = spread(hid_pair)
    offs = (jnp.stack([inner, 1 - inner]) * width).astype(jnp.int32)
    places = (offs[:, None] + at[None, :] * (2 * width)).reshape(-1)
    grad_gate, grad_up, done = grads(
        places, [*ring, *others], down_weight, gate_act, up_act, [hid_pair]
    )
    grad_pair = pair_slices(outer_at, grad_kept, grad_came, [done, hid_sums], "grad_pair")
    grad_sums = [x if j == 0 else shift(x, "fsdp", 2 * j) for j, x in enumerate(grad_pair)]
    weight_grad, done = wgrad(offs, tok_offs, own_cols, other_cols, hids, [grad_pair[0]])

    mine = score_line(assign, hid_sums, grad_sums, [done], n_dp * rows_here, n_dp * n_fs)
    every = lax.all_to_all(
        mine, ("dp", "fsdp"), split_axis=0, concat_axis=0, tiled=True
    ).reshape(n_dp, n_fs, 128)

    rows = n_dp * rows_here
    scale = 1.0 / jnp.sqrt(F32(L) * VAL * FFW * D)
    scores = jnp.sum(every[:, :, :rows], axis=1) * scale
    groups = every[:, 0, rows : rows + rows_here].reshape(rows)
    onehot = (groups[None, :] == jnp.arange(n_dp, dtype=F32)[:, None]).astype(F32)
    group_values = jnp.sum(onehot * scores, axis=1)
    row_scores = lax.dynamic_slice_in_dim(scores, d * rows_here, rows_here, axis=1).T
    return (grad_gate, grad_up, weight_grad, row_scores, group_values)


def per_device_any(gate_act, up_act, out_grad, down_weight, val_hidden, val_grad, assign):
    n_dp = lax.axis_size("dp")
    me = lax.axis_index("dp")
    rows_here = assign.shape[0]
    toks = gate_act.shape[0]
    gate = gate_act.astype(F32)
    up = up_act.astype(F32)
    sig = jax.nn.sigmoid(gate)
    act = gate * sig
    hidden = (act * up).astype(BF16)
    grad_feat = lax.all_gather(out_grad, "dp", axis=0, tiled=True)
    piece = lax.all_gather(out_grad, "fsdp", axis=1, tiled=True)
    hidden_all = lax.all_gather(hidden, "dp", axis=0, tiled=True)
    grad_gram = lax.psum(dot_nt(grad_feat, val_grad), "fsdp")
    grad_cols = lax.all_to_all(piece, "dp", split_axis=1, concat_axis=0, tiled=True)
    grad_hidden = dot_nt(piece, down_weight)
    grad_gate = (grad_hidden * up * sig * (1.0 + gate * (1.0 - sig))).astype(BF16)
    grad_up = (grad_hidden * act).astype(BF16)
    product = dot_nt(hidden_all, val_hidden) * grad_gram
    part = jnp.sum(product.reshape(n_dp * rows_here, toks // rows_here * VAL), axis=1)
    weight_grad = dot_tn(hidden_all, grad_cols).astype(BF16)
    scale = 1.0 / jnp.sqrt(F32(L) * VAL * FFW * D)
    scores = lax.all_gather(lax.psum(part, "fsdp"), "dp") * scale
    groups = lax.all_gather(assign, "dp", tiled=True)
    onehot = (groups[None, :] == jnp.arange(n_dp, dtype=jnp.int32)[:, None]).astype(F32)
    group_values = jnp.sum(onehot * scores, axis=1)
    row_scores = lax.dynamic_slice_in_dim(scores, me * rows_here, rows_here, axis=1).T
    return (grad_gate, grad_up, weight_grad, row_scores, group_values)


def solution(mesh):
    in_specs = (
        P("dp", "fsdp"),
        P("dp", "fsdp"),
        P("dp", "fsdp"),
        P("fsdp", None),
        P("dp", "fsdp"),
        P("dp", "fsdp"),
        P("dp"),
    )
    out_specs = (P("dp", "fsdp"), P("dp", "fsdp"), P("fsdp", "dp"), P("dp", None), P())
    n_dp, n_fs = mesh.shape["dp"], mesh.shape["fsdp"]
    fits = n_dp == 4 and n_fs == 2 * n_dp
    return jax.shard_map(
        per_device if fits else per_device_any,
        mesh=mesh, in_specs=in_specs, out_specs=out_specs, check_vma=False,
    )
```

```python
import functools

import jax
import jax.numpy as jnp
from jax import lax
from jax.experimental import pallas as pl
from jax.experimental.pallas import tpu as pltpu
from jax.sharding import PartitionSpec as P

D = 5120
FFW = 14336
L = 128
VAL = 256

F32 = jnp.float32
BF16 = jnp.bfloat16
TILE = 256
VMEM_LIMIT = 63 * 1024 * 1024


def dot_nt(a, b):
    return lax.dot_general(a, b, (((1,), (1,)), ((), ())), preferred_element_type=F32)


def dot_tn(a, b):
    return lax.dot_general(a, b, (((0,), (0,)), ((), ())), preferred_element_type=F32)


def swap(x, axis, k):
    n = lax.axis_size(axis)
    return lax.ppermute(x, axis, [(s, s ^ k) for s in range(n)])


def shift(x, axis, k):
    n = lax.axis_size(axis)
    return lax.ppermute(x, axis, [(s, (s + k) % n) for s in range(n)])


def whole(shape):
    return pl.BlockSpec(shape, lambda *_: (0,) * len(shape))


def each(arrays):
    return [whole(x.shape) for x in arrays]


ANY = pl.BlockSpec(memory_space=pl.ANY)
HBM = pl.BlockSpec(memory_space=pltpu.HBM)
SMALL = pl.CostEstimate(flops=1024, bytes_accessed=1024, transcendentals=0)


def params():
    return pltpu.CompilerParams(vmem_limit_bytes=VMEM_LIMIT)


def after_body(*refs):
    pass


def after(x, *order):
    return pl.pallas_call(
        after_body,
        in_specs=[ANY] * (1 + len(order)),
        out_specs=ANY,
        out_shape=jax.ShapeDtypeStruct(x.shape, x.dtype),
        input_output_aliases={0: 0},
        compiler_params=params(),
        cost_estimate=SMALL,
        name="after",
    )(x, *order)


def hidden_body(gate_ref, up_ref, hid_ref):
    gate = gate_ref[...].astype(F32)
    hid_ref[...] = (gate * jax.nn.sigmoid(gate) * up_ref[...].astype(F32)).astype(BF16).T


def hidden_units(gate, up, first, count, name):
    toks = gate.shape[0]
    cols = pl.BlockSpec((toks, TILE), lambda i: (0, first + i))
    return pl.pallas_call(
        hidden_body,
        grid=(count,),
        in_specs=[cols, cols],
        out_specs=pl.BlockSpec((TILE, toks), lambda i: (i, 0)),
        out_shape=jax.ShapeDtypeStruct((count * TILE, toks), BF16),
        compiler_params=params(),
        cost_estimate=SMALL,
        name=name,
    )(gate, up)


def stack_body(n, at_ref, *refs):
    blocks, out_ref, sems = refs[:n], refs[-2], refs[-1]
    copies = [
        pltpu.make_async_copy(blocks[j], out_ref.at[at_ref[j]], sems.at[j]) for j in range(n)
    ]
    for copy in copies:
        copy.start()
    for copy in copies:
        copy.wait()


def stack(at, blocks, order, name):
    n = len(blocks)
    shape = (n,) + blocks[0].shape
    return pl.pallas_call(
        functools.partial(stack_body, n),
        grid=(1,),
        in_specs=[pl.BlockSpec(memory_space=pltpu.SMEM)] + [ANY] * (n + len(order)),
        out_specs=whole(shape),
        out_shape=jax.ShapeDtypeStruct(shape, BF16),
        scratch_shapes=[pltpu.SemaphoreType.DMA((n,))],
        compiler_params=params(),
        cost_estimate=SMALL,
        name=name,
    )(at, *blocks, *order)


def arrange_body(n, to_ref, *refs):
    blocks, outs, sems = refs[:n], refs[-n - 1 : -1], refs[-1]
    for j in range(n):
        for k in range(n):

            @pl.when(to_ref[j] == k)
            def _():
                pltpu.make_async_copy(blocks[j], outs[k], sems.at[j]).start()

    for j in range(n):
        pltpu.make_async_copy(blocks[j], outs[0], sems.at[j]).wait()


def arrange(to, blocks, order, name):
    n = len(blocks)
    return pl.pallas_call(
        functools.partial(arrange_body, n),
        grid=(1,),
        in_specs=[pl.BlockSpec(memory_space=pltpu.SMEM)] + [ANY] * (n + len(order)),
        out_specs=each(blocks),
        out_shape=[jax.ShapeDtypeStruct(x.shape, BF16) for x in blocks],
        scratch_shapes=[pltpu.SemaphoreType.DMA((n,))],
        compiler_params=params(),
        cost_estimate=SMALL,
        name=name,
    )(to, *blocks, *order)


def grads_body(n, offs_ref, *refs):
    blocks, (w_ref, gate_ref, up_ref), (gg_ref, gu_ref, done_ref, piece) = (
        refs[:n], refs[n : n + 3], refs[-4:]
    )
    width = blocks[0].shape[1]

    @pl.when(pl.program_id(0) == 0)
    def _():
        for j in range(n):
            piece[:, pl.ds(pl.multiple_of(offs_ref[j], 128), width)] = blocks[j][...]
        done_ref[...] = jnp.zeros_like(done_ref)

    total = dot_nt(piece[...], w_ref[...])
    gate = gate_ref[...].astype(F32)
    up = up_ref[...].astype(F32)
    sig = jax.nn.sigmoid(gate)
    gg_ref[...] = (total * up * sig * (1.0 + gate * (1.0 - sig))).astype(BF16)
    gu_ref[...] = (total * (gate * sig)).astype(BF16)


def grads(offs, blocks, weight, gate, up, order):
    n = len(blocks)
    toks, width = blocks[0].shape
    units, feats = weight.shape
    cols = pl.BlockSpec((toks, TILE), lambda i, _: (0, i))
    out = jax.ShapeDtypeStruct((toks, units), BF16)
    return pl.pallas_call(
        functools.partial(grads_body, n),
        grid_spec=pltpu.PrefetchScalarGridSpec(
            num_scalar_prefetch=1,
            grid=(units // TILE,),
            in_specs=[whole((toks, width))] * n
            + [pl.BlockSpec((TILE, feats), lambda i, _: (i, 0)), cols, cols]
            + [ANY] * len(order),
            out_specs=[cols, cols, whole((8, 128))],
            scratch_shapes=[pltpu.VMEM((toks, feats), BF16)],
        ),
        out_shape=(out, out, jax.ShapeDtypeStruct((8, 128), F32)),
        compiler_params=params(),
        cost_estimate=pl.CostEstimate(
            flops=2 * toks * units * feats,
            bytes_accessed=2 * (units * feats + toks * feats + 4 * toks * units),
            transcendentals=toks * units,
        ),
        name="grads",
    )(offs, *blocks, weight, gate, up, *order)


def wgrad_body(n, starts, offs_ref, toks_ref, own_ref, *refs):
    steps = len(starts) - 1
    others, hids = refs[:n], refs[n : (1 + steps) * n]
    out_ref, done_ref, hid, cols, outs, hid_sems, col_sems, out_sems = refs[-8:]
    done_ref[...] = jnp.zeros_like(done_ref)
    _, toks, width = own_ref.shape
    own, other = (pl.ds(pl.multiple_of(offs_ref[half], 128), width) for half in range(2))
    came = []
    for k in range(n):
        rows = pl.ds(pl.multiple_of(toks_ref[k], 128), toks)
        came.append((own_ref.at[k], cols.at[k * toks : (k + 1) * toks, own]))
        came.append((others[k], cols.at[rows, other]))
    came = [pltpu.make_async_copy(a, b, col_sems.at[j]) for j, (a, b) in enumerate(came)]
    units = []
    for i in range(steps):
        part = slice(starts[i], starts[i + 1])
        for k in range(n):
            place = pl.ds(pl.multiple_of(toks_ref[k], 128), toks)
            copy = (hids[i * n + k], hid.at[part, place], hid_sems.at[i * n + k])
            units.append(pltpu.make_async_copy(*copy))
    for copy in [*units[:n], *came, *units[n:]]:
        copy.start()
    for copy in came:
        copy.wait()
    gone = []
    for i in range(steps):
        for copy in units[i * n : (i + 1) * n]:
            copy.wait()
        part = slice(starts[i], starts[i + 1])
        outs[part] = lax.dot_general(
            hid[part], cols[...], (((1,), (0,)), ((), ())), preferred_element_type=F32
        ).astype(BF16)
        gone.append(pltpu.make_async_copy(outs.at[part], out_ref.at[part], out_sems.at[i]))
        gone[-1].start()
    for copy in gone:
        copy.wait()


def wgrad(offs, tok_offs, own, others, hids, order):
    n, toks, width = own.shape
    total = n * toks
    starts = [0]
    for part in hids:
        starts.append(starts[-1] + part[0].shape[0])
    units = starts[-1]
    operands = [offs, tok_offs, own, *others, *(x for part in hids for x in part), *order]
    return pl.pallas_call(
        functools.partial(wgrad_body, n, tuple(starts)),
        in_specs=[pl.BlockSpec(memory_space=pltpu.SMEM)] * 2 + [ANY] * (len(operands) - 2),
        out_specs=[ANY, pl.BlockSpec(memory_space=pltpu.VMEM)],
        out_shape=[
            jax.ShapeDtypeStruct((units, 2 * width), BF16),
            jax.ShapeDtypeStruct((8, 128), F32),
        ],
        scratch_shapes=[
            pltpu.VMEM((units, total), BF16),
            pltpu.VMEM((total, 2 * width), BF16),
            pltpu.VMEM((units, 2 * width), BF16),
            pltpu.SemaphoreType.DMA((len(hids) * n,)),
            pltpu.SemaphoreType.DMA((2 * n,)),
            pltpu.SemaphoreType.DMA((len(hids),)),
        ],
        compiler_params=params(),
        cost_estimate=pl.CostEstimate(
            flops=16 * total * units * width,
            bytes_accessed=2 * (total * (units + 2 * width) + 2 * units * width),
            transcendentals=0,
        ),
        name="wgrad",
    )(*operands)


def put_slices(inner_ref, part, kept_ref, away_refs):
    outer, size, total = kept_ref.shape
    cut = total // len(away_refs)
    for inner in range(2):

        @pl.when(inner_ref[0] == inner)
        def _():
            for p in range(2 * outer):
                rows = part[p * size : (p + 1) * size]
                if p % 2 == inner:
                    kept_ref[p // 2] = rows
                else:
                    for h, away_ref in enumerate(away_refs):
                        away_ref[p // 2] = rows[:, h * cut : (h + 1) * cut]


def grad_gram_body(n, cuts, inner_ref, offs_ref, *refs):
    toks_refs, val_ref, (kept_ref, *away_refs, wide) = refs[:n], refs[n], refs[-2 - cuts :]
    for k, ref in enumerate(toks_refs):
        toks = ref.shape[0]
        wide[:, pl.ds(pl.multiple_of(offs_ref[k], 128), toks)] = dot_nt(val_ref[...], ref[...])
    put_slices(inner_ref, wide, kept_ref, away_refs)


def hidden_gram_body(n, cuts, inner_ref, offs_ref, *refs):
    hid, val_ref, (kept_ref, *away_refs, wide) = refs[:n], refs[n], refs[-2 - cuts :]
    dp_count = offs_ref.shape[0]
    for k in range(dp_count):
        start, total = 0, None
        for ref in hid[k::dp_count]:
            count, toks = ref.shape
            term = lax.dot_general(
                val_ref[:, start : start + count], ref[...], (((1,), (0,)), ((), ())),
                preferred_element_type=F32,
            )
            start, total = start + count, term if total is None else total + term
        wide[:, pl.ds(pl.multiple_of(offs_ref[k], 128), toks)] = total
    put_slices(inner_ref, wide, kept_ref, away_refs)


def gram(body, inner, offs, operands, order, parts, cuts, name):
    smem = pl.BlockSpec(memory_space=pltpu.SMEM)
    *toks, vals = operands
    total = sum(x.size for x in toks) // vals.shape[1]
    kept = jax.ShapeDtypeStruct((parts // 2, vals.shape[0] // parts, total), F32)
    away = jax.ShapeDtypeStruct((parts // 2, vals.shape[0] // parts, total // cuts), F32)
    shapes = [kept] + [away] * cuts
    kept, *away = pl.pallas_call(
        functools.partial(body, len(toks), cuts),
        grid=(1,),
        in_specs=[smem, smem] + each(operands) + [ANY] * len(order),
        out_specs=each(shapes),
        out_shape=shapes,
        scratch_shapes=[pltpu.VMEM((vals.shape[0], total), F32)],
        compiler_params=params(),
        cost_estimate=SMALL,
        name=name,
    )(inner, offs, *operands, *order)
    return kept, away, [swap(x, "fsdp", 1) for x in away]


def pair_body(cuts, kept_ref, *refs):
    came_refs, out_ref = refs[:cuts], refs[-1]
    cut = kept_ref.shape[2] // cuts
    for h in range(cuts):
        cols = slice(h * cut, (h + 1) * cut)
        out_ref[:, :, cols] = kept_ref[:, :, cols] + came_refs[h][...]


def pair_sum(kept, came, order, name):
    return pl.pallas_call(
        functools.partial(pair_body, len(came)),
        grid=(1,),
        in_specs=each([kept, *came]) + [ANY] * len(order),
        out_specs=whole(kept.shape),
        out_shape=jax.ShapeDtypeStruct(kept.shape, F32),
        compiler_params=params(),
        cost_estimate=SMALL,
        name=name,
    )(kept, *came, *order)


def slices_body(n, cuts, outer_ref, kept_ref, *refs):
    came_refs, outs = refs[:cuts], refs[-n:]
    cut = kept_ref.shape[2] // cuts
    for step, out_ref in enumerate(outs):
        at = lax.rem(outer_ref[0] + step, n)
        for h in range(cuts):
            cols = slice(h * cut, (h + 1) * cut)
            out_ref[:, cols] = kept_ref[at, :, cols] + came_refs[h][at]


def pair_slices(outer, kept, came, order, name):
    n, *size = kept.shape
    outs = [jax.ShapeDtypeStruct(size, F32)] * n
    return pl.pallas_call(
        functools.partial(slices_body, n, len(came)),
        grid=(1,),
        in_specs=[pl.BlockSpec(memory_space=pltpu.SMEM)]
        + each([kept, *came])
        + [ANY] * len(order),
        out_specs=each(outs),
        out_shape=outs,
        compiler_params=params(),
        cost_estimate=SMALL,
        name=name,
    )(outer, kept, *came, *order)


def spread(pair):
    n_fs = lax.axis_size("fsdp")
    groups = [list(range(x, n_fs, 2)) for x in range(2)]
    return lax.all_to_all(
        pair, "fsdp", split_axis=0, concat_axis=0, axis_index_groups=groups, tiled=True
    )


def line_body(rows, n, assign_ref, hid_ref, *refs):
    grad, out_ref = refs[:n], refs[-1]
    hid_sum = sum(hid_ref[j] for j in range(n))
    grad_sum = sum(ref[...] for ref in grad)
    by_tok = jnp.sum(hid_sum * grad_sum, axis=0, keepdims=True)
    size = by_tok.shape[1] // rows
    lane = lax.broadcasted_iota(jnp.int32, (1, 128), 1)
    line = jnp.zeros((1, 128), F32)
    for r in range(rows):
        row = jnp.sum(by_tok[:, r * size : (r + 1) * size], axis=1, keepdims=True)
        line = jnp.where(lane == r, row, line)
    for r in range(assign_ref.shape[0]):
        line = jnp.where(lane == rows + r, assign_ref[r].astype(F32), line)
    out_ref[...] = jnp.broadcast_to(line, out_ref.shape)


def score_line(assign, hid, grad, order, rows, copies):
    return pl.pallas_call(
        functools.partial(line_body, rows, len(grad)),
        grid=(1,),
        in_specs=[pl.BlockSpec(memory_space=pltpu.SMEM)] + each([hid, *grad]) + [ANY] * len(order),
        out_specs=whole((copies, 128)),
        out_shape=jax.ShapeDtypeStruct((copies, 128), F32),
        compiler_params=params(),
        cost_estimate=SMALL,
        name="score_line",
    )(assign, hid, *grad, *order)


def per_device(gate_act, up_act, out_grad, down_weight, val_hidden, val_grad, assign):
    n_dp = lax.axis_size("dp")
    n_fs = lax.axis_size("fsdp")
    d = lax.axis_index("dp")
    f = lax.axis_index("fsdp")
    rows_here = assign.shape[0]
    toks, width = out_grad.shape
    units = gate_act.shape[1]
    total = n_dp * toks
    n_out = n_fs // 2
    outer, inner = f // 2, f % 2

    at = (outer - jnp.arange(n_out, dtype=jnp.int32)) % n_out
    tok_offs = (d ^ jnp.arange(n_dp, dtype=jnp.int32)) * toks
    inner_at = inner.reshape(1).astype(jnp.int32)
    to = at ^ d
    outer_at = outer.reshape(1).astype(jnp.int32)

    def over_dp(x):
        far = swap(x, "dp", 2)
        return [x, swap(x, "dp", 1), far, None]

    tiles = units // TILE
    cuts = [0, tiles // 3, tiles - tiles // 3, tiles]
    hids = [
        over_dp(hidden_units(gate_act, up_act, a, b - a, f"hidden_{a}"))
        for a, b in zip(cuts, cuts[1:])
    ]

    ring, others = [out_grad], [swap(out_grad, "fsdp", 1)]
    for step in range(2):
        came = shift(ring[-1], "fsdp", 2)
        ring.append(after(came, others[-1], hids[step][2], hids[step][1]))
        others.append(swap(ring[-1], "fsdp", 1))
    for part in hids:
        part[3] = swap(part[2], "dp", 1)
    hid_kept, away, hid_came = gram(
        hidden_gram_body, inner_at, tok_offs, [*(x for part in hids for x in part), val_hidden],
        [ring[2]], n_fs, 1, "hidden_gram",
    )
    ring.append(after(shift(ring[2], "fsdp", 2), others[2], *away))
    others.append(shift(others[2], "fsdp", 2))

    far = swap(out_grad, "dp", 2)
    own = stack(at, ring, [far], "own_features")
    own_cols = lax.all_to_all(own, "dp", split_axis=0, concat_axis=0, tiled=True)

    grad_dp = [out_grad, swap(out_grad, "dp", 1), far, swap(far, "dp", 1)]
    grad_kept, away, grad_came = gram(
        grad_gram_body, inner_at, tok_offs, [*grad_dp, val_grad], [own], n_fs, 1, "grad_gram"
    )
    other = arrange(to, others, away, "other_features")
    other_cols = [x if k == 0 else swap(x, "dp", k) for k, x in enumerate(other)]
    hid_pair = pair_sum(hid_kept, hid_came, [other[0], own_cols], "hidden_pair")
    hid_sums = spread(hid_pair)
    offs = (jnp.stack([inner, 1 - inner]) * width).astype(jnp.int32)
    places = (offs[:, None] + at[None, :] * (2 * width)).reshape(-1)
    grad_gate, grad_up, done = grads(
        places, [*ring, *others], down_weight, gate_act, up_act, [hid_pair]
    )
    grad_pair = pair_slices(outer_at, grad_kept, grad_came, [done, hid_sums], "grad_pair")
    grad_sums = [x if j == 0 else shift(x, "fsdp", 2 * j) for j, x in enumerate(grad_pair)]
    weight_grad, done = wgrad(offs, tok_offs, own_cols, other_cols, hids, [grad_pair[0]])

    mine = score_line(assign, hid_sums, grad_sums, [done], n_dp * rows_here, n_dp * n_fs)
    every = lax.all_to_all(
        mine, ("dp", "fsdp"), split_axis=0, concat_axis=0, tiled=True
    ).reshape(n_dp, n_fs, 128)

    rows = n_dp * rows_here
    scale = 1.0 / jnp.sqrt(F32(L) * VAL * FFW * D)
    scores = jnp.sum(every[:, :, :rows], axis=1) * scale
    groups = every[:, 0, rows : rows + rows_here].reshape(rows)
    onehot = (groups[None, :] == jnp.arange(n_dp, dtype=F32)[:, None]).astype(F32)
    group_values = jnp.sum(onehot * scores, axis=1)
    row_scores = lax.dynamic_slice_in_dim(scores, d * rows_here, rows_here, axis=1).T
    return (grad_gate, grad_up, weight_grad, row_scores, group_values)


def per_device_any(gate_act, up_act, out_grad, down_weight, val_hidden, val_grad, assign):
    n_dp = lax.axis_size("dp")
    me = lax.axis_index("dp")
    rows_here = assign.shape[0]
    toks = gate_act.shape[0]
    gate = gate_act.astype(F32)
    up = up_act.astype(F32)
    sig = jax.nn.sigmoid(gate)
    act = gate * sig
    hidden = (act * up).astype(BF16)
    grad_feat = lax.all_gather(out_grad, "dp", axis=0, tiled=True)
    piece = lax.all_gather(out_grad, "fsdp", axis=1, tiled=True)
    hidden_all = lax.all_gather(hidden, "dp", axis=0, tiled=True)
    grad_gram = lax.psum(dot_nt(grad_feat, val_grad), "fsdp")
    grad_cols = lax.all_to_all(piece, "dp", split_axis=1, concat_axis=0, tiled=True)
    grad_hidden = dot_nt(piece, down_weight)
    grad_gate = (grad_hidden * up * sig * (1.0 + gate * (1.0 - sig))).astype(BF16)
    grad_up = (grad_hidden * act).astype(BF16)
    product = dot_nt(hidden_all, val_hidden) * grad_gram
    part = jnp.sum(product.reshape(n_dp * rows_here, toks // rows_here * VAL), axis=1)
    weight_grad = dot_tn(hidden_all, grad_cols).astype(BF16)
    scale = 1.0 / jnp.sqrt(F32(L) * VAL * FFW * D)
    scores = lax.all_gather(lax.psum(part, "fsdp"), "dp") * scale
    groups = lax.all_gather(assign, "dp", tiled=True)
    onehot = (groups[None, :] == jnp.arange(n_dp, dtype=jnp.int32)[:, None]).astype(F32)
    group_values = jnp.sum(onehot * scores, axis=1)
    row_scores = lax.dynamic_slice_in_dim(scores, me * rows_here, rows_here, axis=1).T
    return (grad_gate, grad_up, weight_grad, row_scores, group_values)


def solution(mesh):
    in_specs = (
        P("dp", "fsdp"),
        P("dp", "fsdp"),
        P("dp", "fsdp"),
        P("fsdp", None),
        P("dp", "fsdp"),
        P("dp", "fsdp"),
        P("dp"),
    )
    out_specs = (P("dp", "fsdp"), P("dp", "fsdp"), P("fsdp", "dp"), P("dp", None), P())
    n_dp, n_fs = mesh.shape["dp"], mesh.shape["fsdp"]
    fits = n_dp == 4 and n_fs == 2 * n_dp
    return jax.shard_map(
        per_device if fits else per_device_any,
        mesh=mesh, in_specs=in_specs, out_specs=out_specs, check_vma=False,
    )
```

```python
import functools

import jax
import jax.numpy as jnp
from jax import lax
from jax.experimental import pallas as pl
from jax.experimental.pallas import tpu as pltpu
from jax.sharding import PartitionSpec as P

D = 5120
FFW = 14336
L = 128
VAL = 256

F32 = jnp.float32
BF16 = jnp.bfloat16
TILE = 256
VMEM_LIMIT = 63 * 1024 * 1024


def dot_nt(a, b):
    return lax.dot_general(a, b, (((1,), (1,)), ((), ())), preferred_element_type=F32)


def dot_tn(a, b):
    return lax.dot_general(a, b, (((0,), (0,)), ((), ())), preferred_element_type=F32)


def swap(x, axis, k):
    n = lax.axis_size(axis)
    return lax.ppermute(x, axis, [(s, s ^ k) for s in range(n)])


def shift(x, axis, k):
    n = lax.axis_size(axis)
    return lax.ppermute(x, axis, [(s, (s + k) % n) for s in range(n)])


def whole(shape):
    return pl.BlockSpec(shape, lambda *_: (0,) * len(shape))


def each(arrays):
    return [whole(x.shape) for x in arrays]


ANY = pl.BlockSpec(memory_space=pl.ANY)
HBM = pl.BlockSpec(memory_space=pltpu.HBM)
SMALL = pl.CostEstimate(flops=1024, bytes_accessed=1024, transcendentals=0)


def params():
    return pltpu.CompilerParams(vmem_limit_bytes=VMEM_LIMIT)


def after_body(*refs):
    pass


def after(x, *order):
    return pl.pallas_call(
        after_body,
        in_specs=[ANY] * (1 + len(order)),
        out_specs=ANY,
        out_shape=jax.ShapeDtypeStruct(x.shape, x.dtype),
        input_output_aliases={0: 0},
        compiler_params=params(),
        cost_estimate=SMALL,
        name="after",
    )(x, *order)


def hidden_body(gate_ref, up_ref, hid_ref):
    gate = gate_ref[...].astype(F32)
    hid_ref[...] = (gate * jax.nn.sigmoid(gate) * up_ref[...].astype(F32)).astype(BF16).T


def hidden_units(gate, up, first, count, name):
    toks = gate.shape[0]
    cols = pl.BlockSpec((toks, TILE), lambda i: (0, first + i))
    return pl.pallas_call(
        hidden_body,
        grid=(count,),
        in_specs=[cols, cols],
        out_specs=pl.BlockSpec((TILE, toks), lambda i: (i, 0)),
        out_shape=jax.ShapeDtypeStruct((count * TILE, toks), BF16),
        compiler_params=params(),
        cost_estimate=SMALL,
        name=name,
    )(gate, up)


def stack_body(n, at_ref, *refs):
    blocks, out_ref, sems = refs[:n], refs[-2], refs[-1]
    copies = [
        pltpu.make_async_copy(blocks[j], out_ref.at[at_ref[j]], sems.at[j]) for j in range(n)
    ]
    for copy in copies:
        copy.start()
    for copy in copies:
        copy.wait()


def stack(at, blocks, order, name):
    n = len(blocks)
    shape = (n,) + blocks[0].shape
    return pl.pallas_call(
        functools.partial(stack_body, n),
        grid=(1,),
        in_specs=[pl.BlockSpec(memory_space=pltpu.SMEM)] + [ANY] * (n + len(order)),
        out_specs=whole(shape),
        out_shape=jax.ShapeDtypeStruct(shape, BF16),
        scratch_shapes=[pltpu.SemaphoreType.DMA((n,))],
        compiler_params=params(),
        cost_estimate=SMALL,
        name=name,
    )(at, *blocks, *order)


def arrange_body(n, to_ref, *refs):
    blocks, outs, sems = refs[:n], refs[-n - 1 : -1], refs[-1]
    for j in range(n):
        for k in range(n):

            @pl.when(to_ref[j] == k)
            def _():
                pltpu.make_async_copy(blocks[j], outs[k], sems.at[j]).start()

    for j in range(n):
        pltpu.make_async_copy(blocks[j], outs[0], sems.at[j]).wait()


def arrange(to, blocks, order, name):
    n = len(blocks)
    return pl.pallas_call(
        functools.partial(arrange_body, n),
        grid=(1,),
        in_specs=[pl.BlockSpec(memory_space=pltpu.SMEM)] + [ANY] * (n + len(order)),
        out_specs=each(blocks),
        out_shape=[jax.ShapeDtypeStruct(x.shape, BF16) for x in blocks],
        scratch_shapes=[pltpu.SemaphoreType.DMA((n,))],
        compiler_params=params(),
        cost_estimate=SMALL,
        name=name,
    )(to, *blocks, *order)


def grads_body(n, offs_ref, *refs):
    blocks, (w_ref, gate_ref, up_ref), (gg_ref, gu_ref, done_ref, piece) = (
        refs[:n], refs[n : n + 3], refs[-4:]
    )
    width = blocks[0].shape[1]

    @pl.when(pl.program_id(0) == 0)
    def _():
        for j in range(n):
            piece[:, pl.ds(pl.multiple_of(offs_ref[j], 128), width)] = blocks[j][...]
        done_ref[...] = jnp.zeros_like(done_ref)

    total = dot_nt(piece[...], w_ref[...])
    gate = gate_ref[...].astype(F32)
    up = up_ref[...].astype(F32)
    sig = jax.nn.sigmoid(gate)
    gg_ref[...] = (total * up * sig * (1.0 + gate * (1.0 - sig))).astype(BF16)
    gu_ref[...] = (total * (gate * sig)).astype(BF16)


def grads(offs, blocks, weight, gate, up, order):
    n = len(blocks)
    toks, width = blocks[0].shape
    units, feats = weight.shape
    cols = pl.BlockSpec((toks, TILE), lambda i, _: (0, i))
    out = jax.ShapeDtypeStruct((toks, units), BF16)
    return pl.pallas_call(
        functools.partial(grads_body, n),
        grid_spec=pltpu.PrefetchScalarGridSpec(
            num_scalar_prefetch=1,
            grid=(units // TILE,),
            in_specs=[whole((toks, width))] * n
            + [pl.BlockSpec((TILE, feats), lambda i, _: (i, 0)), cols, cols]
            + [ANY] * len(order),
            out_specs=[cols, cols, whole((8, 128))],
            scratch_shapes=[pltpu.VMEM((toks, feats), BF16)],
        ),
        out_shape=(out, out, jax.ShapeDtypeStruct((8, 128), F32)),
        compiler_params=params(),
        cost_estimate=pl.CostEstimate(
            flops=2 * toks * units * feats,
            bytes_accessed=2 * (units * feats + toks * feats + 4 * toks * units),
            transcendentals=toks * units,
        ),
        name="grads",
    )(offs, *blocks, weight, gate, up, *order)


def wgrad_body(n, starts, offs_ref, toks_ref, own_ref, *refs):
    steps = len(starts) - 1
    others, hids = refs[:n], refs[n : (1 + steps) * n]
    out_ref, done_ref, hid, cols, outs, hid_sems, col_sems, out_sems = refs[-8:]
    done_ref[...] = jnp.zeros_like(done_ref)
    _, toks, width = own_ref.shape
    own, other = (pl.ds(pl.multiple_of(offs_ref[half], 128), width) for half in range(2))
    came = []
    for k in range(n):
        rows = pl.ds(pl.multiple_of(toks_ref[k], 128), toks)
        came.append((own_ref.at[k], cols.at[k * toks : (k + 1) * toks, own]))
        came.append((others[k], cols.at[rows, other]))
    came = [pltpu.make_async_copy(a, b, col_sems.at[j]) for j, (a, b) in enumerate(came)]
    units = []
    for i in range(steps):
        part = slice(starts[i], starts[i + 1])
        for k in range(n):
            place = pl.ds(pl.multiple_of(toks_ref[k], 128), toks)
            copy = (hids[i * n + k], hid.at[part, place], hid_sems.at[i * n + k])
            units.append(pltpu.make_async_copy(*copy))
    for copy in [*units[:n], *came, *units[n:]]:
        copy.start()
    for copy in came:
        copy.wait()
    gone = []
    for i in range(steps):
        for copy in units[i * n : (i + 1) * n]:
            copy.wait()
        part = slice(starts[i], starts[i + 1])
        outs[part] = lax.dot_general(
            hid[part], cols[...], (((1,), (0,)), ((), ())), preferred_element_type=F32
        ).astype(BF16)
        gone.append(pltpu.make_async_copy(outs.at[part], out_ref.at[part], out_sems.at[i]))
        gone[-1].start()
    for copy in gone:
        copy.wait()


def wgrad(offs, tok_offs, own, others, hids, order):
    n, toks, width = own.shape
    total = n * toks
    starts = [0]
    for part in hids:
        starts.append(starts[-1] + part[0].shape[0])
    units = starts[-1]
    operands = [offs, tok_offs, own, *others, *(x for part in hids for x in part), *order]
    return pl.pallas_call(
        functools.partial(wgrad_body, n, tuple(starts)),
        in_specs=[pl.BlockSpec(memory_space=pltpu.SMEM)] * 2 + [ANY] * (len(operands) - 2),
        out_specs=[ANY, pl.BlockSpec(memory_space=pltpu.VMEM)],
        out_shape=[
            jax.ShapeDtypeStruct((units, 2 * width), BF16),
            jax.ShapeDtypeStruct((8, 128), F32),
        ],
        scratch_shapes=[
            pltpu.VMEM((units, total), BF16),
            pltpu.VMEM((total, 2 * width), BF16),
            pltpu.VMEM((units, 2 * width), BF16),
            pltpu.SemaphoreType.DMA((len(hids) * n,)),
            pltpu.SemaphoreType.DMA((2 * n,)),
            pltpu.SemaphoreType.DMA((len(hids),)),
        ],
        compiler_params=params(),
        cost_estimate=pl.CostEstimate(
            flops=16 * total * units * width,
            bytes_accessed=2 * (total * (units + 2 * width) + 2 * units * width),
            transcendentals=0,
        ),
        name="wgrad",
    )(*operands)


def put_slices(inner_ref, part, kept_ref, away_refs):
    outer, size, total = kept_ref.shape
    cut = total // len(away_refs)
    for inner in range(2):

        @pl.when(inner_ref[0] == inner)
        def _():
            for p in range(2 * outer):
                rows = part[p * size : (p + 1) * size]
                if p % 2 == inner:
                    kept_ref[p // 2] = rows
                else:
                    for h, away_ref in enumerate(away_refs):
                        away_ref[p // 2] = rows[:, h * cut : (h + 1) * cut]


def grad_gram_body(n, cuts, inner_ref, offs_ref, *refs):
    toks_refs, val_ref, (kept_ref, *away_refs, wide) = refs[:n], refs[n], refs[-2 - cuts :]
    for k, ref in enumerate(toks_refs):
        toks = ref.shape[0]
        wide[:, pl.ds(pl.multiple_of(offs_ref[k], 128), toks)] = dot_nt(val_ref[...], ref[...])
    put_slices(inner_ref, wide, kept_ref, away_refs)


def hidden_gram_body(n, cuts, inner_ref, offs_ref, *refs):
    hid, val_ref, (kept_ref, *away_refs, wide) = refs[:n], refs[n], refs[-2 - cuts :]
    dp_count = offs_ref.shape[0]
    for k in range(dp_count):
        start, total = 0, None
        for ref in hid[k::dp_count]:
            count, toks = ref.shape
            term = lax.dot_general(
                val_ref[:, start : start + count], ref[...], (((1,), (0,)), ((), ())),
                preferred_element_type=F32,
            )
            start, total = start + count, term if total is None else total + term
        wide[:, pl.ds(pl.multiple_of(offs_ref[k], 128), toks)] = total
    put_slices(inner_ref, wide, kept_ref, away_refs)


def gram(body, inner, offs, operands, order, parts, cuts, name):
    smem = pl.BlockSpec(memory_space=pltpu.SMEM)
    *toks, vals = operands
    total = sum(x.size for x in toks) // vals.shape[1]
    kept = jax.ShapeDtypeStruct((parts // 2, vals.shape[0] // parts, total), F32)
    away = jax.ShapeDtypeStruct((parts // 2, vals.shape[0] // parts, total // cuts), F32)
    shapes = [kept] + [away] * cuts
    kept, *away = pl.pallas_call(
        functools.partial(body, len(toks), cuts),
        grid=(1,),
        in_specs=[smem, smem] + each(operands) + [ANY] * len(order),
        out_specs=each(shapes),
        out_shape=shapes,
        scratch_shapes=[pltpu.VMEM((vals.shape[0], total), F32)],
        compiler_params=params(),
        cost_estimate=SMALL,
        name=name,
    )(inner, offs, *operands, *order)
    return kept, away, [swap(x, "fsdp", 1) for x in away]


def pair_body(cuts, kept_ref, *refs):
    came_refs, out_ref = refs[:cuts], refs[-1]
    cut = kept_ref.shape[2] // cuts
    for h in range(cuts):
        cols = slice(h * cut, (h + 1) * cut)
        out_ref[:, :, cols] = kept_ref[:, :, cols] + came_refs[h][...]


def pair_sum(kept, came, order, name):
    return pl.pallas_call(
        functools.partial(pair_body, len(came)),
        grid=(1,),
        in_specs=each([kept, *came]) + [ANY] * len(order),
        out_specs=whole(kept.shape),
        out_shape=jax.ShapeDtypeStruct(kept.shape, F32),
        compiler_params=params(),
        cost_estimate=SMALL,
        name=name,
    )(kept, *came, *order)


def spread(pair):
    n_fs = lax.axis_size("fsdp")
    groups = [list(range(x, n_fs, 2)) for x in range(2)]
    return lax.all_to_all(
        pair, "fsdp", split_axis=0, concat_axis=0, axis_index_groups=groups, tiled=True
    )


def line_body(rows, assign_ref, hid_ref, grad_ref, *refs):
    out_ref = refs[-1]
    n = hid_ref.shape[0]
    hid_sum = sum(hid_ref[j] for j in range(n))
    grad_sum = sum(grad_ref[j] for j in range(n))
    by_tok = jnp.sum(hid_sum * grad_sum, axis=0, keepdims=True)
    size = by_tok.shape[1] // rows
    lane = lax.broadcasted_iota(jnp.int32, (1, 128), 1)
    line = jnp.zeros((1, 128), F32)
    for r in range(rows):
        row = jnp.sum(by_tok[:, r * size : (r + 1) * size], axis=1, keepdims=True)
        line = jnp.where(lane == r, row, line)
    for r in range(assign_ref.shape[0]):
        line = jnp.where(lane == rows + r, assign_ref[r].astype(F32), line)
    out_ref[...] = jnp.broadcast_to(line, out_ref.shape)


def score_line(assign, hid, grad, order, rows, copies):
    return pl.pallas_call(
        functools.partial(line_body, rows),
        grid=(1,),
        in_specs=[pl.BlockSpec(memory_space=pltpu.SMEM)] + each([hid, grad]) + [ANY] * len(order),
        out_specs=whole((copies, 128)),
        out_shape=jax.ShapeDtypeStruct((copies, 128), F32),
        compiler_params=params(),
        cost_estimate=SMALL,
        name="score_line",
    )(assign, hid, grad, *order)


def per_device(gate_act, up_act, out_grad, down_weight, val_hidden, val_grad, assign):
    n_dp = lax.axis_size("dp")
    n_fs = lax.axis_size("fsdp")
    d = lax.axis_index("dp")
    f = lax.axis_index("fsdp")
    rows_here = assign.shape[0]
    toks, width = out_grad.shape
    units = gate_act.shape[1]
    total = n_dp * toks
    n_out = n_fs // 2
    outer, inner = f // 2, f % 2

    at = (outer - jnp.arange(n_out, dtype=jnp.int32)) % n_out
    tok_offs = (d ^ jnp.arange(n_dp, dtype=jnp.int32)) * toks
    inner_at = inner.reshape(1).astype(jnp.int32)
    to = at ^ d

    def over_dp(x):
        far = swap(x, "dp", 2)
        return [x, swap(x, "dp", 1), far, None]

    tiles = units // TILE
    cuts = [0, tiles // 7, tiles // 7 * 4, tiles]
    hids = [
        over_dp(hidden_units(gate_act, up_act, a, b - a, f"hidden_{a}"))
        for a, b in zip(cuts, cuts[1:])
    ]

    ring, others = [out_grad], [swap(out_grad, "fsdp", 1)]
    for step in range(2):
        came = shift(ring[-1], "fsdp", 2)
        ring.append(after(came, others[-1], hids[step][2]))
        others.append(swap(ring[-1], "fsdp", 1))
    for part in hids:
        part[3] = swap(part[2], "dp", 1)
    hid_kept, away, hid_came = gram(
        hidden_gram_body, inner_at, tok_offs, [*(x for part in hids for x in part), val_hidden],
        [ring[2]], n_fs, 1, "hidden_gram",
    )
    ring.append(after(shift(ring[2], "fsdp", 2), others[2], *away))
    others.append(shift(others[2], "fsdp", 2))

    far = swap(out_grad, "dp", 2)
    own = stack(at, ring, [far], "own_features")
    own_cols = lax.all_to_all(own, "dp", split_axis=0, concat_axis=0, tiled=True)

    grad_dp = [out_grad, swap(out_grad, "dp", 1), far, swap(far, "dp", 1)]
    grad_kept, away, grad_came = gram(
        grad_gram_body, inner_at, tok_offs, [*grad_dp, val_grad], [own], n_fs, 1, "grad_gram"
    )
    other = arrange(to, others, away, "other_features")
    other_cols = [x if k == 0 else swap(x, "dp", k) for k, x in enumerate(other)]
    hid_pair = pair_sum(hid_kept, hid_came, [other[0]], "hidden_pair")
    hid_sums = spread(hid_pair)
    offs = (jnp.stack([inner, 1 - inner]) * width).astype(jnp.int32)
    places = (offs[:, None] + at[None, :] * (2 * width)).reshape(-1)
    grad_gate, grad_up, done = grads(
        places, [*ring, *others], down_weight, gate_act, up_act, [hid_pair]
    )
    grad_pair = pair_sum(grad_kept, grad_came, [done], "grad_pair")
    grad_sums = spread(grad_pair)
    weight_grad, done = wgrad(offs, tok_offs, own_cols, other_cols, hids, [grad_pair])

    mine = score_line(assign, hid_sums, grad_sums, [done], n_dp * rows_here, n_dp * n_fs)
    every = lax.all_to_all(
        mine, ("dp", "fsdp"), split_axis=0, concat_axis=0, tiled=True
    ).reshape(n_dp, n_fs, 128)

    rows = n_dp * rows_here
    scale = 1.0 / jnp.sqrt(F32(L) * VAL * FFW * D)
    scores = jnp.sum(every[:, :, :rows], axis=1) * scale
    groups = every[:, 0, rows : rows + rows_here].reshape(rows)
    onehot = (groups[None, :] == jnp.arange(n_dp, dtype=F32)[:, None]).astype(F32)
    group_values = jnp.sum(onehot * scores, axis=1)
    row_scores = lax.dynamic_slice_in_dim(scores, d * rows_here, rows_here, axis=1).T
    return (grad_gate, grad_up, weight_grad, row_scores, group_values)


def per_device_any(gate_act, up_act, out_grad, down_weight, val_hidden, val_grad, assign):
    n_dp = lax.axis_size("dp")
    me = lax.axis_index("dp")
    rows_here = assign.shape[0]
    toks = gate_act.shape[0]
    gate = gate_act.astype(F32)
    up = up_act.astype(F32)
    sig = jax.nn.sigmoid(gate)
    act = gate * sig
    hidden = (act * up).astype(BF16)
    grad_feat = lax.all_gather(out_grad, "dp", axis=0, tiled=True)
    piece = lax.all_gather(out_grad, "fsdp", axis=1, tiled=True)
    hidden_all = lax.all_gather(hidden, "dp", axis=0, tiled=True)
    grad_gram = lax.psum(dot_nt(grad_feat, val_grad), "fsdp")
    grad_cols = lax.all_to_all(piece, "dp", split_axis=1, concat_axis=0, tiled=True)
    grad_hidden = dot_nt(piece, down_weight)
    grad_gate = (grad_hidden * up * sig * (1.0 + gate * (1.0 - sig))).astype(BF16)
    grad_up = (grad_hidden * act).astype(BF16)
    product = dot_nt(hidden_all, val_hidden) * grad_gram
    part = jnp.sum(product.reshape(n_dp * rows_here, toks // rows_here * VAL), axis=1)
    weight_grad = dot_tn(hidden_all, grad_cols).astype(BF16)
    scale = 1.0 / jnp.sqrt(F32(L) * VAL * FFW * D)
    scores = lax.all_gather(lax.psum(part, "fsdp"), "dp") * scale
    groups = lax.all_gather(assign, "dp", tiled=True)
    onehot = (groups[None, :] == jnp.arange(n_dp, dtype=jnp.int32)[:, None]).astype(F32)
    group_values = jnp.sum(onehot * scores, axis=1)
    row_scores = lax.dynamic_slice_in_dim(scores, me * rows_here, rows_here, axis=1).T
    return (grad_gate, grad_up, weight_grad, row_scores, group_values)


def solution(mesh):
    in_specs = (
        P("dp", "fsdp"),
        P("dp", "fsdp"),
        P("dp", "fsdp"),
        P("fsdp", None),
        P("dp", "fsdp"),
        P("dp", "fsdp"),
        P("dp"),
    )
    out_specs = (P("dp", "fsdp"), P("dp", "fsdp"), P("fsdp", "dp"), P("dp", None), P())
    n_dp, n_fs = mesh.shape["dp"], mesh.shape["fsdp"]
    fits = n_dp == 4 and n_fs == 2 * n_dp
    return jax.shard_map(
        per_device if fits else per_device_any,
        mesh=mesh, in_specs=in_specs, out_specs=out_specs, check_vma=False,
    )
```

```python
import functools

import jax
import jax.numpy as jnp
from jax import lax
from jax.experimental import pallas as pl
from jax.experimental.pallas import tpu as pltpu
from jax.sharding import PartitionSpec as P

D = 5120
FFW = 14336
L = 128
VAL = 256

F32 = jnp.float32
BF16 = jnp.bfloat16
TILE = 256
VMEM_LIMIT = 63 * 1024 * 1024


def dot_nt(a, b):
    return lax.dot_general(a, b, (((1,), (1,)), ((), ())), preferred_element_type=F32)


def dot_tn(a, b):
    return lax.dot_general(a, b, (((0,), (0,)), ((), ())), preferred_element_type=F32)


def swap(x, axis, k):
    n = lax.axis_size(axis)
    return lax.ppermute(x, axis, [(s, s ^ k) for s in range(n)])


def shift(x, axis, k):
    n = lax.axis_size(axis)
    return lax.ppermute(x, axis, [(s, (s + k) % n) for s in range(n)])


def whole(shape):
    return pl.BlockSpec(shape, lambda *_: (0,) * len(shape))


def each(arrays):
    return [whole(x.shape) for x in arrays]


ANY = pl.BlockSpec(memory_space=pl.ANY)
HBM = pl.BlockSpec(memory_space=pltpu.HBM)
SMALL = pl.CostEstimate(flops=1024, bytes_accessed=1024, transcendentals=0)


def params():
    return pltpu.CompilerParams(vmem_limit_bytes=VMEM_LIMIT)


def after_body(*refs):
    pass


def after(x, *order):
    return pl.pallas_call(
        after_body,
        in_specs=[ANY] * (1 + len(order)),
        out_specs=ANY,
        out_shape=jax.ShapeDtypeStruct(x.shape, x.dtype),
        input_output_aliases={0: 0},
        compiler_params=params(),
        cost_estimate=SMALL,
        name="after",
    )(x, *order)


def hidden_body(gate_ref, up_ref, hid_ref):
    gate = gate_ref[...].astype(F32)
    hid_ref[...] = (gate * jax.nn.sigmoid(gate) * up_ref[...].astype(F32)).astype(BF16).T


def hidden_units(gate, up, first, count, name):
    toks = gate.shape[0]
    cols = pl.BlockSpec((toks, TILE), lambda i: (0, first + i))
    return pl.pallas_call(
        hidden_body,
        grid=(count,),
        in_specs=[cols, cols],
        out_specs=pl.BlockSpec((TILE, toks), lambda i: (i, 0)),
        out_shape=jax.ShapeDtypeStruct((count * TILE, toks), BF16),
        compiler_params=params(),
        cost_estimate=SMALL,
        name=name,
    )(gate, up)


def stack_body(n, at_ref, *refs):
    blocks, out_ref, sems = refs[:n], refs[-2], refs[-1]
    copies = [
        pltpu.make_async_copy(blocks[j], out_ref.at[at_ref[j]], sems.at[j]) for j in range(n)
    ]
    for copy in copies:
        copy.start()
    for copy in copies:
        copy.wait()


def stack(at, blocks, order, name):
    n = len(blocks)
    shape = (n,) + blocks[0].shape
    return pl.pallas_call(
        functools.partial(stack_body, n),
        grid=(1,),
        in_specs=[pl.BlockSpec(memory_space=pltpu.SMEM)] + [ANY] * (n + len(order)),
        out_specs=whole(shape),
        out_shape=jax.ShapeDtypeStruct(shape, BF16),
        scratch_shapes=[pltpu.SemaphoreType.DMA((n,))],
        compiler_params=params(),
        cost_estimate=SMALL,
        name=name,
    )(at, *blocks, *order)


def arrange_body(n, to_ref, *refs):
    blocks, outs, sems = refs[:n], refs[-n - 1 : -1], refs[-1]
    for j in range(n):
        for k in range(n):

            @pl.when(to_ref[j] == k)
            def _():
                pltpu.make_async_copy(blocks[j], outs[k], sems.at[j]).start()

    for j in range(n):
        pltpu.make_async_copy(blocks[j], outs[0], sems.at[j]).wait()


def arrange(to, blocks, order, name):
    n = len(blocks)
    return pl.pallas_call(
        functools.partial(arrange_body, n),
        grid=(1,),
        in_specs=[pl.BlockSpec(memory_space=pltpu.SMEM)] + [ANY] * (n + len(order)),
        out_specs=each(blocks),
        out_shape=[jax.ShapeDtypeStruct(x.shape, BF16) for x in blocks],
        scratch_shapes=[pltpu.SemaphoreType.DMA((n,))],
        compiler_params=params(),
        cost_estimate=SMALL,
        name=name,
    )(to, *blocks, *order)


def grads_body(n, offs_ref, *refs):
    blocks, (w_ref, gate_ref, up_ref), (gg_ref, gu_ref, done_ref, piece) = (
        refs[:n], refs[n : n + 3], refs[-4:]
    )
    width = blocks[0].shape[1]

    @pl.when(pl.program_id(0) == 0)
    def _():
        for j in range(n):
            piece[:, pl.ds(pl.multiple_of(offs_ref[j], 128), width)] = blocks[j][...]
        done_ref[...] = jnp.zeros_like(done_ref)

    total = dot_nt(piece[...], w_ref[...])
    gate = gate_ref[...].astype(F32)
    up = up_ref[...].astype(F32)
    sig = jax.nn.sigmoid(gate)
    gg_ref[...] = (total * up * sig * (1.0 + gate * (1.0 - sig))).astype(BF16)
    gu_ref[...] = (total * (gate * sig)).astype(BF16)


def grads(offs, blocks, weight, gate, up, order):
    n = len(blocks)
    toks, width = blocks[0].shape
    units, feats = weight.shape
    cols = pl.BlockSpec((toks, TILE), lambda i, _: (0, i))
    out = jax.ShapeDtypeStruct((toks, units), BF16)
    return pl.pallas_call(
        functools.partial(grads_body, n),
        grid_spec=pltpu.PrefetchScalarGridSpec(
            num_scalar_prefetch=1,
            grid=(units // TILE,),
            in_specs=[whole((toks, width))] * n
            + [pl.BlockSpec((TILE, feats), lambda i, _: (i, 0)), cols, cols]
            + [ANY] * len(order),
            out_specs=[cols, cols, whole((8, 128))],
            scratch_shapes=[pltpu.VMEM((toks, feats), BF16)],
        ),
        out_shape=(out, out, jax.ShapeDtypeStruct((8, 128), F32)),
        compiler_params=params(),
        cost_estimate=pl.CostEstimate(
            flops=2 * toks * units * feats,
            bytes_accessed=2 * (units * feats + toks * feats + 4 * toks * units),
            transcendentals=toks * units,
        ),
        name="grads",
    )(offs, *blocks, weight, gate, up, *order)


def wgrad_body(n, starts, offs_ref, toks_ref, own_ref, *refs):
    steps = len(starts) - 1
    others, hids = refs[:n], refs[n : (1 + steps) * n]
    out_ref, done_ref, hid, cols, outs, hid_sems, col_sems, out_sems = refs[-8:]
    done_ref[...] = jnp.zeros_like(done_ref)
    _, toks, width = own_ref.shape
    own, other = (pl.ds(pl.multiple_of(offs_ref[half], 128), width) for half in range(2))
    came = []
    for k in range(n):
        rows = pl.ds(pl.multiple_of(toks_ref[k], 128), toks)
        came.append((own_ref.at[k], cols.at[k * toks : (k + 1) * toks, own]))
        came.append((others[k], cols.at[rows, other]))
    came = [pltpu.make_async_copy(a, b, col_sems.at[j]) for j, (a, b) in enumerate(came)]
    units = []
    for i in range(steps):
        part = slice(starts[i], starts[i + 1])
        for k in range(n):
            place = pl.ds(pl.multiple_of(toks_ref[k], 128), toks)
            copy = (hids[i * n + k], hid.at[part, place], hid_sems.at[i * n + k])
            units.append(pltpu.make_async_copy(*copy))
    for copy in [*units[:n], *came, *units[n:]]:
        copy.start()
    for copy in came:
        copy.wait()
    gone = []
    for i in range(steps):
        for copy in units[i * n : (i + 1) * n]:
            copy.wait()
        part = slice(starts[i], starts[i + 1])
        outs[part] = lax.dot_general(
            hid[part], cols[...], (((1,), (0,)), ((), ())), preferred_element_type=F32
        ).astype(BF16)
        gone.append(pltpu.make_async_copy(outs.at[part], out_ref.at[part], out_sems.at[i]))
        gone[-1].start()
    for copy in gone:
        copy.wait()


def wgrad(offs, tok_offs, own, others, hids, order):
    n, toks, width = own.shape
    total = n * toks
    starts = [0]
    for part in hids:
        starts.append(starts[-1] + part[0].shape[0])
    units = starts[-1]
    operands = [offs, tok_offs, own, *others, *(x for part in hids for x in part), *order]
    return pl.pallas_call(
        functools.partial(wgrad_body, n, tuple(starts)),
        in_specs=[pl.BlockSpec(memory_space=pltpu.SMEM)] * 2 + [ANY] * (len(operands) - 2),
        out_specs=[ANY, pl.BlockSpec(memory_space=pltpu.VMEM)],
        out_shape=[
            jax.ShapeDtypeStruct((units, 2 * width), BF16),
            jax.ShapeDtypeStruct((8, 128), F32),
        ],
        scratch_shapes=[
            pltpu.VMEM((units, total), BF16),
            pltpu.VMEM((total, 2 * width), BF16),
            pltpu.VMEM((units, 2 * width), BF16),
            pltpu.SemaphoreType.DMA((len(hids) * n,)),
            pltpu.SemaphoreType.DMA((2 * n,)),
            pltpu.SemaphoreType.DMA((len(hids),)),
        ],
        compiler_params=params(),
        cost_estimate=pl.CostEstimate(
            flops=16 * total * units * width,
            bytes_accessed=2 * (total * (units + 2 * width) + 2 * units * width),
            transcendentals=0,
        ),
        name="wgrad",
    )(*operands)


def put_slices(inner_ref, part, kept_ref, away_refs):
    outer, size, total = kept_ref.shape
    cut = total // len(away_refs)
    for inner in range(2):

        @pl.when(inner_ref[0] == inner)
        def _():
            for p in range(2 * outer):
                rows = part[p * size : (p + 1) * size]
                if p % 2 == inner:
                    kept_ref[p // 2] = rows
                else:
                    for h, away_ref in enumerate(away_refs):
                        away_ref[p // 2] = rows[:, h * cut : (h + 1) * cut]


def grad_gram_body(n, cuts, inner_ref, offs_ref, *refs):
    toks_refs, val_ref, (kept_ref, *away_refs, wide) = refs[:n], refs[n], refs[-2 - cuts :]
    for k, ref in enumerate(toks_refs):
        toks = ref.shape[0]
        wide[:, pl.ds(pl.multiple_of(offs_ref[k], 128), toks)] = dot_nt(val_ref[...], ref[...])
    put_slices(inner_ref, wide, kept_ref, away_refs)


def hidden_gram_body(n, cuts, inner_ref, offs_ref, *refs):
    hid, val_ref, (kept_ref, *away_refs, wide) = refs[:n], refs[n], refs[-2 - cuts :]
    dp_count = offs_ref.shape[0]
    for k in range(dp_count):
        start, total = 0, None
        for ref in hid[k::dp_count]:
            count, toks = ref.shape
            term = lax.dot_general(
                val_ref[:, start : start + count], ref[...], (((1,), (0,)), ((), ())),
                preferred_element_type=F32,
            )
            start, total = start + count, term if total is None else total + term
        wide[:, pl.ds(pl.multiple_of(offs_ref[k], 128), toks)] = total
    put_slices(inner_ref, wide, kept_ref, away_refs)


def gram(body, inner, offs, operands, order, parts, cuts, name):
    smem = pl.BlockSpec(memory_space=pltpu.SMEM)
    *toks, vals = operands
    total = sum(x.size for x in toks) // vals.shape[1]
    kept = jax.ShapeDtypeStruct((parts // 2, vals.shape[0] // parts, total), F32)
    away = jax.ShapeDtypeStruct((parts // 2, vals.shape[0] // parts, total // cuts), F32)
    shapes = [kept] + [away] * cuts
    kept, *away = pl.pallas_call(
        functools.partial(body, len(toks), cuts),
        grid=(1,),
        in_specs=[smem, smem] + each(operands) + [ANY] * len(order),
        out_specs=each(shapes),
        out_shape=shapes,
        scratch_shapes=[pltpu.VMEM((vals.shape[0], total), F32)],
        compiler_params=params(),
        cost_estimate=SMALL,
        name=name,
    )(inner, offs, *operands, *order)
    return kept, away, [swap(x, "fsdp", 1) for x in away]


def pair_body(cuts, kept_ref, *refs):
    came_refs, out_ref = refs[:cuts], refs[-1]
    cut = kept_ref.shape[2] // cuts
    for h in range(cuts):
        cols = slice(h * cut, (h + 1) * cut)
        out_ref[:, :, cols] = kept_ref[:, :, cols] + came_refs[h][...]


def pair_sum(kept, came, order, name):
    return pl.pallas_call(
        functools.partial(pair_body, len(came)),
        grid=(1,),
        in_specs=each([kept, *came]) + [ANY] * len(order),
        out_specs=whole(kept.shape),
        out_shape=jax.ShapeDtypeStruct(kept.shape, F32),
        compiler_params=params(),
        cost_estimate=SMALL,
        name=name,
    )(kept, *came, *order)


def spread(pair):
    n_fs = lax.axis_size("fsdp")
    groups = [list(range(x, n_fs, 2)) for x in range(2)]
    return lax.all_to_all(
        pair, "fsdp", split_axis=0, concat_axis=0, axis_index_groups=groups, tiled=True
    )


def line_body(rows, assign_ref, hid_ref, grad_ref, *refs):
    out_ref = refs[-1]
    n = hid_ref.shape[0]
    hid_sum = sum(hid_ref[j] for j in range(n))
    grad_sum = sum(grad_ref[j] for j in range(n))
    by_tok = jnp.sum(hid_sum * grad_sum, axis=0, keepdims=True)
    size = by_tok.shape[1] // rows
    lane = lax.broadcasted_iota(jnp.int32, (1, 128), 1)
    line = jnp.zeros((1, 128), F32)
    for r in range(rows):
        row = jnp.sum(by_tok[:, r * size : (r + 1) * size], axis=1, keepdims=True)
        line = jnp.where(lane == r, row, line)
    for r in range(assign_ref.shape[0]):
        line = jnp.where(lane == rows + r, assign_ref[r].astype(F32), line)
    out_ref[...] = jnp.broadcast_to(line, out_ref.shape)


def score_line(assign, hid, grad, order, rows, copies):
    return pl.pallas_call(
        functools.partial(line_body, rows),
        grid=(1,),
        in_specs=[pl.BlockSpec(memory_space=pltpu.SMEM)] + each([hid, grad]) + [ANY] * len(order),
        out_specs=whole((copies, 128)),
        out_shape=jax.ShapeDtypeStruct((copies, 128), F32),
        compiler_params=params(),
        cost_estimate=SMALL,
        name="score_line",
    )(assign, hid, grad, *order)


def per_device(gate_act, up_act, out_grad, down_weight, val_hidden, val_grad, assign):
    n_dp = lax.axis_size("dp")
    n_fs = lax.axis_size("fsdp")
    d = lax.axis_index("dp")
    f = lax.axis_index("fsdp")
    rows_here = assign.shape[0]
    toks, width = out_grad.shape
    units = gate_act.shape[1]
    total = n_dp * toks
    n_out = n_fs // 2
    outer, inner = f // 2, f % 2

    at = (outer - jnp.arange(n_out, dtype=jnp.int32)) % n_out
    tok_offs = (d ^ jnp.arange(n_dp, dtype=jnp.int32)) * toks
    inner_at = inner.reshape(1).astype(jnp.int32)
    to = at ^ d

    def over_dp(x):
        far = swap(x, "dp", 2)
        return [x, swap(x, "dp", 1), far, None]

    tiles = units // TILE
    cuts = [0, tiles // 3, tiles - tiles // 3, tiles]
    hids = [
        over_dp(hidden_units(gate_act, up_act, a, b - a, f"hidden_{a}"))
        for a, b in zip(cuts, cuts[1:])
    ]

    ring, others = [out_grad], [swap(out_grad, "fsdp", 1)]
    for step in range(2):
        came = shift(ring[-1], "fsdp", 2)
        ring.append(after(came, others[-1], hids[step][2]))
        others.append(swap(ring[-1], "fsdp", 1))
    for part in hids:
        part[3] = swap(part[2], "dp", 1)
    hid_kept, away, hid_came = gram(
        hidden_gram_body, inner_at, tok_offs, [*(x for part in hids for x in part), val_hidden],
        [ring[2]], n_fs, 1, "hidden_gram",
    )
    ring.append(after(shift(ring[2], "fsdp", 2), others[2], *away))
    others.append(shift(others[2], "fsdp", 2))

    far = swap(out_grad, "dp", 2)
    own = stack(at, ring, [far], "own_features")
    own_cols = lax.all_to_all(own, "dp", split_axis=0, concat_axis=0, tiled=True)

    grad_dp = [out_grad, swap(out_grad, "dp", 1), far, swap(far, "dp", 1)]
    grad_kept, away, grad_came = gram(
        grad_gram_body, inner_at, tok_offs, [*grad_dp, val_grad], [own], n_fs, 1, "grad_gram"
    )
    other = arrange(to, others, away, "other_features")
    other_cols = [x if k == 0 else swap(x, "dp", k) for k, x in enumerate(other)]
    hid_pair = pair_sum(hid_kept, hid_came, [other[0]], "hidden_pair")
    hid_sums = spread(hid_pair)
    offs = (jnp.stack([inner, 1 - inner]) * width).astype(jnp.int32)
    places = (offs[:, None] + at[None, :] * (2 * width)).reshape(-1)
    grad_gate, grad_up, done = grads(
        places, [*ring, *others], down_weight, gate_act, up_act, [hid_pair]
    )
    grad_pair = grad_kept + after(grad_came[0], done)
    grad_sums = spread(grad_pair)
    weight_grad, done = wgrad(offs, tok_offs, own_cols, other_cols, hids, [grad_pair])

    mine = score_line(assign, hid_sums, grad_sums, [done], n_dp * rows_here, n_dp * n_fs)
    every = lax.all_to_all(
        mine, ("dp", "fsdp"), split_axis=0, concat_axis=0, tiled=True
    ).reshape(n_dp, n_fs, 128)

    rows = n_dp * rows_here
    scale = 1.0 / jnp.sqrt(F32(L) * VAL * FFW * D)
    scores = jnp.sum(every[:, :, :rows], axis=1) * scale
    groups = every[:, 0, rows : rows + rows_here].reshape(rows)
    onehot = (groups[None, :] == jnp.arange(n_dp, dtype=F32)[:, None]).astype(F32)
    group_values = jnp.sum(onehot * scores, axis=1)
    row_scores = lax.dynamic_slice_in_dim(scores, d * rows_here, rows_here, axis=1).T
    return (grad_gate, grad_up, weight_grad, row_scores, group_values)


def per_device_any(gate_act, up_act, out_grad, down_weight, val_hidden, val_grad, assign):
    n_dp = lax.axis_size("dp")
    me = lax.axis_index("dp")
    rows_here = assign.shape[0]
    toks = gate_act.shape[0]
    gate = gate_act.astype(F32)
    up = up_act.astype(F32)
    sig = jax.nn.sigmoid(gate)
    act = gate * sig
    hidden = (act * up).astype(BF16)
    grad_feat = lax.all_gather(out_grad, "dp", axis=0, tiled=True)
    piece = lax.all_gather(out_grad, "fsdp", axis=1, tiled=True)
    hidden_all = lax.all_gather(hidden, "dp", axis=0, tiled=True)
    grad_gram = lax.psum(dot_nt(grad_feat, val_grad), "fsdp")
    grad_cols = lax.all_to_all(piece, "dp", split_axis=1, concat_axis=0, tiled=True)
    grad_hidden = dot_nt(piece, down_weight)
    grad_gate = (grad_hidden * up * sig * (1.0 + gate * (1.0 - sig))).astype(BF16)
    grad_up = (grad_hidden * act).astype(BF16)
    product = dot_nt(hidden_all, val_hidden) * grad_gram
    part = jnp.sum(product.reshape(n_dp * rows_here, toks // rows_here * VAL), axis=1)
    weight_grad = dot_tn(hidden_all, grad_cols).astype(BF16)
    scale = 1.0 / jnp.sqrt(F32(L) * VAL * FFW * D)
    scores = lax.all_gather(lax.psum(part, "fsdp"), "dp") * scale
    groups = lax.all_gather(assign, "dp", tiled=True)
    onehot = (groups[None, :] == jnp.arange(n_dp, dtype=jnp.int32)[:, None]).astype(F32)
    group_values = jnp.sum(onehot * scores, axis=1)
    row_scores = lax.dynamic_slice_in_dim(scores, me * rows_here, rows_here, axis=1).T
    return (grad_gate, grad_up, weight_grad, row_scores, group_values)


def solution(mesh):
    in_specs = (
        P("dp", "fsdp"),
        P("dp", "fsdp"),
        P("dp", "fsdp"),
        P("fsdp", None),
        P("dp", "fsdp"),
        P("dp", "fsdp"),
        P("dp"),
    )
    out_specs = (P("dp", "fsdp"), P("dp", "fsdp"), P("fsdp", "dp"), P("dp", None), P())
    n_dp, n_fs = mesh.shape["dp"], mesh.shape["fsdp"]
    fits = n_dp == 4 and n_fs == 2 * n_dp
    return jax.shard_map(
        per_device if fits else per_device_any,
        mesh=mesh, in_specs=in_specs, out_specs=out_specs, check_vma=False,
    )
```
